128 devices in a mesh: ctx: 8 (over y_hi, x), fsdp: 16 (over z, y_lo, core).
Axes of the slice: x: 4, y: 4 (y_hi: 2, y_lo: 2; y = y_hi * 2 + y_lo), z: 4, core: 2. Of those that a mesh axis runs over, the one named last changes fastest.
Arguments:
- tokens: bfloat16 [16, 2, 512, 1536], P('fsdp', None, 'ctx'), may hold values from -6 to 6
- cotangent: bfloat16 [16, 2, 512, 1536], P('fsdp', None, 'ctx'), may hold values from -6 to 6
- attn_gain: bfloat16 [1536], P(('ctx', 'fsdp')), may hold values from 0.099609375 to 1.8984375
- q_weight: bfloat16 [1536, 1536], P(('ctx', 'fsdp')), may hold values from -0.15625 to 0.15625
- q_bias: bfloat16 [1536], P(('ctx', 'fsdp')), may hold values from -3 to 3
- k_weight: bfloat16 [1536, 256], P(('ctx', 'fsdp')), may hold values from -0.15625 to 0.15625
- k_bias: bfloat16 [256], P(('ctx', 'fsdp')), may hold values from -3 to 3
- v_weight: bfloat16 [1536, 256], P(('ctx', 'fsdp')), may hold values from -0.15625 to 0.15625
- v_bias: bfloat16 [256], P(('ctx', 'fsdp')), may hold values from -1.1953125 to 1.1953125
- o_weight: bfloat16 [1536, 1536], P(('ctx', 'fsdp')), may hold values from -0.75 to 0.75
- mlp_gain: bfloat16 [1536], P(('ctx', 'fsdp')), may hold values from 0.099609375 to 1.8984375
- gate_weight: bfloat16 [1536, 8960], P(('ctx', 'fsdp')), may hold values from -0.15625 to 0.15625
- up_weight: bfloat16 [1536, 8960], P(('ctx', 'fsdp')), may hold values from -0.15625 to 0.15625
- down_weight: bfloat16 [1536, 8960], P(('ctx', 'fsdp')), may hold values from -0.0625 to 0.0625
Outputs:
- layer_out: bfloat16 [16, 2, 512, 1536], P('fsdp', None, 'ctx')
- input_grad: float32 [16, 2, 512, 1536], P('fsdp', None, 'ctx')
- attn_gain_grad: float32 [1536], P(('ctx', 'fsdp'))
- q_weight_grad: float32 [1536, 1536], P(('ctx', 'fsdp'))
- q_bias_grad: float32 [1536], P(('ctx', 'fsdp'))
- k_weight_grad: float32 [1536, 256], P(('ctx', 'fsdp'))
- k_bias_grad: float32 [256], replicated
- v_weight_grad: float32 [1536, 256], P(('ctx', 'fsdp'))
- v_bias_grad: float32 [256], P(('ctx', 'fsdp'))
- o_weight_grad: float32 [1536, 1536], P(('ctx', 'fsdp'))
- mlp_gain_grad: float32 [1536], P(('ctx', 'fsdp'))
- gate_weight_grad: float32 [1536, 8960], P(('ctx', 'fsdp'))
- up_weight_grad: float32 [1536, 8960], P(('ctx', 'fsdp'))
- down_weight_grad: float32 [1536, 8960], P(('ctx', 'fsdp'))
The draws below stay inside these ranges and needn't reach their ends.
All inputs are finite; a program needn't handle non-finite values.
Results may differ from the reference program's by a relative error of at most 0.029.
Values may be sent and summed in bfloat16 or wider, within the bound.
No kernel may reach another device: no remote copies, remote signals or barrier semaphores. Data moves between devices by JAX's collectives and lax.ppermute only.
A program may use at most 320 MiB of HBM per device.

```python
import math
import jax
import jax.numpy as jnp
from jax import lax

D = 1536
H = 12
KVH = 2
HD = 128
FF = 8960
SEQ_LEN = 1024
SEQS = 16
HALF = 512
BLK = 64
N_CTX = 8


def block_levels(key, dims, pieces, low, largest):
    loudness, own = 1.0, jax.random.fold_in(key, 6)
    for position, blocks in pieces:
        heights = jnp.exp(jax.random.uniform(jax.random.fold_in(own, position), (blocks,), jnp.float32, low / len(pieces), largest / len(pieces)))
        loudness = loudness * jnp.repeat(heights, dims[position] // blocks).reshape([-1 if axis == position else 1 for axis in range(len(dims))])
    return loudness


def normal_values(stream_key, extent, scale, limit, split=(), held_as=jnp.bfloat16):
    values = jax.random.normal(stream_key, extent, jnp.float32) * scale
    if len(split) > 0:
        values = block_levels(stream_key, extent, split, -0.22, 0.18) * values
    return jnp.clip(values, min=-limit, max=limit).astype(held_as)


def setup_inputs(seed: int = 0) -> dict:
    keys = jax.random.split(jax.random.key(seed), 15)
    tokens = normal_values(keys[0], (SEQS, 2, HALF, D), 1.0, 6.0, ((0, 16), (2, 8)))
    cotangent = normal_values(keys[1], (SEQS, 2, HALF, D), 1.0, 6.0, ((0, 16), (2, 8)))
    attn_gain = jnp.clip(1.0 + 0.18 * jax.random.normal(keys[2], (D,), jnp.float32), 0.099609375, 1.8984375).astype(jnp.bfloat16)
    q_weight = normal_values(keys[3], (D, H * HD), D ** -0.5, 0.15625, ((0, 128),))
    q_bias = normal_values(keys[4], (H * HD,), 0.5, 3.0, ((0, 128),))
    k_weight = normal_values(keys[5], (D, KVH * HD), D ** -0.5, 0.15625, ((0, 128),))
    k_bias = normal_values(keys[6], (KVH * HD,), 0.5, 3.0, ((0, 128),))
    v_weight = normal_values(keys[7], (D, KVH * HD), D ** -0.5, 0.15625, ((0, 128),))
    v_bias = normal_values(keys[8], (KVH * HD,), 0.2, 1.1953125, ((0, 128),))
    o_weight = normal_values(keys[9], (D, H * HD), 64 ** -0.5, 0.75, ((0, 128),))
    mlp_gain = jnp.clip(1.0 + 0.18 * jax.random.normal(keys[10], (D,), jnp.float32), 0.099609375, 1.8984375).astype(jnp.bfloat16)
    gate_weight = normal_values(keys[11], (D, FF), D ** -0.5, 0.15625, ((0, 128),))
    up_weight = normal_values(keys[12], (D, FF), D ** -0.5, 0.15625, ((0, 128),))
    down_weight = normal_values(keys[13], (D, FF), FF ** -0.5, 0.0625, ((0, 128),))
    return {"tokens": tokens, "cotangent": cotangent, "attn_gain": attn_gain, "q_weight": q_weight, "q_bias": q_bias, "k_weight": k_weight, "k_bias": k_bias, "v_weight": v_weight, "v_bias": v_bias, "o_weight": o_weight, "mlp_gain": mlp_gain, "gate_weight": gate_weight, "up_weight": up_weight, "down_weight": down_weight}


epsilon = 1e-06
rope_base = 1000000.0
highest = lax.Precision.HIGHEST

@jax.custom_vjp
def low(v):
    return lax.optimization_barrier(v.astype(jnp.bfloat16)).astype(jnp.float32)

@jax.custom_vjp
def low_back(v):
    return v

def low_keep(v):
    return (low(v), None)

def low_pass(kept, grad):
    return (grad,)

def back_keep(v):
    return (v, None)

def back_low(kept, grad):
    return (low(grad),)
low.defvjp(low_keep, low_pass)
low_back.defvjp(back_keep, back_low)

def rope_tables(positions):
    half_dim = HD // 2
    frequency = jnp.exp(jnp.arange(half_dim, dtype=jnp.float32) * (-2.0 * math.log(rope_base) / HD))
    angles = positions.astype(jnp.float32)[:, None] * frequency[None, :]
    cosine_tab = jnp.cos(angles)
    sine_tab = jnp.sin(angles)
    return (jnp.concatenate([cosine_tab, cosine_tab], -1), jnp.concatenate([sine_tab, sine_tab], -1))

def rotate(values, cosine_tab, sine_tab):
    half_dim = values.shape[-1] // 2
    turned = jnp.concatenate([-values[..., half_dim:], values[..., :half_dim]], -1)
    return values * cosine_tab + turned * sine_tab

def rms_unit(values):
    return values * lax.rsqrt(lax.optimization_barrier(jnp.mean(values * values, axis=-1, keepdims=True)) + epsilon)

def matmul(left_arr, right_arr):
    return jnp.einsum('gld,de->gle', left_arr, right_arr, precision=highest)

def decoder_layer(group_in, attn_gain, q_weight, q_bias, k_weight, k_bias, v_weight, v_bias, o_weight, mlp_gain, gate_weight, up_weight, down_weight):
    group_count = group_in.shape[0]
    length = group_in.shape[1]
    score_scale = 1.0 / math.sqrt(HD)
    positions = jnp.arange(length, dtype=jnp.int32)
    cosine_tab, sine_tab = rope_tables(positions)
    cosine_b = cosine_tab[None, :, None, :]
    sine_b = sine_tab[None, :, None, :]
    normed_one = low(rms_unit(group_in) * attn_gain)
    query_lin = low_back(matmul(normed_one, q_weight) + q_bias)
    key_lin = low_back(matmul(normed_one, k_weight) + k_bias)
    value_low = low(low_back(matmul(normed_one, v_weight) + v_bias))
    query_rot = low(rotate(query_lin.reshape(group_count, length, H, HD), cosine_b, sine_b))
    key_rot = low(rotate(key_lin.reshape(group_count, length, KVH, HD), cosine_b, sine_b))
    query_heads = query_rot.reshape(group_count, length, KVH, H // KVH, HD)
    value_heads = value_low.reshape(group_count, length, KVH, HD)
    scores = low_back(jnp.einsum('glkrd,gmkd->gkrlm', query_heads, key_rot, precision=highest) * score_scale)
    visible = positions[:, None] >= positions[None, :]
    masked = jnp.where(visible, scores, -jnp.inf)
    row_max = lax.optimization_barrier(jnp.max(masked, axis=-1, keepdims=True))
    exp_terms = jnp.exp(masked - row_max)
    probs = exp_terms / lax.optimization_barrier(jnp.sum(exp_terms, axis=-1, keepdims=True))
    context = jnp.einsum('gkrlm,gmkd->glkrd', low(probs), value_heads, precision=highest)
    context_low = low(low_back(context.reshape(group_count, length, H * HD)))
    branch_one = low_back(jnp.einsum('gle,de->gld', context_low, o_weight, precision=highest))
    hidden_one = group_in + branch_one
    normed_two = low(rms_unit(hidden_one) * mlp_gain)
    gate_val = low_back(matmul(normed_two, gate_weight))
    up_val = low_back(matmul(normed_two, up_weight))
    mixed_low = low(jax.nn.silu(gate_val) * up_val)
    branch_two = low_back(jnp.einsum('glf,df->gld', mixed_low, down_weight, precision=highest))
    return hidden_one + branch_two

def to_natural(arranged):
    first_half = arranged[:, 0]
    second_half = arranged[:, 1].reshape(SEQS, N_CTX, BLK, D)[:, ::-1].reshape(SEQS, HALF, D)
    return jnp.concatenate([first_half, second_half], axis=1)

def to_arranged(natural):
    first_half = natural[:, :HALF]
    second_half = natural[:, HALF:].reshape(SEQS, N_CTX, BLK, D)[:, ::-1].reshape(SEQS, HALF, D)
    return jnp.stack([first_half, second_half], axis=1)

def reference(tokens, cotangent, attn_gain, q_weight, q_bias, k_weight, k_bias, v_weight, v_bias, o_weight, mlp_gain, gate_weight, up_weight, down_weight):
    weights = tuple((weight_arr.astype(jnp.float32) for weight_arr in (attn_gain, q_weight, q_bias, k_weight, k_bias, v_weight, v_bias, o_weight, mlp_gain, gate_weight, up_weight, down_weight)))
    per_group = 4 if SEQS % 4 == 0 else 1
    inputs = to_natural(tokens.astype(jnp.float32)).reshape(SEQS // per_group, per_group, SEQ_LEN, D)
    grads_in = to_natural(cotangent.astype(jnp.float32)).reshape(SEQS // per_group, per_group, SEQ_LEN, D)

    def group_step(running, group_pair):
        group_in, group_ct = group_pair
        result, pullback = jax.vjp(decoder_layer, group_in, *weights)
        pulled = pullback(group_ct)
        running = tuple((running_sum + new_grad for running_sum, new_grad in zip(running, pulled[1:])))
        return (running, (result, pulled[0]))
    zero_grads = tuple((jnp.zeros(weight_arr.shape, jnp.float32) for weight_arr in weights))
    totals, (results, input_grads) = lax.scan(group_step, zero_grads, (inputs, grads_in))
    layer_out = to_arranged(results.reshape(SEQS, SEQ_LEN, D)).astype(jnp.bfloat16)
    input_grad = to_arranged(input_grads.reshape(SEQS, SEQ_LEN, D))
    return (layer_out, input_grad, totals[0], totals[1], totals[2], totals[3], totals[4], totals[5], totals[6], totals[7], totals[8], totals[9], totals[10], totals[11])
```

```python
import math

import jax
import jax.numpy as jnp
from jax import lax
from jax.sharding import Mesh, PartitionSpec as P

H = 12
KVH = 2
HD = 128
GROUP = H // KVH
D = 1536
FF = 8960
BLK = 64
N_CTX = 8
ROWS = 12
PAD = 16
FFS = 1152
HALF_Q = GROUP * HD
QKV = HALF_Q + 2 * HD
MISC = 128
QKVM = QKV + MISC
FFW = 3 * FFS

epsilon = 1e-06
rope_base = 1000000.0

AXES = ("yh", "x", "z", "yl", "core")
Y = ("yh", "yl")
CTX = ("yh", "x")
TP = ("x", "core")
F32 = jnp.float32
BF = jnp.bfloat16
REL = (0, 3, 1, 2)


def shift(arr, axis, by):
    return lax.ppermute(arr, axis, [(i, (i + by) % 4) for i in range(4)])


def swap_core(arr):
    return lax.ppermute(arr, "core", [(0, 1), (1, 0)])


def ring_pieces(arr, axis):
    half = arr.shape[0] // 2
    prev = shift(arr, axis, 1)
    nxt = shift(arr, axis, 3)
    far_a = shift(prev[:half], axis, 1)
    far_b = shift(nxt[half:], axis, 3)
    return [arr, prev, nxt, jnp.concatenate([far_a, far_b], 0)]


def add_low(left, right):
    return (left.astype(F32) + right.astype(F32)).astype(BF)


def ring_reduce(pieces, axis):
    own, to_prev, to_next, far = pieces
    half = own.shape[0] // 2
    in_next = shift(far[:half], axis, 1)
    in_prev = shift(far[half:], axis, 3)
    to_next = jnp.concatenate([add_low(to_next[:half], in_next), to_next[half:]], 0)
    to_prev = jnp.concatenate([to_prev[:half], add_low(to_prev[half:], in_prev)], 0)
    from_prev = shift(to_next, axis, 1)
    from_next = shift(to_prev, axis, 3)
    return (own.astype(F32) + from_prev.astype(F32) + from_next.astype(F32)).astype(BF)


def gather_yz(block_a, block_b):
    first_a = jnp.concatenate(ring_pieces(block_a, "z"), 0)
    first_b = jnp.concatenate(ring_pieces(block_b, Y), 0)
    last_a = ring_pieces(first_a, Y)
    last_b = ring_pieces(first_b, "z")
    rows = block_b.shape[0]
    whole_a = jnp.concatenate(last_a, 0)
    whole_b = jnp.concatenate(
        [last_b[zr][yr * rows : (yr + 1) * rows] for yr in range(4) for zr in range(4)], 0
    )
    return whole_a, whole_b


def reduce_yz(whole_a, whole_b):
    rows = whole_b.shape[0] // 16
    first_a = [whole_a[4 * rows * p : 4 * rows * (p + 1)] for p in range(4)]
    first_b = [
        jnp.concatenate(
            [whole_b[(4 * yr + zr) * rows : (4 * yr + zr + 1) * rows] for yr in range(4)], 0
        )
        for zr in range(4)
    ]
    sum_a = ring_reduce(first_a, Y)
    sum_b = ring_reduce(first_b, "z")
    last_a = [sum_a[rows * p : rows * (p + 1)] for p in range(4)]
    last_b = [sum_b[rows * p : rows * (p + 1)] for p in range(4)]
    return ring_reduce(last_a, "z"), ring_reduce(last_b, Y)


def rope_tables(positions):
    half_dim = HD // 2
    frequency = jnp.exp(
        jnp.arange(half_dim, dtype=F32) * (-2.0 * math.log(rope_base) / HD)
    )
    angles = positions.astype(F32)[:, None] * frequency[None, :]
    cosine_tab = jnp.cos(angles)
    sine_tab = jnp.sin(angles)
    return (
        jnp.concatenate([cosine_tab, cosine_tab], -1),
        jnp.concatenate([sine_tab, sine_tab], -1),
    )


def rotate(values, cosine_tab, sine_tab):
    half_dim = values.shape[-1] // 2
    turned = jnp.concatenate([-values[..., half_dim:], values[..., :half_dim]], -1)
    return values * cosine_tab + turned * sine_tab


def unrotate(grads_in, cosine_tab, sine_tab):
    half_dim = grads_in.shape[-1] // 2
    scaled = grads_in * sine_tab
    return grads_in * cosine_tab + jnp.concatenate(
        [scaled[..., half_dim:], -scaled[..., :half_dim]], -1
    )


def product(left_arr, right_arr):
    return jnp.dot(left_arr, right_arr, preferred_element_type=F32)


def against(left_arr, right_arr):
    return lax.dot_general(
        left_arr, right_arr, (((1,), (1,)), ((), ())), preferred_element_type=F32
    )


def over_rows(left_arr, right_arr):
    return lax.dot_general(
        left_arr, right_arr, (((0,), (0,)), ((), ())), preferred_element_type=F32
    )


def per_device(
    tokens,
    cotangent,
    attn_gain,
    q_weight,
    q_bias,
    k_weight,
    k_bias,
    v_weight,
    v_bias,
    o_weight,
    mlp_gain,
    gate_weight,
    up_weight,
    down_weight,
):
    yh, x, z, yl, core = [lax.axis_index(a) for a in AXES]
    y = yh * 2 + yl
    ctx_rank = yh * 4 + x
    row_count = 2 * BLK
    score_scale = 1.0 / math.sqrt(HD)
    is_zero = core == 0

    place = jnp.arange(D, dtype=jnp.int32)
    rel = jnp.array(REL, jnp.int32)

    def rel_of(index):
        return jnp.where(index == 0, 0, jnp.where(index == 1, 3, index - 1))

    place_r = place % ROWS
    place_x = place // ROWS % 4
    place_c = place // (ROWS * 4) % 2
    place_z = (z + rel_of(place // (ROWS * 8) % 4)) % 4
    place_y = (y + rel_of(place // (ROWS * 32))) % 4
    place_dev = (((place_y // 2 * 4 + place_x) * 4 + place_z) * 2 + place_y % 2) * 2 + place_c
    natural = place_dev * ROWS + place_r
    to_order = (place[:, None] == natural[None, :]).astype(BF)

    def padded(arr):
        return jnp.pad(arr, ((0, PAD - ROWS), (0, 0)))

    misc = jnp.concatenate(
        [
            attn_gain[:, None],
            mlp_gain[:, None],
            q_bias[:, None],
            jnp.pad(k_bias[:, None], ((0, ROWS - 2), (0, 0))),
            jnp.pad(v_bias[:, None], ((0, ROWS - 2), (0, 0))),
            jnp.zeros((ROWS, MISC - 5), BF),
        ],
        1,
    )

    def side(h):
        return [
            q_weight[:, h * HALF_Q : (h + 1) * HALF_Q],
            k_weight[:, h * HD : (h + 1) * HD],
            v_weight[:, h * HD : (h + 1) * HD],
            misc,
            o_weight[:, h * HALF_Q : (h + 1) * HALF_Q],
        ]

    attn_pack = padded(jnp.concatenate(side(0) + side(1), 1))
    side_width = QKVM + HALF_Q
    along_x = jnp.concatenate(
        [attn_pack, shift(attn_pack, "x", 1), shift(attn_pack, "x", 3), shift(attn_pack, "x", 2)],
        0,
    )
    left_side, right_side = along_x[:, :side_width], along_x[:, side_width:]
    keep_side = jnp.where(is_zero, left_side, right_side)
    send_side = jnp.where(is_zero, right_side, left_side)
    both_rows = jnp.concatenate([keep_side, swap_core(send_side)], 0)
    want = jnp.arange(8 * ROWS, dtype=jnp.int32)
    want_c = want // (4 * ROWS)
    want_x = want // ROWS % 4
    x_off = (want_x - x) % 4
    x_rel = jnp.where(x_off == 0, 0, jnp.where(x_off == 3, 1, x_off + 1))
    at = ((want_c ^ core) * 4 + x_rel) * PAD + want % ROWS
    pick = (at[:, None] == jnp.arange(8 * PAD, dtype=jnp.int32)[None, :]).astype(BF)
    attn_rows = product(pick, both_rows).astype(BF)
    cut_q, cut_o = 5 * HD, 3 * HD
    qkv_a, qkv_b = gather_yz(attn_rows[:, :cut_q], attn_rows[:, cut_q:QKVM])
    qkvm_own = jnp.concatenate([qkv_a, qkv_b], 1)
    weight_own = qkvm_own[:, :QKV]
    weight_sib = swap_core(weight_own)
    o_a, o_b = gather_yz(
        attn_rows[:, QKVM : QKVM + cut_o], attn_rows[:, QKVM + cut_o :]
    )
    o_own = jnp.concatenate([o_a, o_b], 1)
    o_sib = swap_core(o_own)

    def ff_padded(arr):
        return jnp.pad(arr, ((0, PAD - ROWS), (0, 8 * FFS - FF)))

    ff_arrs = [ff_padded(a) for a in (gate_weight, up_weight, down_weight)]
    ff_send = jnp.stack(
        [
            jnp.concatenate([a[:, t * FFS : (t + 1) * FFS] for a in ff_arrs], 1)
            for t in range(8)
        ]
    )
    ff_got = lax.all_to_all(ff_send, TP, split_axis=0, concat_axis=0, tiled=True)
    ff_at = (want_x * 2 + want_c) * PAD + want % ROWS
    ff_pick = (ff_at[:, None] == jnp.arange(8 * PAD, dtype=jnp.int32)[None, :]).astype(BF)
    ff_rows = product(ff_pick, ff_got.reshape(8 * PAD, FFW)).astype(BF)
    cut_f = 14 * HD
    ff_a, ff_b = gather_yz(ff_rows[:, :cut_f], ff_rows[:, cut_f:])
    ff_all = jnp.concatenate([ff_a, ff_b], 1)
    weight_gate = ff_all[:, :FFS]
    weight_up = ff_all[:, FFS : 2 * FFS]
    weight_down = ff_all[:, 2 * FFS :]

    misc_rows = against(
        (jnp.arange(8)[:, None] == jnp.arange(MISC)[None, :]).astype(BF), qkvm_own[:, QKV:]
    )
    gain_one = misc_rows[0:1]
    gain_two = misc_rows[1:2]
    bias_rows = misc_rows.astype(BF)
    bias_q = against(bias_rows[2:3], to_order).reshape(2, HALF_Q)
    small = jnp.arange(KVH * HD, dtype=jnp.int32)
    to_small = (
        (place_dev * 2 + place_r)[:, None] == small[None, :]
    ) & (place_r < 2)[:, None]
    bias_kv = product(bias_rows[3:5], to_small.astype(BF))
    bias_k = bias_kv[0].reshape(2, HD)
    bias_v = bias_kv[1].reshape(2, HD)

    def sided(pair):
        return jnp.where(is_zero, pair, pair[::-1])

    bias_q, bias_k, bias_v = sided(bias_q), sided(bias_k), sided(bias_v)

    offsets = jnp.arange(BLK, dtype=jnp.int32)
    query_pos = jnp.concatenate(
        [ctx_rank * BLK + offsets, (2 * N_CTX - 1 - ctx_rank) * BLK + offsets]
    )
    sources = ctx_rank ^ jnp.arange(N_CTX, dtype=jnp.int32)
    key_pos = jnp.stack(
        [
            sources[:, None] * BLK + offsets[None, :],
            (2 * N_CTX - 1 - sources)[:, None] * BLK + offsets[None, :],
        ],
        1,
    ).reshape(-1)
    visible = query_pos[:, None] >= key_pos[None, :]
    cosine_tab, sine_tab = rope_tables(query_pos)
    cosine_b = cosine_tab[:, None, :]
    sine_b = sine_tab[:, None, :]

    inputs_low = product(tokens.reshape(row_count, D), to_order).astype(BF)
    grad_low = product(cotangent.reshape(row_count, D), to_order).astype(BF)
    inputs = inputs_low.astype(F32)
    grad_out = grad_low.astype(F32)
    grad_rows = lax.all_gather(grad_low, TP, axis=0, tiled=True)

    scale_one = lax.rsqrt(jnp.mean(inputs * inputs, axis=-1, keepdims=True) + epsilon)
    unit_one = inputs * scale_one
    normed_one = (unit_one * gain_one).astype(BF)
    lin = [product(normed_one, weight_own), product(normed_one, weight_sib)]
    query_lin = jnp.stack([lin[s][:, :HALF_Q] + bias_q[s] for s in range(2)], 1)
    key_lin = jnp.stack([lin[s][:, HALF_Q : HALF_Q + HD] + bias_k[s] for s in range(2)], 1)
    value_low = jnp.stack([lin[s][:, HALF_Q + HD :] + bias_v[s] for s in range(2)], 1).astype(BF)
    query_rot = rotate(
        query_lin.reshape(row_count, H, HD), cosine_b, sine_b
    ).astype(BF).reshape(row_count, KVH, GROUP, HD)
    key_rot = rotate(key_lin, cosine_b, sine_b).astype(BF)
    kv_send = jnp.concatenate(
        [key_rot.reshape(row_count, KVH * HD), value_low.reshape(row_count, KVH * HD)], 1
    )

    def to_ctx(arr, k):
        return lax.ppermute(arr, CTX, [(i, i ^ k) for i in range(N_CTX)])

    kv_all = jnp.concatenate([kv_send] + [to_ctx(kv_send, k) for k in range(1, N_CTX)], 0)
    key_heads = kv_all[:, : KVH * HD].reshape(N_CTX * row_count, KVH, HD)
    value_heads = kv_all[:, KVH * HD :].reshape(N_CTX * row_count, KVH, HD)
    scores = (
        jnp.einsum("lkrd,mkd->krlm", query_rot, key_heads, preferred_element_type=F32)
        * score_scale
    )
    masked = jnp.where(visible, scores, -jnp.inf)
    row_max = jnp.max(masked, axis=-1, keepdims=True)
    exp_terms = jnp.exp(masked - row_max)
    row_sum = jnp.sum(exp_terms, axis=-1, keepdims=True)
    probs = exp_terms / row_sum
    probs_low = probs.astype(BF)
    context = jnp.einsum("krlm,mkd->lkrd", probs_low, value_heads, preferred_element_type=F32)
    context_low = context.reshape(row_count, H * HD).astype(BF)
    hidden_one = (
        inputs
        + against(context_low[:, :HALF_Q], o_own)
        + against(context_low[:, HALF_Q:], o_sib)
    )
    scale_two = lax.rsqrt(jnp.mean(hidden_one * hidden_one, axis=-1, keepdims=True) + epsilon)
    unit_two = hidden_one * scale_two
    normed_two = (unit_two * gain_two).astype(BF)

    normed_rows = lax.all_gather(normed_two, TP, axis=0, tiled=True)
    grad_mixed = product(grad_rows, weight_down)
    gate_val = product(normed_rows, weight_gate)
    up_val = product(normed_rows, weight_up)
    gate_sig = jax.nn.sigmoid(gate_val)
    swish = gate_val * gate_sig
    mixed_low = (swish * up_val).astype(BF)
    grad_up = (grad_mixed * swish).astype(BF)
    grad_gate = (grad_mixed * up_val * gate_sig * (1.0 + gate_val * (1.0 - gate_sig))).astype(BF)
    grad_norm_part = (against(grad_gate, weight_gate) + against(grad_up, weight_up)).astype(BF)
    grad_norm_two = lax.psum_scatter(
        grad_norm_part, TP, scatter_dimension=0, tiled=True
    ).astype(F32)
    down_part = against(mixed_low, weight_down).astype(BF)
    down_terms = lax.psum_scatter(down_part, TP, scatter_dimension=0, tiled=True)
    layer_sum = (hidden_one + down_terms.astype(F32)).astype(BF)
    layer_out = against(layer_sum, to_order).astype(BF).reshape(tokens.shape)
    ff_grads = jnp.concatenate(
        [
            over_rows(normed_rows, grad_gate).astype(BF),
            over_rows(normed_rows, grad_up).astype(BF),
            over_rows(grad_rows, mixed_low).astype(BF),
        ],
        1,
    )
    ff_sum_a, ff_sum_b = reduce_yz(ff_grads[:, :cut_f], ff_grads[:, cut_f:])
    ff_sum = jnp.concatenate([ff_sum_a, ff_sum_b], 1)
    ff_back = lax.dot_general(
        ff_pick, ff_sum, (((0,), (0,)), ((), ())), preferred_element_type=F32
    ).astype(BF)
    ff_back = lax.all_to_all(
        ff_back.reshape(8, PAD, FFW), TP, split_axis=0, concat_axis=0, tiled=True
    )
    gate_weight_grad, up_weight_grad, down_weight_grad = [
        jnp.concatenate(
            [ff_back[t, :ROWS, i * FFS : (i + 1) * FFS] for t in range(8)], 1
        )[:, :FF].astype(F32)
        for i in range(3)
    ]

    gain_two_term = jnp.sum(grad_norm_two * unit_two, axis=0)
    grad_unit_two = grad_norm_two * gain_two
    grad_hidden = grad_out + scale_two * (
        grad_unit_two - unit_two * jnp.mean(grad_unit_two * unit_two, axis=-1, keepdims=True)
    )
    grad_branch = grad_hidden.astype(BF)
    grad_context = jnp.concatenate(
        [product(grad_branch, o_own), product(grad_branch, o_sib)], 1
    ).astype(BF)
    grad_ctx_heads = grad_context.reshape(row_count, KVH, GROUP, HD)
    grad_probs = jnp.einsum(
        "lkrd,mkd->krlm", grad_ctx_heads, value_heads, preferred_element_type=F32
    )
    row_delta = jnp.sum(probs * grad_probs, axis=-1, keepdims=True)
    grad_scores = (probs * (grad_probs - row_delta)).astype(BF)
    grad_query = (
        jnp.einsum("krlm,mkd->lkrd", grad_scores, key_heads, preferred_element_type=F32)
        * score_scale
    )
    grad_key_all = (
        jnp.einsum("krlm,lkrd->mkd", grad_scores, query_rot, preferred_element_type=F32)
        * score_scale
    )
    grad_value_all = jnp.einsum(
        "krlm,lkrd->mkd", probs_low, grad_ctx_heads, preferred_element_type=F32
    )
    grad_kv = jnp.concatenate(
        [
            grad_key_all.reshape(N_CTX * row_count, KVH * HD),
            grad_value_all.reshape(N_CTX * row_count, KVH * HD),
        ],
        1,
    ).astype(BF)
    grad_kv_sum = grad_kv[:row_count].astype(F32)
    for k in range(1, N_CTX):
        grad_kv_sum = grad_kv_sum + to_ctx(
            grad_kv[k * row_count : (k + 1) * row_count], k
        ).astype(F32)
    grad_key = grad_kv_sum[:, : KVH * HD].reshape(row_count, KVH, HD)
    grad_q_lin = unrotate(grad_query.reshape(row_count, H, HD), cosine_b, sine_b).astype(BF)
    grad_q_lin = grad_q_lin.reshape(row_count, KVH, HALF_Q)
    grad_k_lin = unrotate(grad_key, cosine_b, sine_b).astype(BF)
    grad_v_lin = grad_kv_sum[:, KVH * HD :].astype(BF).reshape(row_count, KVH, HD)
    grad_lin = [
        jnp.concatenate([grad_q_lin[:, s], grad_k_lin[:, s], grad_v_lin[:, s]], 1)
        for s in range(2)
    ]
    grad_norm_one = against(grad_lin[0], weight_own) + against(grad_lin[1], weight_sib)
    gain_one_term = jnp.sum(grad_norm_one * unit_one, axis=0)
    grad_unit_one = grad_norm_one * gain_one
    input_grad = grad_hidden + scale_one * (
        grad_unit_one - unit_one * jnp.mean(grad_unit_one * unit_one, axis=-1, keepdims=True)
    )
    input_high = input_grad.astype(BF)
    input_rest = (input_grad - input_high.astype(F32)).astype(BF)
    input_grad = (against(input_high, to_order) + against(input_rest, to_order)).reshape(
        tokens.shape
    )

    def unsided(pair):
        return jnp.where(is_zero, pair, pair[::-1])

    q_bias_term = unsided(jnp.sum(grad_q_lin.astype(F32), axis=0)).reshape(1, D)
    k_bias_term = unsided(jnp.sum(grad_k_lin.astype(F32), axis=0)).reshape(1, KVH * HD)
    v_bias_term = unsided(jnp.sum(grad_v_lin.astype(F32), axis=0)).reshape(1, KVH * HD)
    k_bias_grad = jnp.pad(k_bias_term, ((0, 7), (0, 0)))
    k_bias_grad = k_bias_grad + swap_core(k_bias_grad)
    for axis in ("x", Y, "z"):
        for k in (1, 2):
            k_bias_grad = k_bias_grad + lax.ppermute(
                k_bias_grad, axis, [(i, i ^ k) for i in range(4)]
            )
    k_bias_grad = k_bias_grad[0]
    q_bias_ordered = product(q_bias_term.astype(BF), to_order)
    v_bias_ordered = against(v_bias_term.astype(BF), to_small.astype(BF))
    terms = jnp.concatenate(
        [
            gain_one_term[None],
            gain_two_term[None],
            q_bias_ordered,
            jnp.zeros((1, D), F32),
            v_bias_ordered,
            jnp.zeros((3, D), F32),
        ],
        0,
    ).astype(BF)
    misc_grad = over_rows(
        terms, (jnp.arange(8)[:, None] == jnp.arange(MISC)[None, :]).astype(BF)
    ).astype(BF)

    def to_owners(own, sib, cut):
        total = add_low(own, swap_core(sib))
        part_a, part_b = reduce_yz(total[:, :cut], total[:, cut:])
        part = jnp.concatenate([part_a, part_b], 1)
        spread_at = (place_spread := jnp.arange(8 * PAD, dtype=jnp.int32))
        sp_xr = place_spread // (2 * PAD)
        sp_c = place_spread // PAD % 2
        sp_r = place_spread % PAD
        sp_x = (x + jnp.where(sp_xr == 0, 0, jnp.where(sp_xr == 1, 3, sp_xr - 1))) % 4
        source = jnp.where(sp_r < ROWS, (sp_c * 4 + sp_x) * ROWS + sp_r, -1)
        spread = (source[:, None] == jnp.arange(8 * ROWS)[None, :]).astype(BF)
        spaced = product(spread, part).astype(BF)
        two = 2 * PAD
        mine = spaced[:two].astype(F32)
        mine = mine + shift(spaced[two : 2 * two], "x", 3).astype(F32)
        mine = mine + shift(spaced[2 * two : 3 * two], "x", 1).astype(F32)
        mine = mine + shift(spaced[3 * two :], "x", 2).astype(F32)
        mine = mine.astype(BF)
        keep = jnp.where(is_zero, mine[:PAD], mine[PAD:])
        give = jnp.where(is_zero, mine[PAD:], mine[:PAD])
        got = swap_core(give)
        side0 = jnp.where(is_zero, keep, got)[:ROWS].astype(F32)
        side1 = jnp.where(is_zero, got, keep)[:ROWS].astype(F32)
        return side0, side1

    o_grads = to_owners(
        over_rows(grad_branch, context_low[:, :HALF_Q]).astype(BF),
        over_rows(grad_branch, context_low[:, HALF_Q:]).astype(BF),
        cut_o,
    )
    o_weight_grad = jnp.concatenate(o_grads, 1)
    qkvm_grads = to_owners(
        jnp.concatenate([over_rows(normed_one, grad_lin[0]).astype(BF), misc_grad], 1),
        jnp.concatenate([over_rows(normed_one, grad_lin[1]).astype(BF), misc_grad], 1),
        cut_q,
    )
    q_weight_grad = jnp.concatenate([g[:, :HALF_Q] for g in qkvm_grads], 1)
    k_weight_grad = jnp.concatenate([g[:, HALF_Q : HALF_Q + HD] for g in qkvm_grads], 1)
    v_weight_grad = jnp.concatenate([g[:, HALF_Q + HD : QKV] for g in qkvm_grads], 1)
    misc_mine = qkvm_grads[0][:, QKV:]
    attn_gain_grad = misc_mine[:, 0]
    mlp_gain_grad = misc_mine[:, 1]
    q_bias_grad = misc_mine[:, 2]
    v_bias_grad = misc_mine[:2, 4]
    return (
        layer_out,
        input_grad,
        attn_gain_grad,
        q_weight_grad,
        q_bias_grad,
        k_weight_grad,
        k_bias_grad,
        v_weight_grad,
        v_bias_grad,
        o_weight_grad,
        mlp_gain_grad,
        gate_weight_grad,
        up_weight_grad,
        down_weight_grad,
    )


def solution(mesh):
    fine = Mesh(mesh.devices.reshape(2, 4, 4, 2, 2), AXES)
    acts = P(("z", "yl", "core"), None, CTX, None)
    vec, mat = P(AXES), P(AXES, None)
    return jax.shard_map(
        per_device,
        mesh=fine,
        in_specs=(acts, acts, vec, mat, vec, mat, vec, mat, vec, mat, vec, mat, mat, mat),
        out_specs=(acts, acts, vec, mat, vec, mat, P(), mat, vec, mat, vec, mat, mat, mat),
        check_vma=False,
    )
```

```python
import math

import jax
import jax.numpy as jnp
from jax import lax
from jax.experimental import pallas as pl
from jax.experimental.layout import Layout, with_layout_constraint
from jax.experimental.pallas import tpu as pltpu
from jax.sharding import Mesh, PartitionSpec as P

H = 12
KVH = 2
HD = 128
GROUP = H // KVH
D = 1536
FF = 8960
BLK = 64
N_CTX = 8
ROWS = 12
PAD = 16
FFS = 1152
HALF_Q = GROUP * HD
QKV = HALF_Q + 2 * HD
MISC = 128
QKVM = QKV + MISC
FFW = 3 * FFS
SIDE = QKVM + HALF_Q

epsilon = 1e-06
rope_base = 1000000.0

AXES = ("yh", "x", "z", "yl", "core")
Y = ("yh", "yl")
CTX = ("yh", "x")
TP = ("x", "core")
F32 = jnp.float32
BF = jnp.bfloat16


def add_low(left, right):
    return (left.astype(F32) + right.astype(F32)).astype(BF)


def swap_core(arr):
    return lax.ppermute(arr, "core", [(0, 1), (1, 0)])


def swap_yh(arr):
    return lax.ppermute(arr, "yh", [(0, 1), (1, 0)])


def to_x(arr, k):
    return lax.ppermute(arr, "x", [(i, i ^ k) for i in range(4)])


def after(arr, *earlier):
    return lax.optimization_barrier((arr,) + earlier)[0]


def row_major(arr):
    return with_layout_constraint(arr, Layout(major_to_minor=(0, 1)))


def exchange(arr, axis):
    return lax.all_to_all(arr, axis, split_axis=0, concat_axis=0, tiled=True)


def spread(block, axis, count):
    return exchange(jnp.tile(block, (count, 1)), axis)


def neighbours(block):
    mine = jnp.concatenate([block] + [to_x(block, k) for k in range(1, 4)], 0)
    return mine, swap_core(mine)


def neighbours_sum(mine):
    rows = mine.shape[0] // 4
    total = mine[:rows].astype(F32)
    for k in range(1, 4):
        total = total + to_x(mine[k * rows : (k + 1) * rows], k).astype(F32)
    return total


def collect(whole, axis, count):
    got = exchange(whole, axis).reshape(count, whole.shape[0] // count, whole.shape[1])
    return jnp.sum(got.astype(F32), axis=0).astype(BF)


def rope_tables(positions):
    half_dim = HD // 2
    frequency = jnp.exp(
        jnp.arange(half_dim, dtype=F32) * (-2.0 * math.log(rope_base) / HD)
    )
    angles = positions.astype(F32)[:, None] * frequency[None, :]
    cosine_tab = jnp.cos(angles)
    sine_tab = jnp.sin(angles)
    return (
        jnp.concatenate([cosine_tab, cosine_tab], -1),
        jnp.concatenate([sine_tab, sine_tab], -1),
    )


def rotate(values, cosine_tab, sine_tab):
    half_dim = values.shape[-1] // 2
    turned = jnp.concatenate([-values[..., half_dim:], values[..., :half_dim]], -1)
    return values * cosine_tab + turned * sine_tab


def unrotate(grads_in, cosine_tab, sine_tab):
    half_dim = grads_in.shape[-1] // 2
    scaled = grads_in * sine_tab
    return grads_in * cosine_tab + jnp.concatenate(
        [scaled[..., half_dim:], -scaled[..., :half_dim]], -1
    )


def product(left_arr, right_arr):
    return jnp.dot(left_arr, right_arr, preferred_element_type=F32)


def against(left_arr, right_arr):
    return lax.dot_general(
        left_arr, right_arr, (((1,), (1,)), ((), ())), preferred_element_type=F32
    )


def over_rows(left_arr, right_arr):
    return lax.dot_general(
        left_arr, right_arr, (((0,), (0,)), ((), ())), preferred_element_type=F32
    )


VMEM = pl.BlockSpec(memory_space=pltpu.VMEM)
ANY = pl.BlockSpec(memory_space=pl.ANY)
MIB = 1 << 20


def call(body, outs, ins, out_specs, scratch=(), flops=0, moved=0, vmem=48 * MIB):
    return pl.pallas_call(
        body,
        out_shape=outs,
        in_specs=ins,
        out_specs=out_specs,
        scratch_shapes=scratch,
        compiler_params=pltpu.CompilerParams(vmem_limit_bytes=vmem),
        cost_estimate=pl.CostEstimate(flops=flops, bytes_accessed=moved, transcendentals=0),
    )


def fetch(sources, targets, sems):
    copies = [
        pltpu.make_async_copy(src, dst, sems.at[i])
        for i, (src, dst) in enumerate(zip(sources, targets))
    ]
    for one in copies:
        one.start()
    for one in copies:
        one.wait()


def pack_attn_body(vectors, q, k, v, o, out, q_v, k_v, v_v, o_v, square, sems):
    square[...] = jnp.zeros_like(square)
    start = 0
    for i, width in enumerate((ROWS, ROWS, ROWS, 2, 2)):
        square[i : i + 1, :width] = vectors[:, start : start + width].astype(F32)
        start += width
    misc = square[...].T[:PAD].astype(BF)
    fetch((q, k, v, o), (q_v, k_v, v_v, o_v), sems)
    for t in range(8):
        h = t % 2
        rows = slice(t * PAD, t * PAD + ROWS)
        out[t * PAD : (t + 1) * PAD, :] = jnp.zeros((PAD, SIDE), BF)
        out[rows, :HALF_Q] = q_v[:, h * HALF_Q : (h + 1) * HALF_Q]
        out[rows, HALF_Q : HALF_Q + HD] = k_v[:, h * HD : (h + 1) * HD]
        out[rows, HALF_Q + HD : QKV] = v_v[:, h * HD : (h + 1) * HD]
        out[t * PAD : (t + 1) * PAD, QKV:QKVM] = misc
        out[rows, QKVM:SIDE] = o_v[:, h * HALF_Q : (h + 1) * HALF_Q]


def pack_attn(vectors, *arrays):
    out = jax.ShapeDtypeStruct((8 * PAD, SIDE), BF)
    scratch = [pltpu.VMEM(a.shape, BF) for a in arrays]
    scratch += [pltpu.VMEM((MISC, MISC), F32), pltpu.SemaphoreType.DMA((4,))]
    return call(pack_attn_body, out, [VMEM] + [ANY] * 4, VMEM, scratch, moved=MIB)(
        vectors, *arrays
    )


def pack_ff_body(gate, up, down, out, gate_v, up_v, down_v, sems):
    fetch((gate, up, down), (gate_v, up_v, down_v), sems)
    for t in range(8):
        out[t * PAD : (t + 1) * PAD, :] = jnp.zeros((PAD, FFW), BF)
        width = min(FFS, FF - t * FFS)
        for i, ref in enumerate((gate_v, up_v, down_v)):
            out[t * PAD : t * PAD + ROWS, i * FFS : i * FFS + width] = ref[
                :, t * FFS : t * FFS + width
            ]


def pack_ff(*arrays):
    out = jax.ShapeDtypeStruct((8 * PAD, FFW), BF)
    scratch = [pltpu.VMEM(a.shape, BF) for a in arrays] + [pltpu.SemaphoreType.DMA((3,))]
    return call(pack_ff_body, out, [ANY] * 3, VMEM, scratch, moved=2 * MIB)(*arrays)


def unpack_body(
    mine, q_w, k_w, v_w, gate_w, up_w, q, k, v, o, gate, up, down, biases, gains
):
    def side(h, start, stop):
        return sum(
            mine[(2 * i + h) * PAD : (2 * i + h) * PAD + PAD, start:stop].astype(F32)
            for i in range(4)
        )

    def gain_part(weight, start, grad):
        width = grad.shape[1]
        part = weight[:, start : start + width].astype(F32) * grad
        return jnp.sum(part, axis=1, keepdims=True)

    attn = jnp.zeros((ROWS, 1), F32)
    for h in range(2):
        part = side(h, 0, QKV)
        biases[h : h + 1, :] = part[ROWS : ROWS + 1]
        for ref, weight, start, width in (
            (q, q_w, 0, HALF_Q),
            (k, k_w, HALF_Q, HD),
            (v, v_w, HALF_Q + HD, HD),
        ):
            piece = part[:ROWS, start : start + width]
            ref[:, h * width : (h + 1) * width] = piece
            attn = attn + gain_part(weight, h * width, piece)
        o[:, h * HALF_Q : (h + 1) * HALF_Q] = side(h, QKV + FFW, QKV + FFW + HALF_Q)[:ROWS]
    mlp = jnp.zeros((ROWS, 1), F32)
    for t in range(8):
        width = min(FFS, FF - t * FFS)
        for i, (ref, weight) in enumerate(((gate, gate_w), (up, up_w), (down, None))):
            start = QKV + i * FFS
            piece = mine[t * PAD : (t + 1) * PAD, start : start + width].astype(F32)[:ROWS]
            ref[:, t * FFS : t * FFS + width] = piece
            if weight is not None:
                mlp = mlp + gain_part(weight, t * FFS, piece)
    gains[:, 0:1] = attn
    gains[:, 1:2] = mlp


def unpack_grads(mine, *weights):
    shapes = [(ROWS, D), (ROWS, KVH * HD), (ROWS, KVH * HD), (ROWS, D)]
    shapes += [(ROWS, FF)] * 3 + [(2, QKV), (ROWS, 2)]
    outs = [jax.ShapeDtypeStruct(dims, F32) for dims in shapes]
    return call(unpack_body, outs, [VMEM] * 6, [VMEM] * 9, moved=5 * MIB)(mine, *weights)


def ffn_body(
    rows, others, grads, grads_others, weights, mixed, inner, back, back_others,
    rows_v, grads_v, gate_v, up_v, down_v, g_v, u_v, sems,
):
    half = rows.shape[0]
    low, high = pl.ds(0, half), pl.ds(half, half)
    pairs = [
        (rows, rows_v.at[low]),
        (weights.at[:, pl.ds(0, FFS)], gate_v),
        (others, rows_v.at[high]),
        (weights.at[:, pl.ds(FFS, FFS)], up_v),
        (grads, grads_v.at[low]),
        (grads_others, grads_v.at[high]),
        (weights.at[:, pl.ds(2 * FFS, FFS)], down_v),
    ]
    loads = [
        pltpu.make_async_copy(src, dst, sems.at[i]) for i, (src, dst) in enumerate(pairs)
    ]
    for one in loads:
        one.start()
    tile = 256
    steps = half // tile
    for one in loads[:3]:
        one.wait()

    @pl.loop(0, 2 * steps)
    def _(i):
        at = pl.ds(pl.multiple_of(i * tile, tile), tile)
        g_v[at, :] = product(rows_v[at, :], gate_v[...])

    loads[3].wait()

    @pl.loop(0, 2 * steps)
    def _(i):
        at = pl.ds(pl.multiple_of(i * tile, tile), tile)
        u_v[at, :] = product(rows_v[at, :], up_v[...])

    for one in loads[4:]:
        one.wait()

    for base, out in ((half, back_others), (0, back)):

        @pl.loop(0, steps)
        def _(i):
            at = pl.ds(pl.multiple_of(base + i * tile, tile), tile)
            grad_mixed = product(grads_v[at, :], down_v[...])
            gate_val = g_v[at, :]
            up_val = u_v[at, :]
            gate_sig = jax.nn.sigmoid(gate_val)
            swish = gate_val * gate_sig
            mixed[at, :] = (swish * up_val).astype(BF)
            grad_up = (grad_mixed * swish).astype(BF)
            grad_gate = (
                grad_mixed * up_val * gate_sig * (1.0 + gate_val * (1.0 - gate_sig))
            ).astype(BF)
            inner[at, :FFS] = grad_gate
            inner[at, FFS:] = grad_up
            to = pl.ds(pl.multiple_of(i * tile, tile), tile)
            out[to, :] = (
                against(grad_gate, gate_v[...]) + against(grad_up, up_v[...])
            ).astype(BF)


def ffn(rows, others, grads, grads_others, weights):
    half = rows.shape[0]
    count = 2 * half
    dims = [(count, FFS), (count, 2 * FFS), (half, D), (half, D)]
    outs = [jax.ShapeDtypeStruct(d, BF) for d in dims]
    scratch = [pltpu.VMEM((count, D), BF)] * 2 + [pltpu.VMEM((D, FFS), BF)] * 3
    scratch += [pltpu.VMEM((count, FFS), F32)] * 2 + [pltpu.SemaphoreType.DMA((7,))]
    return call(
        ffn_body, outs, [ANY] * 5, [VMEM] * 4, scratch,
        flops=10 * count * D * FFS, moved=28 * MIB, vmem=56 * MIB,
    )(rows, others, grads, grads_others, weights)


def per_device(
    tokens,
    cotangent,
    attn_gain,
    q_weight,
    q_bias,
    k_weight,
    k_bias,
    v_weight,
    v_bias,
    o_weight,
    mlp_gain,
    gate_weight,
    up_weight,
    down_weight,
):
    yh, x, z, yl, core = [lax.axis_index(a) for a in AXES]
    y = yh * 2 + yl
    ctx_rank = yh * 4 + x
    own = 2 * BLK
    both = 2 * own
    score_scale = 1.0 / math.sqrt(HD)
    is_zero = core == 0

    place = jnp.arange(D, dtype=jnp.int32)
    place_r = place % ROWS
    place_x = place // ROWS % 4
    place_c = place // (ROWS * 4) % 2
    place_y = place // (ROWS * 8) % 4
    place_z = place // (ROWS * 32)
    place_dev = (((place_y // 2 * 4 + place_x) * 4 + place_z) * 2 + place_y % 2) * 2 + place_c
    natural = place_dev * ROWS + place_r
    to_order = (place[:, None] == natural[None, :]).astype(BF)

    tokens_flat = tokens.reshape(own, D)
    tokens_both = jnp.concatenate([tokens_flat, swap_core(tokens_flat)], 0)

    vectors = jnp.concatenate([attn_gain, mlp_gain, q_bias, k_bias, v_bias])
    got = exchange(pack_attn(vectors[None], q_weight, k_weight, v_weight, o_weight), TP)
    got_ff = after(pack_ff(gate_weight, up_weight, down_weight), got)
    got_ff = exchange(got_ff, TP)
    grad_low = product(cotangent.reshape(own, D), to_order).astype(BF)
    want = jnp.arange(8 * ROWS, dtype=jnp.int32)
    at = (want // ROWS % 4 * 2 + want // (4 * ROWS)) * PAD + want % ROWS
    pick = (at[:, None] == jnp.arange(8 * PAD, dtype=jnp.int32)[None, :]).astype(BF)
    rows_attn = product(pick, got).astype(BF)
    rows_ff = product(pick, got_ff).astype(BF)

    plane = ("z",) + Y
    grad_rows = neighbours(after(grad_low, rows_attn))
    attn_all = lax.all_gather(rows_attn, plane, axis=0, tiled=True)
    ff_all = lax.all_gather(rows_ff, plane, axis=0, tiled=True)
    attn_all = after(attn_all, *grad_rows)
    weight_qkv = attn_all[:, :QKV]
    weight_o = attn_all[:, QKVM:]

    eight = (jnp.arange(8)[:, None] == jnp.arange(MISC)[None, :]).astype(BF)
    misc_rows = against(eight, attn_all[:, QKV:QKVM])
    gain_one = misc_rows[0:1]
    gain_two = misc_rows[1:2]
    bias_rows = misc_rows.astype(BF)
    bias_q = against(bias_rows[2:3], to_order)
    small = jnp.arange(KVH * HD, dtype=jnp.int32)
    to_small = (
        ((place_dev * 2 + place_r)[:, None] == small[None, :]) & (place_r < 2)[:, None]
    ).astype(BF)
    bias_kv = product(bias_rows[3:5], to_small)

    def side_of(row, width):
        return jnp.where(is_zero, row[:, :width], row[:, width:])

    bias_qkv = jnp.concatenate(
        [
            side_of(bias_q, HALF_Q),
            side_of(bias_kv[0:1], HD),
            side_of(bias_kv[1:2], HD),
        ],
        1,
    )

    offsets = jnp.arange(BLK, dtype=jnp.int32)
    query_pos = jnp.concatenate(
        [ctx_rank * BLK + offsets, (2 * N_CTX - 1 - ctx_rank) * BLK + offsets]
    )
    sources = jnp.arange(N_CTX, dtype=jnp.int32)
    sources = ((sources % 2) ^ yh) * 4 + ((sources // 2) ^ x)
    key_pos = jnp.stack(
        [
            sources[:, None] * BLK + offsets[None, :],
            (2 * N_CTX - 1 - sources)[:, None] * BLK + offsets[None, :],
        ],
        1,
    ).reshape(-1)
    visible = query_pos[:, None] >= key_pos[None, :]
    cosine_tab, sine_tab = rope_tables(query_pos)
    cosine_b = jnp.concatenate([cosine_tab, cosine_tab], 0)[:, None, :]
    sine_b = jnp.concatenate([sine_tab, sine_tab], 0)[:, None, :]

    inputs = product(tokens_both, to_order)
    scale_one = lax.rsqrt(jnp.mean(inputs * inputs, axis=-1, keepdims=True) + epsilon)
    unit_one = inputs * scale_one
    normed_one = (unit_one * gain_one).astype(BF)
    lin = product(normed_one, weight_qkv) + bias_qkv
    turned = rotate(
        lin[:, : HALF_Q + HD].reshape(both, GROUP + 1, HD), cosine_b, sine_b
    ).astype(BF)
    query_rot = turned[:, :GROUP].reshape(2, own, GROUP, HD)
    kv_send = jnp.concatenate([turned[:, GROUP], lin[:, HALF_Q + HD :].astype(BF)], 1)
    kv_all = jnp.concatenate([kv_send, swap_yh(kv_send)], 0)
    kv_all = jnp.concatenate([kv_all] + [to_x(kv_all, k) for k in range(1, 4)], 0)
    kv_all = kv_all.reshape(N_CTX, 2, own, 2 * HD).transpose(1, 0, 2, 3)
    kv_all = kv_all.reshape(2, N_CTX * own, 2 * HD)
    key_heads = kv_all[..., :HD]
    value_heads = kv_all[..., HD:]
    ones = jnp.broadcast_to(
        (jnp.arange(PAD) == 0).astype(BF)[None, :], (both, PAD)
    )
    normed_ext = jnp.concatenate(
        [
            piece
            for i in range(4)
            for piece in (normed_one[:, i * D // 4 : (i + 1) * D // 4], ones)
        ],
        1,
    )
    query_rot = after(query_rot, normed_ext)
    scores = (
        jnp.einsum("slrd,smd->srlm", query_rot, key_heads, preferred_element_type=F32)
        * score_scale
    )
    masked = jnp.where(visible, scores, -jnp.inf)
    row_max = jnp.max(masked, axis=-1, keepdims=True)
    exp_terms = jnp.exp(masked - row_max)
    row_sum = jnp.sum(exp_terms, axis=-1, keepdims=True)
    probs = exp_terms / row_sum
    probs_low = probs.astype(BF)
    context = jnp.einsum("srlm,smd->slrd", probs_low, value_heads, preferred_element_type=F32)
    context_low = context.reshape(both, HALF_Q).astype(BF)
    branch = against(context_low, weight_o)
    hidden_one = (
        inputs[:own] + branch[:own] + swap_core(branch[own:].astype(BF)).astype(F32)
    )
    scale_two = lax.rsqrt(jnp.mean(hidden_one * hidden_one, axis=-1, keepdims=True) + epsilon)
    unit_two = hidden_one * scale_two
    normed_two = (unit_two * gain_two).astype(BF)

    normed_rows = neighbours(normed_two)
    mixed_low, grad_inner, *grad_norm_part = ffn(
        *normed_rows, *grad_rows, ff_all
    )
    grad_norm_mine = add_low(grad_norm_part[0], swap_core(grad_norm_part[1]))
    grad_norm_two = neighbours_sum(grad_norm_mine)
    normed_late, grad_late = [
        after(jnp.concatenate(pair, 0), grad_norm_mine) for pair in (normed_rows, grad_rows)
    ]
    ff_grads = [
        row_major(over_rows(normed_late, grad_inner).astype(BF)),
        row_major(over_rows(grad_late, mixed_low).astype(BF)),
    ]
    grad_norm_two = after(grad_norm_two, *ff_grads)

    grad_unit_two = grad_norm_two * gain_two
    grad_hidden = grad_low.astype(F32) + scale_two * (
        grad_unit_two - unit_two * jnp.mean(grad_unit_two * unit_two, axis=-1, keepdims=True)
    )
    grad_branch = grad_hidden.astype(BF)
    grad_branch = jnp.concatenate([grad_branch, swap_core(grad_branch)], 0)
    o_grads = row_major(over_rows(grad_branch, context_low).astype(BF))
    late_grads = jnp.concatenate(ff_grads + [o_grads], 1)
    late_sum = lax.psum_scatter(late_grads, plane, scatter_dimension=0, tiled=True)
    grad_context = product(grad_branch, weight_o).astype(BF)
    grad_context = after(grad_context, late_grads)
    grad_heads = grad_context.reshape(2, own, GROUP, HD)
    grad_probs = jnp.einsum(
        "slrd,smd->srlm", grad_heads, value_heads, preferred_element_type=F32
    )
    row_delta = jnp.sum(probs * grad_probs, axis=-1, keepdims=True)
    grad_scores = (probs * (grad_probs - row_delta)).astype(BF)
    grad_query = (
        jnp.einsum("srlm,smd->slrd", grad_scores, key_heads, preferred_element_type=F32)
        * score_scale
    )
    grad_key = (
        jnp.einsum("srlm,slrd->smd", grad_scores, query_rot, preferred_element_type=F32)
        * score_scale
    )
    grad_value = jnp.einsum(
        "srlm,slrd->smd", probs_low, grad_heads, preferred_element_type=F32
    )
    grad_kv = jnp.concatenate([grad_key, grad_value], 2).astype(BF)
    weight_down = ff_all[:, 2 * FFS :]
    down_part = against(after(mixed_low, grad_kv), weight_down).astype(BF)
    down_part = add_low(down_part[: 4 * own], swap_core(down_part[4 * own :]))
    down_terms = neighbours_sum(down_part)
    layer_sum = (hidden_one + down_terms).astype(BF)
    layer_out = against(layer_sum, to_order).astype(BF).reshape(tokens.shape)
    grad_kv = grad_kv.reshape(2, N_CTX, own, 2 * HD).transpose(1, 0, 2, 3)
    grad_kv = grad_kv.reshape(4, 2 * both, 2 * HD)
    over_x = grad_kv[0].astype(F32)
    for k in range(1, 4):
        over_x = over_x + to_x(grad_kv[k], k).astype(F32)
    grad_kv = over_x[:both] + swap_yh(over_x[both:].astype(BF)).astype(F32)
    grad_turned = jnp.concatenate([grad_query.reshape(both, HALF_Q), grad_kv[:, :HD]], 1)
    grad_turned = unrotate(grad_turned.reshape(both, GROUP + 1, HD), cosine_b, sine_b)
    grad_lin = jnp.concatenate(
        [grad_turned.reshape(both, HALF_Q + HD).astype(BF), grad_kv[:, HD:].astype(BF)], 1
    )
    grad_norm_one = against(grad_lin, weight_qkv)
    grad_norm_one = grad_norm_one[:own] + swap_core(grad_norm_one[own:].astype(BF)).astype(F32)
    unit_own = unit_one[:own]
    grad_unit_one = grad_norm_one * gain_one
    input_grad = grad_hidden + scale_one[:own] * (
        grad_unit_one - unit_own * jnp.mean(grad_unit_one * unit_own, axis=-1, keepdims=True)
    )
    input_high = input_grad.astype(BF)
    input_rest = (input_grad - input_high.astype(F32)).astype(BF)
    input_grad = (against(input_high, to_order) + against(input_rest, to_order)).reshape(
        tokens.shape
    )

    qkv_grads = row_major(over_rows(normed_ext, grad_lin).astype(BF))
    qkv_half = collect(qkv_grads, "z", 4)
    quarter = D // 16
    qkv_half = jnp.concatenate(
        [
            piece
            for i in range(4)
            for piece in (qkv_half[i * quarter : (i + 1) * quarter], qkv_half[D // 4 :])
        ],
        0,
    )
    qkv_sum = collect(qkv_half, Y, 4)
    slot = jnp.arange(8 * PAD, dtype=jnp.int32)
    extra = jnp.arange(PAD, dtype=jnp.int32)
    pick_ext = jnp.concatenate(
        [pick, ((extra[:, None] == 0) & (slot[None, :] % PAD == ROWS)).astype(BF)], 0
    )
    spaced = jnp.concatenate(
        [over_rows(pick_ext, qkv_sum).astype(BF), over_rows(pick, late_sum).astype(BF)], 1
    )
    (
        q_weight_grad,
        k_weight_grad,
        v_weight_grad,
        o_weight_grad,
        gate_weight_grad,
        up_weight_grad,
        down_weight_grad,
        bias_sum,
        gain_sum,
    ) = unpack_grads(
        exchange(spaced, TP), q_weight, k_weight, v_weight, gate_weight, up_weight
    )
    attn_gain_grad = gain_sum[:, 0] / attn_gain.astype(F32)
    mlp_gain_grad = gain_sum[:, 1] / mlp_gain.astype(F32)
    device = ctx_rank * 16 + z * 4 + yl * 2 + core
    q_bias_grad = lax.dynamic_slice_in_dim(
        bias_sum[:, :HALF_Q].reshape(D), device * ROWS, ROWS, 0
    )
    k_bias_grad = bias_sum[:, HALF_Q : HALF_Q + HD].reshape(KVH * HD)
    v_bias_grad = lax.dynamic_slice_in_dim(
        bias_sum[:, HALF_Q + HD :].reshape(KVH * HD), device * 2, 2, 0
    )
    return (
        layer_out,
        input_grad,
        attn_gain_grad,
        q_weight_grad,
        q_bias_grad,
        k_weight_grad,
        k_bias_grad,
        v_weight_grad,
        v_bias_grad,
        o_weight_grad,
        mlp_gain_grad,
        gate_weight_grad,
        up_weight_grad,
        down_weight_grad,
    )


def solution(mesh):
    fine = Mesh(mesh.devices.reshape(2, 4, 4, 2, 2), AXES)
    acts = P(("z", "yl", "core"), None, CTX, None)
    vec, mat = P(AXES), P(AXES, None)
    return jax.shard_map(
        per_device,
        mesh=fine,
        in_specs=(acts, acts, vec, mat, vec, mat, vec, mat, vec, mat, vec, mat, mat, mat),
        out_specs=(acts, acts, vec, mat, vec, mat, P(), mat, vec, mat, vec, mat, mat, mat),
        check_vma=False,
    )
```

```python
import math

import jax
import jax.numpy as jnp
from jax import lax
from jax.experimental import pallas as pl
from jax.experimental.layout import Layout, with_layout_constraint
from jax.experimental.pallas import tpu as pltpu
from jax.sharding import Mesh, PartitionSpec as P

H = 12
KVH = 2
HD = 128
GROUP = H // KVH
D = 1536
FF = 8960
BLK = 64
N_CTX = 8
ROWS = 12
PAD = 16
FFS = 1152
HALF_Q = GROUP * HD
QKV = HALF_Q + 2 * HD
MISC = 128
QKVM = QKV + MISC
FFW = 3 * FFS
XCOLS = D // 4 + PAD
SIDE = QKVM + HALF_Q

epsilon = 1e-06
rope_base = 1000000.0

AXES = ("yh", "x", "z", "yl", "core")
Y = ("yh", "yl")
CTX = ("yh", "x")
TP = ("x", "core")
F32 = jnp.float32
BF = jnp.bfloat16


def add_low(left, right):
    return (left.astype(F32) + right.astype(F32)).astype(BF)


def swap_core(arr):
    return lax.ppermute(arr, "core", [(0, 1), (1, 0)])


def swap_yh(arr):
    return lax.ppermute(arr, "yh", [(0, 1), (1, 0)])


def to_x(arr, k):
    return lax.ppermute(arr, "x", [(i, i ^ k) for i in range(4)])


def after(arr, *earlier):
    return lax.optimization_barrier((arr,) + earlier)[0]


def row_major(arr):
    return with_layout_constraint(arr, Layout(major_to_minor=(0, 1)))


def exchange(arr, axis):
    return lax.all_to_all(arr, axis, split_axis=0, concat_axis=0, tiled=True)


def spread(block, axis, count):
    return exchange(jnp.tile(block, (count, 1)), axis)


def neighbours(block):
    mine = jnp.concatenate([block] + [to_x(block, k) for k in range(1, 4)], 0)
    return mine, swap_core(mine)


def neighbours_sum(mine):
    rows = mine.shape[0] // 4
    total = mine[:rows].astype(F32)
    for k in range(1, 4):
        total = total + to_x(mine[k * rows : (k + 1) * rows], k).astype(F32)
    return total


def collect(whole, axis, count):
    got = exchange(whole, axis).reshape(count, whole.shape[0] // count, whole.shape[1])
    return jnp.sum(got.astype(F32), axis=0).astype(BF)


def rope_tables(positions):
    half_dim = HD // 2
    frequency = jnp.exp(
        jnp.arange(half_dim, dtype=F32) * (-2.0 * math.log(rope_base) / HD)
    )
    angles = positions.astype(F32)[:, None] * frequency[None, :]
    cosine_tab = jnp.cos(angles)
    sine_tab = jnp.sin(angles)
    return (
        jnp.concatenate([cosine_tab, cosine_tab], -1),
        jnp.concatenate([sine_tab, sine_tab], -1),
    )


def rotate(values, cosine_tab, sine_tab):
    half_dim = values.shape[-1] // 2
    turned = jnp.concatenate([-values[..., half_dim:], values[..., :half_dim]], -1)
    return values * cosine_tab + turned * sine_tab


def unrotate(grads_in, cosine_tab, sine_tab):
    half_dim = grads_in.shape[-1] // 2
    scaled = grads_in * sine_tab
    return grads_in * cosine_tab + jnp.concatenate(
        [scaled[..., half_dim:], -scaled[..., :half_dim]], -1
    )


def product(left_arr, right_arr):
    return jnp.dot(left_arr, right_arr, preferred_element_type=F32)


def against(left_arr, right_arr):
    return lax.dot_general(
        left_arr, right_arr, (((1,), (1,)), ((), ())), preferred_element_type=F32
    )


def over_rows(left_arr, right_arr):
    return lax.dot_general(
        left_arr, right_arr, (((0,), (0,)), ((), ())), preferred_element_type=F32
    )


VMEM = pl.BlockSpec(memory_space=pltpu.VMEM)
ANY = pl.BlockSpec(memory_space=pl.ANY)
MIB = 1 << 20


def call(body, outs, ins, out_specs, scratch=(), flops=0, moved=0, vmem=48 * MIB):
    return pl.pallas_call(
        body,
        out_shape=outs,
        in_specs=ins,
        out_specs=out_specs,
        scratch_shapes=scratch,
        compiler_params=pltpu.CompilerParams(vmem_limit_bytes=vmem),
        cost_estimate=pl.CostEstimate(flops=flops, bytes_accessed=moved, transcendentals=0),
    )


def fetch(sources, targets, sems):
    copies = [
        pltpu.make_async_copy(src, dst, sems.at[i])
        for i, (src, dst) in enumerate(zip(sources, targets))
    ]
    for one in copies:
        one.start()
    for one in copies:
        one.wait()


def hold(arr, *earlier):
    def body(*refs):
        refs[-1][...] = refs[0][...]

    out = jax.ShapeDtypeStruct(arr.shape, arr.dtype)
    size = 2 * arr.size * arr.dtype.itemsize
    return call(body, out, [VMEM] + [ANY] * len(earlier), VMEM, moved=size)(arr, *earlier)


def pack_attn_body(vectors, q, k, v, o, out, q_v, k_v, v_v, o_v, square, sems):
    square[...] = jnp.zeros_like(square)
    start = 0
    for i, width in enumerate((ROWS, ROWS, ROWS, 2, 2)):
        square[i : i + 1, :width] = vectors[:, start : start + width].astype(F32)
        start += width
    misc = square[...].T[:PAD].astype(BF)
    fetch((q, k, v, o), (q_v, k_v, v_v, o_v), sems)
    for t in range(8):
        h = t % 2
        rows = slice(t * PAD, t * PAD + ROWS)
        out[t * PAD : (t + 1) * PAD, :] = jnp.zeros((PAD, SIDE), BF)
        out[rows, :HALF_Q] = q_v[:, h * HALF_Q : (h + 1) * HALF_Q]
        out[rows, HALF_Q : HALF_Q + HD] = k_v[:, h * HD : (h + 1) * HD]
        out[rows, HALF_Q + HD : QKV] = v_v[:, h * HD : (h + 1) * HD]
        out[t * PAD : (t + 1) * PAD, QKV:QKVM] = misc
        out[rows, QKVM:SIDE] = o_v[:, h * HALF_Q : (h + 1) * HALF_Q]


def pack_attn(vectors, *arrays):
    out = jax.ShapeDtypeStruct((8 * PAD, SIDE), BF)
    scratch = [pltpu.VMEM(a.shape, BF) for a in arrays]
    scratch += [pltpu.VMEM((MISC, MISC), F32), pltpu.SemaphoreType.DMA((4,))]
    return call(pack_attn_body, out, [VMEM] + [ANY] * 4, VMEM, scratch, moved=MIB)(
        vectors, *arrays
    )


def pack_ff_body(gate, up, down, out, gate_v, up_v, down_v, sems):
    fetch((gate, up, down), (gate_v, up_v, down_v), sems)
    for t in range(8):
        out[t * PAD : (t + 1) * PAD, :] = jnp.zeros((PAD, FFW), BF)
        width = min(FFS, FF - t * FFS)
        for i, ref in enumerate((gate_v, up_v, down_v)):
            out[t * PAD : t * PAD + ROWS, i * FFS : i * FFS + width] = ref[
                :, t * FFS : t * FFS + width
            ]


def pack_ff(*arrays):
    out = jax.ShapeDtypeStruct((8 * PAD, FFW), BF)
    scratch = [pltpu.VMEM(a.shape, BF) for a in arrays] + [pltpu.SemaphoreType.DMA((3,))]
    return call(pack_ff_body, out, [ANY] * 3, VMEM, scratch, moved=2 * MIB)(*arrays)


def unpack_body(
    index, attn, late, q_w, k_w, v_w, gate_w, up_w,
    q, k, v, o, gate, up, down, biases, gains,
):
    x, core = index[0], index[1]

    def block(i, h, start, width):
        row = pl.multiple_of((core ^ h) * PAD, PAD)
        return late[x ^ i, pl.ds(row, PAD), start : start + width].astype(F32)[:ROWS]

    def gain_part(weight, start, grad):
        width = grad.shape[1]
        part = weight[:, start : start + width].astype(F32) * grad
        return jnp.sum(part, axis=1, keepdims=True)

    attn_gain = jnp.zeros((ROWS, 1), F32)
    for h in range(2):
        part = attn[core ^ h].astype(F32)
        biases[h : h + 1, :] = part[ROWS : ROWS + 1]
        for ref, weight, start, width in (
            (q, q_w, 0, HALF_Q),
            (k, k_w, HALF_Q, HD),
            (v, v_w, HALF_Q + HD, HD),
        ):
            piece = part[:ROWS, start : start + width]
            ref[:, h * width : (h + 1) * width] = piece
            attn_gain = attn_gain + gain_part(weight, h * width, piece)
        o[:, h * HALF_Q : (h + 1) * HALF_Q] = sum(block(i, h, FFW, HALF_Q) for i in range(4))
    mlp_gain = jnp.zeros((ROWS, 1), F32)
    for t in range(8):
        width = min(FFS, FF - t * FFS)
        for i, (ref, weight) in enumerate(((gate, gate_w), (up, up_w), (down, None))):
            piece = block(t // 2, t % 2, i * FFS, width)
            ref[:, t * FFS : t * FFS + width] = piece
            if weight is not None:
                mlp_gain = mlp_gain + gain_part(weight, t * FFS, piece)
    gains[:, 0:1] = attn_gain
    gains[:, 1:2] = mlp_gain


def unpack_grads(index, *arrays):
    shapes = [(ROWS, D), (ROWS, KVH * HD), (ROWS, KVH * HD), (ROWS, D)]
    shapes += [(ROWS, FF)] * 3 + [(2, QKV), (ROWS, 2)]
    outs = [jax.ShapeDtypeStruct(dims, F32) for dims in shapes]
    ins = [pl.BlockSpec(memory_space=pltpu.SMEM)] + [VMEM] * 7
    return call(unpack_body, outs, ins, [VMEM] * 9, moved=5 * MIB)(index, *arrays)


def turn(values, cosine, sine, back):
    low = lax.broadcasted_iota(jnp.int32, values.shape, 1) < HD // 2
    if back:
        moved = pltpu.roll(values * sine, HD // 2, 1)
        return values * cosine + jnp.where(low, moved, -moved)
    moved = pltpu.roll(values, HD // 2, 1)
    return values * cosine + jnp.where(low, -moved, moved) * sine


def project_body(normed, weights, bias, cosine, sine, query, kv, w_v, sems):
    fetch((weights.at[:, pl.ds(0, QKV)],), (w_v,), sems)
    lin = product(normed[...], w_v[...]) + bias[...]
    for s in range(2):
        rows = slice(s * 2 * BLK, (s + 1) * 2 * BLK)
        for r in range(GROUP + 1):
            head = turn(lin[rows, r * HD : (r + 1) * HD], cosine[...], sine[...], False)
            if r < GROUP:
                query[rows, r * HD : (r + 1) * HD] = head.astype(BF)
            else:
                kv[rows, :HD] = head.astype(BF)
    kv[:, HD:] = lin[:, HALF_Q + HD :].astype(BF)


def project(normed, weights, bias, cosine, sine):
    count = normed.shape[0]
    outs = [jax.ShapeDtypeStruct((count, w), BF) for w in (HALF_Q, 2 * HD)]
    scratch = [pltpu.VMEM((D, QKV), BF), pltpu.SemaphoreType.DMA((1,))]
    return call(
        project_body, outs, [VMEM, ANY] + [VMEM] * 3, [VMEM] * 2, scratch,
        flops=2 * count * D * QKV, moved=5 * MIB,
    )(normed, weights, bias, cosine, sine)


def stacked(parts, s, start):
    own = 2 * BLK
    return jnp.concatenate(
        [
            part[(2 * h + s) * own : (2 * h + s + 1) * own, start : start + HD]
            for part in parts
            for h in range(2)
        ],
        0,
    )


def positions_of(block, iota):
    return jnp.where(iota < BLK, block * BLK, (2 * N_CTX - 2 - block) * BLK) + iota


def attend_body(index, query, kv0, kv1, kv2, kv3, context, probs, mask, p_v, sems):
    own = 2 * BLK
    yh, x = index[0], index[1]
    here = positions_of(yh * 4 + x, lax.broadcasted_iota(jnp.int32, (own, own), 1))
    for j in range(N_CTX):
        source = ((j % 2) ^ yh) * 4 + ((j // 2) ^ x)
        there = positions_of(source, lax.broadcasted_iota(jnp.int32, (own, own), 0))
        mask[j * own : (j + 1) * own, :] = jnp.where(here >= there, 0.0, -1e30)
    parts = (kv0, kv1, kv2, kv3)
    copies = []
    for s in range(2):
        keys = stacked(parts, s, 0)
        values = stacked(parts, s, HD).T
        rows = slice(s * own, (s + 1) * own)
        for r in range(GROUP):
            head = s * GROUP + r
            scores = against(keys, query[rows, r * HD : (r + 1) * HD])
            scores = scores * (1.0 / math.sqrt(HD)) + mask[...]
            terms = jnp.exp(scores - jnp.max(scores, axis=0, keepdims=True))
            p = terms / jnp.sum(terms, axis=0, keepdims=True)
            p_v[head] = p
            copies.append(pltpu.make_async_copy(p_v.at[head], probs.at[head], sems.at[head]))
            copies[-1].start()
            context[rows, r * HD : (r + 1) * HD] = product(values, p.astype(BF)).T.astype(BF)
    for one in copies:
        one.wait()


def attend(index, query, parts):
    heads, keys, own = 2 * GROUP, 2 * N_CTX * BLK, 2 * BLK
    outs = [
        jax.ShapeDtypeStruct(query.shape, BF),
        jax.ShapeDtypeStruct((heads, keys, own), F32),
    ]
    scratch = [
        pltpu.VMEM((keys, own), F32),
        pltpu.VMEM((heads, keys, own), F32),
        pltpu.SemaphoreType.DMA((heads,)),
    ]
    return call(
        attend_body, outs, [pl.BlockSpec(memory_space=pltpu.SMEM)] + [VMEM] * 5, [VMEM, ANY],
        scratch, flops=4 * heads * keys * own * HD, moved=8 * MIB,
    )(index, query, *parts)


def attend_back_body(
    branch, weights, query, kv0, kv1, kv2, kv3, probs, cosine, sine,
    grad_query, out0, out1, out2, out3, w_v, p_v, sems,
):
    own, heads = 2 * BLK, 2 * GROUP
    scale = 1.0 / math.sqrt(HD)
    weight = pltpu.make_async_copy(weights.at[:, pl.ds(QKVM, HALF_Q)], w_v, sems.at[heads])
    weight.start()
    loads = [
        pltpu.make_async_copy(probs.at[i], p_v.at[i], sems.at[i]) for i in range(heads)
    ]
    for one in loads:
        one.start()
    weight.wait()
    grad_context = product(branch[...], w_v[...]).astype(BF)
    parts, outs = (kv0, kv1, kv2, kv3), (out0, out1, out2, out3)
    for s in range(2):
        keys = stacked(parts, s, 0).T
        values = stacked(parts, s, HD)
        rows = slice(s * own, (s + 1) * own)
        grad_key = jnp.zeros((2 * N_CTX * BLK, HD), F32)
        grad_value = jnp.zeros((2 * N_CTX * BLK, HD), F32)
        for r in range(GROUP):
            columns = slice(r * HD, (r + 1) * HD)
            loads[s * GROUP + r].wait()
            p = p_v[s * GROUP + r]
            grad = grad_context[rows, columns]
            grad_p = against(values, grad)
            delta = jnp.sum(p * grad_p, axis=0, keepdims=True)
            grad_s = (p * (grad_p - delta)).astype(BF)
            back = product(keys, grad_s).T * scale
            grad_query[rows, columns] = turn(back, cosine[...], sine[...], True).astype(BF)
            grad_key = grad_key + product(grad_s, query[rows, columns])
            grad_value = grad_value + product(p.astype(BF), grad)
        for k, out in enumerate(outs):
            for h in range(2):
                to = slice((2 * h + s) * own, (2 * h + s + 1) * own)
                at = slice((2 * k + h) * own, (2 * k + h + 1) * own)
                out[to, :HD] = (grad_key[at] * scale).astype(BF)
                out[to, HD:] = grad_value[at].astype(BF)


def attend_back(branch, weights, query, parts, probs, cosine, sine):
    heads, keys, own = probs.shape
    outs = [jax.ShapeDtypeStruct(query.shape, BF)]
    outs += [jax.ShapeDtypeStruct(p.shape, BF) for p in parts]
    scratch = [
        pltpu.VMEM((D, HALF_Q), BF),
        pltpu.VMEM(probs.shape, F32),
        pltpu.SemaphoreType.DMA((heads + 1,)),
    ]
    return call(
        attend_back_body, outs, [VMEM, ANY] + [VMEM] * 5 + [ANY] + [VMEM] * 2, [VMEM] * 5,
        scratch, flops=10 * heads * keys * own * HD, moved=12 * MIB,
    )(branch, weights, query, *parts, probs, cosine, sine)


def down_body(mixed, weights, *refs):
    mine, others, w_v, sems = refs[-4:]
    fetch((weights.at[:, pl.ds(2 * FFS, FFS)],), (w_v,), sems)
    tile = 256
    half = mine.shape[0]
    for base, out in ((half, others), (0, mine)):

        @pl.loop(0, half // tile)
        def _(i):
            at = pl.ds(pl.multiple_of(base + i * tile, tile), tile)
            to = pl.ds(pl.multiple_of(i * tile, tile), tile)
            out[to, :] = against(mixed[at, :], w_v[...]).astype(BF)


def down(mixed, weights, *earlier):
    half = mixed.shape[0] // 2
    outs = [jax.ShapeDtypeStruct((half, D), BF)] * 2
    scratch = [pltpu.VMEM((D, FFS), BF), pltpu.SemaphoreType.DMA((1,))]
    return call(
        down_body, outs, [VMEM, ANY] + [ANY] * len(earlier), [VMEM] * 2, scratch,
        flops=4 * half * D * FFS, moved=9 * MIB,
    )(mixed, weights, *earlier)


def ffn_body(
    rows, others, grads, grads_others, weights, mixed, inner, back, back_others,
    rows_v, grads_v, gate_v, up_v, down_v, g_v, u_v, sems,
):
    half = rows.shape[0]
    low, high = pl.ds(0, half), pl.ds(half, half)
    pairs = [
        (rows, rows_v.at[low]),
        (weights.at[:, pl.ds(0, FFS)], gate_v),
        (others, rows_v.at[high]),
        (weights.at[:, pl.ds(FFS, FFS)], up_v),
        (grads, grads_v.at[low]),
        (grads_others, grads_v.at[high]),
        (weights.at[:, pl.ds(2 * FFS, FFS)], down_v),
    ]
    loads = [
        pltpu.make_async_copy(src, dst, sems.at[i]) for i, (src, dst) in enumerate(pairs)
    ]
    for one in loads:
        one.start()
    tile = 256
    steps = half // tile
    for one in loads[:3]:
        one.wait()

    @pl.loop(0, 2 * steps)
    def _(i):
        at = pl.ds(pl.multiple_of(i * tile, tile), tile)
        g_v[at, :] = product(rows_v[at, :], gate_v[...])

    loads[3].wait()

    @pl.loop(0, 2 * steps)
    def _(i):
        at = pl.ds(pl.multiple_of(i * tile, tile), tile)
        u_v[at, :] = product(rows_v[at, :], up_v[...])

    for one in loads[4:]:
        one.wait()

    for base, out in ((half, back_others), (0, back)):

        @pl.loop(0, steps)
        def _(i):
            at = pl.ds(pl.multiple_of(base + i * tile, tile), tile)
            grad_mixed = product(grads_v[at, :], down_v[...])
            gate_val = g_v[at, :]
            up_val = u_v[at, :]
            gate_sig = jax.nn.sigmoid(gate_val)
            swish = gate_val * gate_sig
            mixed[at, :] = (swish * up_val).astype(BF)
            grad_up = (grad_mixed * swish).astype(BF)
            grad_gate = (
                grad_mixed * up_val * gate_sig * (1.0 + gate_val * (1.0 - gate_sig))
            ).astype(BF)
            inner[at, :FFS] = grad_gate
            inner[at, FFS:] = grad_up
            to = pl.ds(pl.multiple_of(i * tile, tile), tile)
            out[to, :] = (
                against(grad_gate, gate_v[...]) + against(grad_up, up_v[...])
            ).astype(BF)


def ffn(rows, others, grads, grads_others, weights):
    half = rows.shape[0]
    count = 2 * half
    dims = [(count, FFS), (count, 2 * FFS), (half, D), (half, D)]
    outs = [jax.ShapeDtypeStruct(d, BF) for d in dims]
    scratch = [pltpu.VMEM((count, D), BF)] * 2 + [pltpu.VMEM((D, FFS), BF)] * 3
    scratch += [pltpu.VMEM((count, FFS), F32)] * 2 + [pltpu.SemaphoreType.DMA((7,))]
    return call(
        ffn_body, outs, [ANY] * 5, [VMEM] * 4, scratch,
        flops=10 * count * D * FFS, moved=28 * MIB, vmem=56 * MIB,
    )(rows, others, grads, grads_others, weights)


def per_device(
    tokens,
    cotangent,
    attn_gain,
    q_weight,
    q_bias,
    k_weight,
    k_bias,
    v_weight,
    v_bias,
    o_weight,
    mlp_gain,
    gate_weight,
    up_weight,
    down_weight,
):
    yh, x, z, yl, core = [lax.axis_index(a) for a in AXES]
    y = yh * 2 + yl
    ctx_rank = yh * 4 + x
    own = 2 * BLK
    both = 2 * own
    is_zero = core == 0

    place = jnp.arange(D, dtype=jnp.int32)
    place_r = place % ROWS
    place_x = place // ROWS % 4
    place_c = place // (ROWS * 4) % 2
    place_y = place // (ROWS * 8) % 4
    place_z = place // (ROWS * 32)
    place_dev = (((place_y // 2 * 4 + place_x) * 4 + place_z) * 2 + place_y % 2) * 2 + place_c
    natural = place_dev * ROWS + place_r
    to_order = (place[:, None] == natural[None, :]).astype(BF)

    tokens_flat = tokens.reshape(own, D)
    tokens_both = jnp.concatenate([tokens_flat, swap_core(tokens_flat)], 0)

    vectors = jnp.concatenate([attn_gain, mlp_gain, q_bias, k_bias, v_bias])
    got = exchange(pack_attn(vectors[None], q_weight, k_weight, v_weight, o_weight), TP)
    got_ff = after(pack_ff(gate_weight, up_weight, down_weight), got)
    got_ff = exchange(got_ff, TP)
    grad_low = product(cotangent.reshape(own, D), to_order).astype(BF)
    want = jnp.arange(8 * ROWS, dtype=jnp.int32)
    at = (want // ROWS % 4 * 2 + want // (4 * ROWS)) * PAD + want % ROWS
    pick = (at[:, None] == jnp.arange(8 * PAD, dtype=jnp.int32)[None, :]).astype(BF)
    rows_attn = product(pick, got).astype(BF)
    rows_ff = product(pick, got_ff).astype(BF)

    plane = ("z",) + Y
    grad_rows = neighbours(after(grad_low, rows_attn))
    attn_all = lax.all_gather(rows_attn, plane, axis=0, tiled=True)
    ff_all = lax.all_gather(rows_ff, plane, axis=0, tiled=True)
    attn_all = after(attn_all, *grad_rows)
    weight_qkv = attn_all[:, :QKV]
    weight_o = attn_all[:, QKVM:]

    eight = (jnp.arange(8)[:, None] == jnp.arange(MISC)[None, :]).astype(BF)
    misc_rows = against(eight, attn_all[:, QKV:QKVM])
    gain_one = misc_rows[0:1]
    gain_two = misc_rows[1:2]
    bias_rows = misc_rows.astype(BF)
    bias_q = against(bias_rows[2:3], to_order)
    small = jnp.arange(KVH * HD, dtype=jnp.int32)
    to_small = (
        ((place_dev * 2 + place_r)[:, None] == small[None, :]) & (place_r < 2)[:, None]
    ).astype(BF)
    bias_kv = product(bias_rows[3:5], to_small)

    def side_of(row, width):
        return jnp.where(is_zero, row[:, :width], row[:, width:])

    bias_qkv = jnp.concatenate(
        [
            side_of(bias_q, HALF_Q),
            side_of(bias_kv[0:1], HD),
            side_of(bias_kv[1:2], HD),
        ],
        1,
    )

    offsets = jnp.arange(BLK, dtype=jnp.int32)
    query_pos = jnp.concatenate(
        [ctx_rank * BLK + offsets, (2 * N_CTX - 1 - ctx_rank) * BLK + offsets]
    )
    cosine_tab, sine_tab = rope_tables(query_pos)
    cosine_b = jnp.concatenate([cosine_tab, cosine_tab], 0)
    sine_b = jnp.concatenate([sine_tab, sine_tab], 0)

    inputs = product(tokens_both, to_order)
    scale_one = lax.rsqrt(jnp.mean(inputs * inputs, axis=-1, keepdims=True) + epsilon)
    unit_one = inputs * scale_one
    normed_one = (unit_one * gain_one).astype(BF)
    query_rot, kv_send = project(normed_one, attn_all, bias_qkv, cosine_tab, sine_tab)
    kv_parts = jnp.concatenate([kv_send, swap_yh(kv_send)], 0)
    kv_parts = [kv_parts] + [to_x(kv_parts, k) for k in range(1, 4)]
    slot = jnp.arange(4 * XCOLS, dtype=jnp.int32)
    slot_p = slot % XCOLS
    slot_zy = slot_p // (2 * ROWS)
    slot_dev = (slot_zy % 4 // 2 * 4 + slot // XCOLS) * 4 + slot_zy // 4
    slot_dev = (slot_dev * 2 + slot_zy % 2) * 2 + slot_p // ROWS % 2
    slot_at = jnp.where(slot_p < D // 4, slot_dev * ROWS + slot_p % ROWS, -1)
    by_x = (natural[:, None] == slot_at[None, :]).astype(BF)
    normed_x = jnp.where(
        (slot_p == D // 4)[None, :], 1.0, product(normed_one, by_x)
    ).astype(BF)
    query_rot = after(query_rot, normed_x)
    context_low, probs = attend(jnp.stack([yh, x]), query_rot, kv_parts)
    branch = against(context_low, weight_o)
    hidden_one = (
        inputs[:own] + branch[:own] + swap_core(branch[own:].astype(BF)).astype(F32)
    )
    scale_two = lax.rsqrt(jnp.mean(hidden_one * hidden_one, axis=-1, keepdims=True) + epsilon)
    unit_two = hidden_one * scale_two
    normed_two = (unit_two * gain_two).astype(BF)

    normed_rows = neighbours(normed_two)
    mixed_low, grad_inner, *grad_norm_part = ffn(
        *normed_rows, *grad_rows, ff_all
    )
    grad_norm_mine = add_low(grad_norm_part[0], swap_core(grad_norm_part[1]))
    grad_norm_two = neighbours_sum(grad_norm_mine)
    normed_late, grad_late = [
        after(jnp.concatenate(pair, 0), grad_norm_mine) for pair in (normed_rows, grad_rows)
    ]
    ff_grads = [
        row_major(over_rows(normed_late, grad_inner).astype(BF)),
        row_major(over_rows(grad_late, mixed_low).astype(BF)),
    ]
    grad_norm_two = after(grad_norm_two, *ff_grads)

    grad_unit_two = grad_norm_two * gain_two
    grad_hidden = grad_low.astype(F32) + scale_two * (
        grad_unit_two - unit_two * jnp.mean(grad_unit_two * unit_two, axis=-1, keepdims=True)
    )
    grad_branch = grad_hidden.astype(BF)
    grad_branch = jnp.concatenate([grad_branch, swap_core(grad_branch)], 0)
    o_grads = row_major(over_rows(grad_branch, context_low).astype(BF))
    late_grads = jnp.concatenate(ff_grads + [o_grads], 1)
    late_sum = lax.psum_scatter(late_grads, plane, scatter_dimension=0, tiled=True)
    branch_ready = hold(grad_branch, late_grads)
    grad_query, *kv_grads = attend_back(
        branch_ready, attn_all, query_rot, kv_parts, probs, cosine_tab, sine_tab
    )
    grad_kv = kv_grads[0].astype(F32)
    for k in range(1, 4):
        grad_kv = grad_kv + to_x(kv_grads[k], k).astype(F32)
    grad_kv = grad_kv[:both] + swap_yh(grad_kv[both:].astype(BF)).astype(F32)
    grad_key = unrotate(grad_kv[:, :HD], cosine_b, sine_b)
    grad_lin = jnp.concatenate(
        [grad_query, grad_key.astype(BF), grad_kv[:, HD:].astype(BF)], 1
    )
    qkv_grads = row_major(over_rows(normed_x, grad_lin).astype(BF))
    down_mine, down_others = down(mixed_low, ff_all, qkv_grads)
    down_terms = neighbours_sum(add_low(down_mine, swap_core(down_others)))
    layer_sum = (hidden_one + down_terms).astype(BF)
    layer_out = against(layer_sum, to_order).astype(BF).reshape(tokens.shape)
    grad_lin = hold(grad_lin, qkv_grads)
    grad_norm_one = against(grad_lin, weight_qkv)
    grad_norm_one = grad_norm_one[:own] + swap_core(grad_norm_one[own:].astype(BF)).astype(F32)
    unit_own = unit_one[:own]
    grad_unit_one = grad_norm_one * gain_one
    input_grad = grad_hidden + scale_one[:own] * (
        grad_unit_one - unit_own * jnp.mean(grad_unit_one * unit_own, axis=-1, keepdims=True)
    )
    input_high = input_grad.astype(BF)
    input_rest = (input_grad - input_high.astype(F32)).astype(BF)
    input_grad = (against(input_high, to_order) + against(input_rest, to_order)).reshape(
        tokens.shape
    )

    qkv_sum = collect(qkv_grads, "x", 4)
    spot = jnp.arange(16 * 2 * PAD, dtype=jnp.int32)
    spot_r = spot % PAD
    spot_at = spot // PAD * ROWS + spot_r
    spot_at = jnp.where(spot_r < ROWS, spot_at, jnp.where(spot_r == ROWS, D // 4, -1))
    room = (spot_at[:, None] == jnp.arange(XCOLS, dtype=jnp.int32)[None, :]).astype(BF)
    qkv_sum = exchange(product(room, qkv_sum).astype(BF), plane)
    qkv_sum = jnp.sum(qkv_sum.reshape(16, 2, PAD, QKV).astype(F32), axis=0).astype(BF)

    spot = jnp.arange(8 * PAD, dtype=jnp.int32)
    spot_at = ((spot // (4 * PAD)) ^ core) * 4 + ((spot // PAD % 4) ^ x)
    spot_at = jnp.where(spot % PAD < ROWS, spot_at * ROWS + spot % PAD, -1)
    late_pick = (want[:, None] == spot_at[None, :]).astype(BF)
    late = over_rows(late_pick, late_sum).astype(BF)
    late_pair = [late[: 4 * PAD], swap_core(late[4 * PAD :])]
    late_pair = [part.reshape(4, PAD, FFW + HALF_Q) for part in late_pair]
    late = jnp.concatenate(late_pair, 1)
    late = [late[0]] + [to_x(late[k], k) for k in range(1, 4)]
    qkv_keep = jnp.where(is_zero, qkv_sum[0], qkv_sum[1])
    qkv_give = hold(jnp.where(is_zero, qkv_sum[1], qkv_sum[0]), *late)
    qkv_sum = jnp.stack([qkv_keep, swap_core(qkv_give)])
    (
        q_weight_grad,
        k_weight_grad,
        v_weight_grad,
        o_weight_grad,
        gate_weight_grad,
        up_weight_grad,
        down_weight_grad,
        bias_sum,
        gain_sum,
    ) = unpack_grads(
        jnp.stack([x, core]), qkv_sum, jnp.stack(late),
        q_weight, k_weight, v_weight, gate_weight, up_weight,
    )
    attn_gain_grad = gain_sum[:, 0] / attn_gain.astype(F32)
    mlp_gain_grad = gain_sum[:, 1] / mlp_gain.astype(F32)
    device = ctx_rank * 16 + z * 4 + yl * 2 + core
    q_bias_grad = lax.dynamic_slice_in_dim(
        bias_sum[:, :HALF_Q].reshape(D), device * ROWS, ROWS, 0
    )
    k_bias_grad = bias_sum[:, HALF_Q : HALF_Q + HD].reshape(KVH * HD)
    v_bias_grad = lax.dynamic_slice_in_dim(
        bias_sum[:, HALF_Q + HD :].reshape(KVH * HD), device * 2, 2, 0
    )
    return (
        layer_out,
        input_grad,
        attn_gain_grad,
        q_weight_grad,
        q_bias_grad,
        k_weight_grad,
        k_bias_grad,
        v_weight_grad,
        v_bias_grad,
        o_weight_grad,
        mlp_gain_grad,
        gate_weight_grad,
        up_weight_grad,
        down_weight_grad,
    )


def solution(mesh):
    fine = Mesh(mesh.devices.reshape(2, 4, 4, 2, 2), AXES)
    acts = P(("z", "yl", "core"), None, CTX, None)
    vec, mat = P(AXES), P(AXES, None)
    return jax.shard_map(
        per_device,
        mesh=fine,
        in_specs=(acts, acts, vec, mat, vec, mat, vec, mat, vec, mat, vec, mat, mat, mat),
        out_specs=(acts, acts, vec, mat, vec, mat, P(), mat, vec, mat, vec, mat, mat, mat),
        check_vma=False,
    )
```

```python
import math

import jax
import jax.numpy as jnp
from jax import lax
from jax.experimental import pallas as pl
from jax.experimental.layout import Layout, with_layout_constraint
from jax.experimental.pallas import tpu as pltpu
from jax.sharding import Mesh, PartitionSpec as P

H = 12
KVH = 2
HD = 128
GROUP = H // KVH
D = 1536
FF = 8960
BLK = 64
N_CTX = 8
ROWS = 12
PAD = 16
FFS = 1152
HALF_Q = GROUP * HD
QKV = HALF_Q + 2 * HD
MISC = 128
QKVM = QKV + MISC
FFW = 3 * FFS
XCOLS = D // 4 + PAD
SIDE = QKVM + HALF_Q

epsilon = 1e-06
rope_base = 1000000.0

AXES = ("yh", "x", "z", "yl", "core")
Y = ("yh", "yl")
CTX = ("yh", "x")
TP = ("x", "core")
F32 = jnp.float32
BF = jnp.bfloat16


def add_low(left, right):
    return (left.astype(F32) + right.astype(F32)).astype(BF)


def swap_core(arr):
    return lax.ppermute(arr, "core", [(0, 1), (1, 0)])


def swap_yh(arr):
    return lax.ppermute(arr, "yh", [(0, 1), (1, 0)])


def to_x(arr, k):
    return lax.ppermute(arr, "x", [(i, i ^ k) for i in range(4)])


def after(arr, *earlier):
    return lax.optimization_barrier((arr,) + earlier)[0]


def row_major(arr):
    return with_layout_constraint(arr, Layout(major_to_minor=(0, 1)))


def exchange(arr, axis):
    return lax.all_to_all(arr, axis, split_axis=0, concat_axis=0, tiled=True)


def spread(block, axis, count):
    return exchange(jnp.tile(block, (count, 1)), axis)


def neighbours(block):
    mine = jnp.concatenate([block] + [to_x(block, k) for k in range(1, 4)], 0)
    return jnp.concatenate([mine, swap_core(mine)], 0)


def neighbours_sum(mine):
    rows = mine.shape[0] // 4
    total = mine[:rows].astype(F32)
    for k in range(1, 4):
        total = total + to_x(mine[k * rows : (k + 1) * rows], k).astype(F32)
    return total


def collect(whole, axis, count):
    return added(exchange(whole, axis), count)


def added(got, count):
    got = got.reshape(count, got.shape[0] // count, got.shape[1])
    return jnp.sum(got.astype(F32), axis=0).astype(BF)


def rope_tables(positions):
    half_dim = HD // 2
    frequency = jnp.exp(
        jnp.arange(half_dim, dtype=F32) * (-2.0 * math.log(rope_base) / HD)
    )
    angles = positions.astype(F32)[:, None] * frequency[None, :]
    cosine_tab = jnp.cos(angles)
    sine_tab = jnp.sin(angles)
    return (
        jnp.concatenate([cosine_tab, cosine_tab], -1),
        jnp.concatenate([sine_tab, sine_tab], -1),
    )


def rotate(values, cosine_tab, sine_tab):
    half_dim = values.shape[-1] // 2
    turned = jnp.concatenate([-values[..., half_dim:], values[..., :half_dim]], -1)
    return values * cosine_tab + turned * sine_tab


def unrotate(grads_in, cosine_tab, sine_tab):
    half_dim = grads_in.shape[-1] // 2
    scaled = grads_in * sine_tab
    return grads_in * cosine_tab + jnp.concatenate(
        [scaled[..., half_dim:], -scaled[..., :half_dim]], -1
    )


def product(left_arr, right_arr):
    return jnp.dot(left_arr, right_arr, preferred_element_type=F32)


def against(left_arr, right_arr):
    return lax.dot_general(
        left_arr, right_arr, (((1,), (1,)), ((), ())), preferred_element_type=F32
    )


def over_rows(left_arr, right_arr):
    return lax.dot_general(
        left_arr, right_arr, (((0,), (0,)), ((), ())), preferred_element_type=F32
    )


VMEM = pl.BlockSpec(memory_space=pltpu.VMEM)
ANY = pl.BlockSpec(memory_space=pl.ANY)
HBM = pl.BlockSpec(memory_space=pltpu.HBM)
MIB = 1 << 20


def call(body, outs, ins, out_specs, scratch=(), flops=0, moved=0, vmem=48 * MIB):
    return pl.pallas_call(
        body,
        out_shape=outs,
        in_specs=ins,
        out_specs=out_specs,
        scratch_shapes=scratch,
        compiler_params=pltpu.CompilerParams(vmem_limit_bytes=vmem),
        cost_estimate=pl.CostEstimate(flops=flops, bytes_accessed=moved, transcendentals=0),
    )


def fetch(sources, targets, sems):
    copies = [
        pltpu.make_async_copy(src, dst, sems.at[i])
        for i, (src, dst) in enumerate(zip(sources, targets))
    ]
    for one in copies:
        one.start()
    for one in copies:
        one.wait()


def hold(arr, *earlier):
    def body(*refs):
        refs[-1][...] = refs[0][...]

    out = jax.ShapeDtypeStruct(arr.shape, arr.dtype)
    size = 2 * arr.size * arr.dtype.itemsize
    return call(body, out, [VMEM] + [ANY] * len(earlier), VMEM, moved=size)(arr, *earlier)


def pack_attn_body(*refs):
    out, held, square, sems = refs[9], refs[10:19], refs[19], refs[20]
    fetch(refs[:9], held, sems)
    q_v, k_v, v_v, o_v = held[5:]
    square[...] = jnp.zeros_like(square)
    for i, vector in enumerate(held[:5]):
        square[i : i + 1, : vector.shape[1]] = vector[...].astype(F32)
    misc = square[...].T[:PAD].astype(BF)
    for t in range(8):
        h = t % 2
        rows = slice(t * PAD, t * PAD + ROWS)
        out[t * PAD : (t + 1) * PAD, :] = jnp.zeros((PAD, SIDE), BF)
        out[rows, :HALF_Q] = q_v[:, h * HALF_Q : (h + 1) * HALF_Q]
        out[rows, HALF_Q : HALF_Q + HD] = k_v[:, h * HD : (h + 1) * HD]
        out[rows, HALF_Q + HD : QKV] = v_v[:, h * HD : (h + 1) * HD]
        out[t * PAD : (t + 1) * PAD, QKV:QKVM] = misc
        out[rows, QKVM:SIDE] = o_v[:, h * HALF_Q : (h + 1) * HALF_Q]


def pack_attn(*arrays):
    out = jax.ShapeDtypeStruct((8 * PAD, SIDE), BF)
    scratch = [pltpu.VMEM(a.shape, BF) for a in arrays]
    scratch += [pltpu.VMEM((MISC, MISC), F32), pltpu.SemaphoreType.DMA((9,))]
    return call(pack_attn_body, out, [HBM] * 9, VMEM, scratch, moved=MIB, vmem=60 * MIB)(
        *arrays
    )


def pack_ff_body(gate, up, down, out, gate_v, up_v, down_v, sems):
    fetch((gate, up, down), (gate_v, up_v, down_v), sems)
    for t in range(8):
        out[t * PAD : (t + 1) * PAD, :] = jnp.zeros((PAD, FFW), BF)
        width = min(FFS, FF - t * FFS)
        for i, ref in enumerate((gate_v, up_v, down_v)):
            out[t * PAD : t * PAD + ROWS, i * FFS : i * FFS + width] = ref[
                :, t * FFS : t * FFS + width
            ]


def pack_ff(*arrays):
    out = jax.ShapeDtypeStruct((8 * PAD, FFW), BF)
    scratch = [pltpu.VMEM(a.shape, BF) for a in arrays] + [pltpu.SemaphoreType.DMA((3,))]
    return call(pack_ff_body, out, [HBM] * 3, VMEM, scratch, moved=2 * MIB)(*arrays)


def unpack_body(
    index, attn, late, q_w, k_w, v_w, gate_w, up_w,
    q, k, v, o, gate, up, down, biases, gains,
):
    x, core = index[0], index[1]

    def block(i, h, start, width):
        row = pl.multiple_of((core ^ h) * PAD, PAD)
        return late[x ^ i, pl.ds(row, PAD), start : start + width].astype(F32)[:ROWS]

    def gain_part(weight, start, grad):
        width = grad.shape[1]
        part = weight[:, start : start + width].astype(F32) * grad
        return jnp.sum(part, axis=1, keepdims=True)

    attn_gain = jnp.zeros((ROWS, 1), F32)
    for h in range(2):
        part = attn[core ^ h].astype(F32)
        biases[h : h + 1, :] = part[ROWS : ROWS + 1]
        for ref, weight, start, width in (
            (q, q_w, 0, HALF_Q),
            (k, k_w, HALF_Q, HD),
            (v, v_w, HALF_Q + HD, HD),
        ):
            piece = part[:ROWS, start : start + width]
            ref[:, h * width : (h + 1) * width] = piece
            attn_gain = attn_gain + gain_part(weight, h * width, piece)
        o[:, h * HALF_Q : (h + 1) * HALF_Q] = sum(block(i, h, FFW, HALF_Q) for i in range(4))
    mlp_gain = jnp.zeros((ROWS, 1), F32)
    for t in range(8):
        width = min(FFS, FF - t * FFS)
        for i, (ref, weight) in enumerate(((gate, gate_w), (up, up_w), (down, None))):
            piece = block(t // 2, t % 2, i * FFS, width)
            ref[:, t * FFS : t * FFS + width] = piece
            if weight is not None:
                mlp_gain = mlp_gain + gain_part(weight, t * FFS, piece)
    gains[:, 0:1] = attn_gain
    gains[:, 1:2] = mlp_gain


def unpack_grads(index, *arrays):
    shapes = [(ROWS, D), (ROWS, KVH * HD), (ROWS, KVH * HD), (ROWS, D)]
    shapes += [(ROWS, FF)] * 3 + [(2, QKV), (ROWS, 2)]
    outs = [jax.ShapeDtypeStruct(dims, F32) for dims in shapes]
    ins = [pl.BlockSpec(memory_space=pltpu.SMEM)] + [VMEM] * 7
    return call(unpack_body, outs, ins, [VMEM] * 9, moved=5 * MIB)(index, *arrays)


def turn(values, cosine, sine, back):
    low = lax.broadcasted_iota(jnp.int32, values.shape, 1) < HD // 2
    if back:
        moved = pltpu.roll(values * sine, HD // 2, 1)
        return values * cosine + jnp.where(low, moved, -moved)
    moved = pltpu.roll(values, HD // 2, 1)
    return values * cosine + jnp.where(low, -moved, moved) * sine


def project_body(normed, weights, bias, cosine, sine, query, kv, w_v, sems):
    fetch((weights.at[:, pl.ds(0, QKV)],), (w_v,), sems)
    lin = product(normed[...], w_v[...]) + bias[...]
    for s in range(2):
        rows = slice(s * 2 * BLK, (s + 1) * 2 * BLK)
        for r in range(GROUP + 1):
            head = turn(lin[rows, r * HD : (r + 1) * HD], cosine[...], sine[...], False)
            if r < GROUP:
                query[rows, r * HD : (r + 1) * HD] = head.astype(BF)
            else:
                kv[rows, :HD] = head.astype(BF)
    kv[:, HD:] = lin[:, HALF_Q + HD :].astype(BF)


def project(normed, weights, bias, cosine, sine):
    count = normed.shape[0]
    outs = [jax.ShapeDtypeStruct((count, w), BF) for w in (HALF_Q, 2 * HD)]
    scratch = [pltpu.VMEM((D, QKV), BF), pltpu.SemaphoreType.DMA((1,))]
    return call(
        project_body, outs, [VMEM, ANY] + [VMEM] * 3, [VMEM] * 2, scratch,
        flops=2 * count * D * QKV, moved=5 * MIB,
    )(normed, weights, bias, cosine, sine)


def stacked(parts, s, start):
    own = 2 * BLK
    return jnp.concatenate(
        [
            part[(2 * h + s) * own : (2 * h + s + 1) * own, start : start + HD]
            for part in parts
            for h in range(2)
        ],
        0,
    )


def positions_of(block, iota):
    return jnp.where(iota < BLK, block * BLK, (2 * N_CTX - 2 - block) * BLK) + iota


def attend_body(index, query, kv0, kv1, kv2, kv3, context, probs, mask, p_v, sems):
    own = 2 * BLK
    yh, x = index[0], index[1]
    here = positions_of(yh * 4 + x, lax.broadcasted_iota(jnp.int32, (own, own), 1))
    for j in range(N_CTX):
        source = ((j % 2) ^ yh) * 4 + ((j // 2) ^ x)
        there = positions_of(source, lax.broadcasted_iota(jnp.int32, (own, own), 0))
        mask[j * own : (j + 1) * own, :] = jnp.where(here >= there, 0.0, -1e30)
    parts = (kv0, kv1, kv2, kv3)
    copies = []
    for s in range(2):
        keys = stacked(parts, s, 0)
        values = stacked(parts, s, HD).T
        rows = slice(s * own, (s + 1) * own)
        for r in range(GROUP):
            head = s * GROUP + r
            scores = against(keys, query[rows, r * HD : (r + 1) * HD])
            scores = scores * (1.0 / math.sqrt(HD)) + mask[...]
            terms = jnp.exp(scores - jnp.max(scores, axis=0, keepdims=True))
            p = terms / jnp.sum(terms, axis=0, keepdims=True)
            p_v[head] = p
            copies.append(pltpu.make_async_copy(p_v.at[head], probs.at[head], sems.at[head]))
            copies[-1].start()
            context[rows, r * HD : (r + 1) * HD] = product(values, p.astype(BF)).T.astype(BF)
    for one in copies:
        one.wait()


def attend(index, query, parts):
    heads, keys, own = 2 * GROUP, 2 * N_CTX * BLK, 2 * BLK
    outs = [
        jax.ShapeDtypeStruct(query.shape, BF),
        jax.ShapeDtypeStruct((heads, keys, own), F32),
    ]
    scratch = [
        pltpu.VMEM((keys, own), F32),
        pltpu.VMEM((heads, keys, own), F32),
        pltpu.SemaphoreType.DMA((heads,)),
    ]
    return call(
        attend_body, outs, [pl.BlockSpec(memory_space=pltpu.SMEM)] + [VMEM] * 5, [VMEM, ANY],
        scratch, flops=4 * heads * keys * own * HD, moved=8 * MIB,
    )(index, query, *parts)


def attend_back_body(
    branch, weights, query, kv0, kv1, kv2, kv3, probs, cosine, sine,
    grad_query, out0, out1, out2, out3, w_v, p_v, sems,
):
    own, heads = 2 * BLK, 2 * GROUP
    scale = 1.0 / math.sqrt(HD)
    weight = pltpu.make_async_copy(weights.at[:, pl.ds(QKVM, HALF_Q)], w_v, sems.at[heads])
    weight.start()
    loads = [
        pltpu.make_async_copy(probs.at[i], p_v.at[i], sems.at[i]) for i in range(heads)
    ]
    for one in loads:
        one.start()
    weight.wait()
    grad_context = product(branch[...], w_v[...]).astype(BF)
    parts, outs = (kv0, kv1, kv2, kv3), (out0, out1, out2, out3)
    for s in range(2):
        keys = stacked(parts, s, 0).T
        values = stacked(parts, s, HD)
        rows = slice(s * own, (s + 1) * own)
        grad_key = jnp.zeros((2 * N_CTX * BLK, HD), F32)
        grad_value = jnp.zeros((2 * N_CTX * BLK, HD), F32)
        for r in range(GROUP):
            columns = slice(r * HD, (r + 1) * HD)
            loads[s * GROUP + r].wait()
            p = p_v[s * GROUP + r]
            grad = grad_context[rows, columns]
            grad_p = against(values, grad)
            delta = jnp.sum(p * grad_p, axis=0, keepdims=True)
            grad_s = (p * (grad_p - delta)).astype(BF)
            back = product(keys, grad_s).T * scale
            grad_query[rows, columns] = turn(back, cosine[...], sine[...], True).astype(BF)
            grad_key = grad_key + product(grad_s, query[rows, columns])
            grad_value = grad_value + product(p.astype(BF), grad)
        for k, out in enumerate(outs):
            for h in range(2):
                to = slice((2 * h + s) * own, (2 * h + s + 1) * own)
                at = slice((2 * k + h) * own, (2 * k + h + 1) * own)
                out[to, :HD] = (grad_key[at] * scale).astype(BF)
                out[to, HD:] = grad_value[at].astype(BF)


def attend_back(branch, weights, query, parts, probs, cosine, sine):
    heads, keys, own = probs.shape
    outs = [jax.ShapeDtypeStruct(query.shape, BF)]
    outs += [jax.ShapeDtypeStruct(p.shape, BF) for p in parts]
    scratch = [
        pltpu.VMEM((D, HALF_Q), BF),
        pltpu.VMEM(probs.shape, F32),
        pltpu.SemaphoreType.DMA((heads + 1,)),
    ]
    return call(
        attend_back_body, outs, [VMEM, ANY] + [VMEM] * 5 + [ANY] + [VMEM] * 2, [VMEM] * 5,
        scratch, flops=10 * heads * keys * own * HD, moved=12 * MIB,
    )(branch, weights, query, *parts, probs, cosine, sine)


def weight_terms_body(rows, grads, inner, mixed, *refs):
    out = refs[-1]
    wide = inner.shape[1]
    out[:, :wide] = product(rows[...].T, inner[...]).astype(BF)
    out[:, wide : wide + mixed.shape[1]] = product(grads[...].T, mixed[...]).astype(BF)


def weight_terms(rows, grads, inner, mixed, width, *earlier):
    count = rows.shape[0]
    tile = 256
    column = pl.BlockSpec((count, tile), lambda i: (0, i))
    whole = [pl.BlockSpec(a.shape, lambda i: (0, 0)) for a in (inner, mixed)]
    return pl.pallas_call(
        weight_terms_body,
        grid=(D // tile,),
        out_shape=jax.ShapeDtypeStruct((D, width), BF),
        in_specs=[column, column] + whole + [ANY] * len(earlier),
        out_specs=pl.BlockSpec((tile, width), lambda i: (i, 0)),
        compiler_params=pltpu.CompilerParams(vmem_limit_bytes=48 * MIB),
        cost_estimate=pl.CostEstimate(
            flops=2 * count * D * FFW, bytes_accessed=26 * MIB, transcendentals=0
        ),
    )(rows, grads, inner, mixed, *earlier)


def fill_body(buffer, branch, context, out, part, sems):
    part[...] = product(branch[...].T, context[...]).astype(BF)
    fetch((part,), (out.at[:, pl.ds(FFW, HALF_Q)],), sems)


def fill(buffer, branch, context):
    return pl.pallas_call(
        fill_body,
        out_shape=jax.ShapeDtypeStruct(buffer.shape, BF),
        in_specs=[ANY, VMEM, VMEM],
        out_specs=ANY,
        scratch_shapes=[pltpu.VMEM((D, HALF_Q), BF), pltpu.SemaphoreType.DMA((1,))],
        input_output_aliases={0: 0},
        compiler_params=pltpu.CompilerParams(vmem_limit_bytes=48 * MIB),
        cost_estimate=pl.CostEstimate(
            flops=4 * BLK * 2 * D * HALF_Q, bytes_accessed=4 * MIB, transcendentals=0
        ),
    )(buffer, branch, context)


def plane_sum_body(index, got, *refs):
    keep, give = refs[-2:]
    parts = sum(got[i].astype(F32) for i in range(16)).astype(BF)
    first = index[0] == 0
    keep[...] = jnp.where(first, parts[0], parts[1])
    give[...] = jnp.where(first, parts[1], parts[0])


def plane_sum(index, got, *earlier):
    outs = [jax.ShapeDtypeStruct(got.shape[2:], BF)] * 2
    ins = [pl.BlockSpec(memory_space=pltpu.SMEM), VMEM] + [ANY] * len(earlier)
    return call(plane_sum_body, outs, ins, [VMEM] * 2, moved=2 * MIB)(index, got, *earlier)


def down_body(mixed, weights, *refs):
    mine, others, w_v, sems = refs[-4:]
    fetch((weights.at[:, pl.ds(2 * FFS, FFS)],), (w_v,), sems)
    tile = 256
    half = mine.shape[0]
    for base, out in ((half, others), (0, mine)):

        @pl.loop(0, half // tile)
        def _(i):
            at = pl.ds(pl.multiple_of(base + i * tile, tile), tile)
            to = pl.ds(pl.multiple_of(i * tile, tile), tile)
            out[to, :] = against(mixed[at, :], w_v[...]).astype(BF)


def down(mixed, weights, *earlier):
    half = mixed.shape[0] // 2
    outs = [jax.ShapeDtypeStruct((half, D), BF)] * 2
    scratch = [pltpu.VMEM((D, FFS), BF), pltpu.SemaphoreType.DMA((1,))]
    return call(
        down_body, outs, [VMEM, ANY] + [ANY] * len(earlier), [VMEM] * 2, scratch,
        flops=4 * half * D * FFS, moved=9 * MIB,
    )(mixed, weights, *earlier)


def ffn_body(
    rows, grads, weights, mixed, inner, back, back_others,
    rows_v, grads_v, gate_v, up_v, down_v, g_v, u_v, sems,
):
    half = rows.shape[0] // 2
    pairs = [
        (rows, rows_v),
        (weights.at[:, pl.ds(0, FFS)], gate_v),
        (weights.at[:, pl.ds(FFS, FFS)], up_v),
        (grads, grads_v),
        (weights.at[:, pl.ds(2 * FFS, FFS)], down_v),
    ]
    loads = [
        pltpu.make_async_copy(src, dst, sems.at[i]) for i, (src, dst) in enumerate(pairs)
    ]
    for one in loads:
        one.start()
    tile = 256
    steps = half // tile
    for one in loads[:2]:
        one.wait()

    @pl.loop(0, 2 * steps)
    def _(i):
        at = pl.ds(pl.multiple_of(i * tile, tile), tile)
        g_v[at, :] = product(rows_v[at, :], gate_v[...])

    loads[2].wait()

    @pl.loop(0, 2 * steps)
    def _(i):
        at = pl.ds(pl.multiple_of(i * tile, tile), tile)
        u_v[at, :] = product(rows_v[at, :], up_v[...])

    for one in loads[3:]:
        one.wait()

    for base, out in ((half, back_others), (0, back)):

        @pl.loop(0, steps)
        def _(i):
            at = pl.ds(pl.multiple_of(base + i * tile, tile), tile)
            grad_mixed = product(grads_v[at, :], down_v[...])
            gate_val = g_v[at, :]
            up_val = u_v[at, :]
            gate_sig = jax.nn.sigmoid(gate_val)
            swish = gate_val * gate_sig
            mixed[at, :] = (swish * up_val).astype(BF)
            grad_up = (grad_mixed * swish).astype(BF)
            grad_gate = (
                grad_mixed * up_val * gate_sig * (1.0 + gate_val * (1.0 - gate_sig))
            ).astype(BF)
            inner[at, :FFS] = grad_gate
            inner[at, FFS:] = grad_up
            to = pl.ds(pl.multiple_of(i * tile, tile), tile)
            out[to, :] = (
                against(grad_gate, gate_v[...]) + against(grad_up, up_v[...])
            ).astype(BF)


def ffn(rows, grads, weights):
    count = rows.shape[0]
    half = count // 2
    dims = [(count, FFS), (count, 2 * FFS), (half, D), (half, D)]
    outs = [jax.ShapeDtypeStruct(d, BF) for d in dims]
    scratch = [pltpu.VMEM((count, D), BF)] * 2 + [pltpu.VMEM((D, FFS), BF)] * 3
    scratch += [pltpu.VMEM((count, FFS), F32)] * 2 + [pltpu.SemaphoreType.DMA((5,))]
    return call(
        ffn_body, outs, [ANY] * 3, [VMEM] * 4, scratch,
        flops=10 * count * D * FFS, moved=28 * MIB, vmem=56 * MIB,
    )(rows, grads, weights)


def per_device(
    tokens,
    cotangent,
    attn_gain,
    q_weight,
    q_bias,
    k_weight,
    k_bias,
    v_weight,
    v_bias,
    o_weight,
    mlp_gain,
    gate_weight,
    up_weight,
    down_weight,
):
    yh, x, z, yl, core = [lax.axis_index(a) for a in AXES]
    y = yh * 2 + yl
    ctx_rank = yh * 4 + x
    own = 2 * BLK
    both = 2 * own
    is_zero = core == 0

    place = jnp.arange(D, dtype=jnp.int32)
    place_r = place % ROWS
    place_x = place // ROWS % 4
    place_c = place // (ROWS * 4) % 2
    place_y = place // (ROWS * 8) % 4
    place_z = place // (ROWS * 32)
    place_dev = (((place_y // 2 * 4 + place_x) * 4 + place_z) * 2 + place_y % 2) * 2 + place_c
    natural = place_dev * ROWS + place_r
    to_order = (place[:, None] == natural[None, :]).astype(BF)

    tokens_flat = tokens.reshape(own, D)
    tokens_both = jnp.concatenate([tokens_flat, swap_core(tokens_flat)], 0)

    vectors = [arr[None] for arr in (attn_gain, mlp_gain, q_bias, k_bias, v_bias)]
    got = exchange(pack_attn(*vectors, q_weight, k_weight, v_weight, o_weight), TP)
    got_ff = after(pack_ff(gate_weight, up_weight, down_weight), got)
    got_ff = exchange(got_ff, TP)
    grad_low = product(cotangent.reshape(own, D), to_order).astype(BF)
    want = jnp.arange(8 * ROWS, dtype=jnp.int32)
    at = (want // ROWS % 4 * 2 + want // (4 * ROWS)) * PAD + want % ROWS
    pick = (at[:, None] == jnp.arange(8 * PAD, dtype=jnp.int32)[None, :]).astype(BF)
    rows_attn = product(pick, got).astype(BF)
    rows_ff = product(pick, got_ff).astype(BF)

    plane = ("z",) + Y
    grad_rows = neighbours(after(grad_low, rows_attn))
    attn_all = lax.all_gather(rows_attn, plane, axis=0, tiled=True)
    ff_all = lax.all_gather(rows_ff, plane, axis=0, tiled=True)
    attn_all = after(attn_all, grad_rows)
    weight_qkv = attn_all[:, :QKV]
    weight_o = attn_all[:, QKVM:]

    eight = (jnp.arange(8)[:, None] == jnp.arange(MISC)[None, :]).astype(BF)
    misc_rows = against(eight, attn_all[:, QKV:QKVM])
    gain_one = misc_rows[0:1]
    gain_two = misc_rows[1:2]
    bias_rows = misc_rows.astype(BF)
    bias_q = against(bias_rows[2:3], to_order)
    small = jnp.arange(KVH * HD, dtype=jnp.int32)
    to_small = (
        ((place_dev * 2 + place_r)[:, None] == small[None, :]) & (place_r < 2)[:, None]
    ).astype(BF)
    bias_kv = product(bias_rows[3:5], to_small)

    def side_of(row, width):
        return jnp.where(is_zero, row[:, :width], row[:, width:])

    bias_qkv = jnp.concatenate(
        [
            side_of(bias_q, HALF_Q),
            side_of(bias_kv[0:1], HD),
            side_of(bias_kv[1:2], HD),
        ],
        1,
    )

    offsets = jnp.arange(BLK, dtype=jnp.int32)
    query_pos = jnp.concatenate(
        [ctx_rank * BLK + offsets, (2 * N_CTX - 1 - ctx_rank) * BLK + offsets]
    )
    cosine_tab, sine_tab = rope_tables(query_pos)
    cosine_b = jnp.concatenate([cosine_tab, cosine_tab], 0)
    sine_b = jnp.concatenate([sine_tab, sine_tab], 0)

    inputs = product(tokens_both, to_order)
    scale_one = lax.rsqrt(jnp.mean(inputs * inputs, axis=-1, keepdims=True) + epsilon)
    unit_one = inputs * scale_one
    normed_one = (unit_one * gain_one).astype(BF)
    query_rot, kv_send = project(normed_one, attn_all, bias_qkv, cosine_tab, sine_tab)
    kv_parts = jnp.concatenate([kv_send, swap_yh(kv_send)], 0)
    kv_parts = [kv_parts] + [to_x(kv_parts, k) for k in range(1, 4)]
    slot = jnp.arange(4 * XCOLS, dtype=jnp.int32)
    slot_p = slot % XCOLS
    slot_zy = slot_p // (2 * ROWS)
    slot_dev = (slot_zy % 4 // 2 * 4 + slot // XCOLS) * 4 + slot_zy // 4
    slot_dev = (slot_dev * 2 + slot_zy % 2) * 2 + slot_p // ROWS % 2
    slot_at = jnp.where(slot_p < D // 4, slot_dev * ROWS + slot_p % ROWS, -1)
    by_x = (natural[:, None] == slot_at[None, :]).astype(BF)
    normed_x = jnp.where(
        (slot_p == D // 4)[None, :], 1.0, product(normed_one, by_x)
    ).astype(BF)
    query_rot = after(query_rot, normed_x)
    context_low, probs = attend(jnp.stack([yh, x]), query_rot, kv_parts)
    branch = against(context_low, weight_o)
    hidden_one = (
        inputs[:own] + branch[:own] + swap_core(branch[own:].astype(BF)).astype(F32)
    )
    scale_two = lax.rsqrt(jnp.mean(hidden_one * hidden_one, axis=-1, keepdims=True) + epsilon)
    unit_two = hidden_one * scale_two
    normed_two = (unit_two * gain_two).astype(BF)

    normed_rows = neighbours(normed_two)
    mixed_low, grad_inner, *grad_norm_part = ffn(
        normed_rows, grad_rows, ff_all
    )
    grad_norm_mine = add_low(grad_norm_part[0], swap_core(grad_norm_part[1]))
    grad_norm_two = neighbours_sum(grad_norm_mine)
    ff_buffer = weight_terms(
        normed_rows, grad_rows, grad_inner, mixed_low, FFW + HALF_Q, grad_norm_mine
    )
    grad_norm_two = after(grad_norm_two, ff_buffer)

    grad_unit_two = grad_norm_two * gain_two
    grad_hidden = grad_low.astype(F32) + scale_two * (
        grad_unit_two - unit_two * jnp.mean(grad_unit_two * unit_two, axis=-1, keepdims=True)
    )
    grad_branch = grad_hidden.astype(BF)
    grad_branch = jnp.concatenate([grad_branch, swap_core(grad_branch)], 0)
    late_grads = fill(ff_buffer, grad_branch, context_low)
    late_sum = lax.psum_scatter(late_grads, plane, scatter_dimension=0, tiled=True)
    branch_ready = hold(grad_branch, late_grads)
    grad_query, *kv_grads = attend_back(
        branch_ready, attn_all, query_rot, kv_parts, probs, cosine_tab, sine_tab
    )
    kv_grads = [kv_grads[0]] + [to_x(kv_grads[k], k) for k in range(1, 4)]
    q_grads = row_major(over_rows(normed_x, hold(grad_query, *kv_grads[1:])).astype(BF))
    q_got = exchange(q_grads, "x")
    grad_kv = sum(part.astype(F32) for part in kv_grads)
    grad_kv = grad_kv[:both] + swap_yh(grad_kv[both:].astype(BF)).astype(F32)
    grad_key = unrotate(grad_kv[:, :HD], cosine_b, sine_b)
    grad_kv = jnp.concatenate([grad_key, grad_kv[:, HD:]], 1).astype(BF)
    down_mine, down_others = down(mixed_low, ff_all, q_grads)
    grad_kv = hold(grad_kv, down_mine)
    kv_grads = row_major(over_rows(normed_x, grad_kv).astype(BF))
    kv_pieces = [
        lax.dynamic_slice_in_dim(kv_grads, (x ^ k) * XCOLS, XCOLS, 0) for k in range(4)
    ]
    kv_pieces = [kv_pieces[0]] + [to_x(kv_pieces[k], k) for k in range(1, 4)]
    kv_sum = sum(part.astype(F32) for part in kv_pieces).astype(BF)
    down_both = add_low(down_mine, swap_core(down_others)).reshape(4, own, D)
    down_both = jnp.concatenate(
        [lax.dynamic_index_in_dim(down_both, k ^ x, 0, False) for k in range(4)], 0
    )
    down_terms = lax.psum_scatter(down_both, "x", scatter_dimension=0, tiled=True)
    layer_sum = (hidden_one + down_terms.astype(F32)).astype(BF)
    layer_out = against(layer_sum, to_order).astype(BF).reshape(tokens.shape)
    grad_lin = hold(jnp.concatenate([grad_query, grad_kv], 1), kv_grads)
    grad_norm_one = against(grad_lin, weight_qkv)
    grad_norm_one = grad_norm_one[:own] + swap_core(grad_norm_one[own:].astype(BF)).astype(F32)
    unit_own = unit_one[:own]
    grad_unit_one = grad_norm_one * gain_one
    input_grad = grad_hidden + scale_one[:own] * (
        grad_unit_one - unit_own * jnp.mean(grad_unit_one * unit_own, axis=-1, keepdims=True)
    )
    input_high = input_grad.astype(BF)
    input_rest = (input_grad - input_high.astype(F32)).astype(BF)
    input_grad = (against(input_high, to_order) + against(input_rest, to_order)).reshape(
        tokens.shape
    )

    qkv_sum = jnp.concatenate([added(q_got, 4), kv_sum], 1)
    spot = jnp.arange(16 * 2 * PAD, dtype=jnp.int32)
    spot_r = spot % PAD
    spot_at = spot // PAD * ROWS + spot_r
    spot_at = jnp.where(spot_r < ROWS, spot_at, jnp.where(spot_r == ROWS, D // 4, -1))
    room = (spot_at[:, None] == jnp.arange(XCOLS, dtype=jnp.int32)[None, :]).astype(BF)
    qkv_rows = product(room, qkv_sum).astype(BF)

    spot = jnp.arange(8 * PAD, dtype=jnp.int32)
    spot_at = ((spot // (4 * PAD)) ^ core) * 4 + ((spot // PAD % 4) ^ x)
    spot_at = jnp.where(spot % PAD < ROWS, spot_at * ROWS + spot % PAD, -1)
    late_pick = (want[:, None] == spot_at[None, :]).astype(BF)
    late = over_rows(late_pick, hold(late_sum, qkv_rows)).astype(BF)
    late_pair = [late[: 4 * PAD], swap_core(late[4 * PAD :])]
    late_pair = [part.reshape(4, PAD, FFW + HALF_Q) for part in late_pair]
    late = jnp.concatenate(late_pair, 1)
    late = [late[0]] + [to_x(late[k], k) for k in range(1, 4)]
    qkv_sum = exchange(qkv_rows, plane)
    qkv_keep, qkv_give = plane_sum(core[None], qkv_sum.reshape(16, 2, PAD, QKV), *late[1:])
    qkv_sum = jnp.stack([qkv_keep, swap_core(qkv_give)])
    (
        q_weight_grad,
        k_weight_grad,
        v_weight_grad,
        o_weight_grad,
        gate_weight_grad,
        up_weight_grad,
        down_weight_grad,
        bias_sum,
        gain_sum,
    ) = unpack_grads(
        jnp.stack([x, core]), qkv_sum, jnp.stack(late),
        q_weight, k_weight, v_weight, gate_weight, up_weight,
    )
    attn_gain_grad = gain_sum[:, 0] / attn_gain.astype(F32)
    mlp_gain_grad = gain_sum[:, 1] / mlp_gain.astype(F32)
    device = ctx_rank * 16 + z * 4 + yl * 2 + core
    q_bias_grad = lax.dynamic_slice_in_dim(
        bias_sum[:, :HALF_Q].reshape(D), device * ROWS, ROWS, 0
    )
    k_bias_grad = bias_sum[:, HALF_Q : HALF_Q + HD].reshape(KVH * HD)
    v_bias_grad = lax.dynamic_slice_in_dim(
        bias_sum[:, HALF_Q + HD :].reshape(KVH * HD), device * 2, 2, 0
    )
    return (
        layer_out,
        input_grad,
        attn_gain_grad,
        q_weight_grad,
        q_bias_grad,
        k_weight_grad,
        k_bias_grad,
        v_weight_grad,
        v_bias_grad,
        o_weight_grad,
        mlp_gain_grad,
        gate_weight_grad,
        up_weight_grad,
        down_weight_grad,
    )


def solution(mesh):
    fine = Mesh(mesh.devices.reshape(2, 4, 4, 2, 2), AXES)
    acts = P(("z", "yl", "core"), None, CTX, None)
    vec, mat = P(AXES), P(AXES, None)
    return jax.shard_map(
        per_device,
        mesh=fine,
        in_specs=(acts, acts, vec, mat, vec, mat, vec, mat, vec, mat, vec, mat, mat, mat),
        out_specs=(acts, acts, vec, mat, vec, mat, P(), mat, vec, mat, vec, mat, mat, mat),
        check_vma=False,
    )
```

```python
import math

import jax
import jax.numpy as jnp
from jax import lax
from jax.experimental import pallas as pl
from jax.experimental.layout import Layout, with_layout_constraint
from jax.experimental.pallas import tpu as pltpu
from jax.sharding import Mesh, PartitionSpec as P

H = 12
KVH = 2
HD = 128
GROUP = H // KVH
D = 1536
FF = 8960
BLK = 64
N_CTX = 8
ROWS = 12
PAD = 16
FFS = 1152
HALF_Q = GROUP * HD
QKV = HALF_Q + 2 * HD
MISC = 128
PAIRS = GROUP // 2
QKVM = QKV + MISC
FFW = 3 * FFS
XCOLS = D // 4 + PAD
SIDE = QKVM + HALF_Q

epsilon = 1e-06
rope_base = 1000000.0

AXES = ("yh", "x", "z", "yl", "core")
Y = ("yh", "yl")
CTX = ("yh", "x")
TP = ("x", "core")
F32 = jnp.float32
BF = jnp.bfloat16


def add_low(left, right):
    return (left.astype(F32) + right.astype(F32)).astype(BF)


def swap_core(arr):
    return lax.ppermute(arr, "core", [(0, 1), (1, 0)])


def swap_yh(arr):
    return lax.ppermute(arr, "yh", [(0, 1), (1, 0)])


def to_x(arr, k):
    return lax.ppermute(arr, "x", [(i, i ^ k) for i in range(4)])


def after(arr, *earlier):
    return lax.optimization_barrier((arr,) + earlier)[0]


def row_major(arr):
    return with_layout_constraint(arr, Layout(major_to_minor=(0, 1)))


def exchange(arr, axis):
    return lax.all_to_all(arr, axis, split_axis=0, concat_axis=0, tiled=True)


def spread(block, axis, count):
    return exchange(jnp.tile(block, (count, 1)), axis)


def neighbours(block):
    mine = jnp.concatenate([block] + [to_x(block, k) for k in range(1, 4)], 0)
    return jnp.concatenate([mine, swap_core(mine)], 0)


def neighbours_sum(mine):
    rows = mine.shape[0] // 4
    total = mine[:rows].astype(F32)
    for k in range(1, 4):
        total = total + to_x(mine[k * rows : (k + 1) * rows], k).astype(F32)
    return total


def collect(whole, axis, count):
    return added(exchange(whole, axis), count)


def added(got, count):
    got = got.reshape(count, got.shape[0] // count, got.shape[1])
    return jnp.sum(got.astype(F32), axis=0).astype(BF)


def rope_tables(positions):
    half_dim = HD // 2
    frequency = jnp.exp(
        jnp.arange(half_dim, dtype=F32) * (-2.0 * math.log(rope_base) / HD)
    )
    angles = positions.astype(F32)[:, None] * frequency[None, :]
    cosine_tab = jnp.cos(angles)
    sine_tab = jnp.sin(angles)
    return (
        jnp.concatenate([cosine_tab, cosine_tab], -1),
        jnp.concatenate([sine_tab, sine_tab], -1),
    )


def rotate(values, cosine_tab, sine_tab):
    half_dim = values.shape[-1] // 2
    turned = jnp.concatenate([-values[..., half_dim:], values[..., :half_dim]], -1)
    return values * cosine_tab + turned * sine_tab


def unrotate(grads_in, cosine_tab, sine_tab):
    half_dim = grads_in.shape[-1] // 2
    scaled = grads_in * sine_tab
    return grads_in * cosine_tab + jnp.concatenate(
        [scaled[..., half_dim:], -scaled[..., :half_dim]], -1
    )


def product(left_arr, right_arr):
    return jnp.dot(left_arr, right_arr, preferred_element_type=F32)


def against(left_arr, right_arr):
    return lax.dot_general(
        left_arr, right_arr, (((1,), (1,)), ((), ())), preferred_element_type=F32
    )


def over_rows(left_arr, right_arr):
    return lax.dot_general(
        left_arr, right_arr, (((0,), (0,)), ((), ())), preferred_element_type=F32
    )


VMEM = pl.BlockSpec(memory_space=pltpu.VMEM)
ANY = pl.BlockSpec(memory_space=pl.ANY)
HBM = pl.BlockSpec(memory_space=pltpu.HBM)
MIB = 1 << 20


def call(body, outs, ins, out_specs, scratch=(), flops=0, moved=0, vmem=48 * MIB):
    return pl.pallas_call(
        body,
        out_shape=outs,
        in_specs=ins,
        out_specs=out_specs,
        scratch_shapes=scratch,
        compiler_params=pltpu.CompilerParams(vmem_limit_bytes=vmem),
        cost_estimate=pl.CostEstimate(flops=flops, bytes_accessed=moved, transcendentals=0),
    )


def fetch(sources, targets, sems):
    copies = [
        pltpu.make_async_copy(src, dst, sems.at[i])
        for i, (src, dst) in enumerate(zip(sources, targets))
    ]
    for one in copies:
        one.start()
    for one in copies:
        one.wait()


def hold(arr, *earlier):
    def body(*refs):
        refs[-1][...] = refs[0][...]

    out = jax.ShapeDtypeStruct(arr.shape, arr.dtype)
    size = 2 * arr.size * arr.dtype.itemsize
    return call(body, out, [VMEM] + [ANY] * len(earlier), VMEM, moved=size)(arr, *earlier)


def pack_attn_body(*refs):
    out, held, square, sems = refs[9], refs[10:19], refs[19], refs[20]
    fetch(refs[:9], held, sems)
    q_v, k_v, v_v, o_v = held[5:]
    square[...] = jnp.zeros_like(square)
    for i, vector in enumerate(held[:5]):
        square[i : i + 1, : vector.shape[1]] = vector[...].astype(F32)
    misc = square[...].T[:PAD].astype(BF)
    for t in range(8):
        h = t % 2
        rows = slice(t * PAD, t * PAD + ROWS)
        out[t * PAD : (t + 1) * PAD, :] = jnp.zeros((PAD, SIDE), BF)
        out[rows, :HALF_Q] = q_v[:, h * HALF_Q : (h + 1) * HALF_Q]
        out[rows, HALF_Q : HALF_Q + HD] = k_v[:, h * HD : (h + 1) * HD]
        out[rows, HALF_Q + HD : QKV] = v_v[:, h * HD : (h + 1) * HD]
        out[t * PAD : (t + 1) * PAD, QKV:QKVM] = misc
        out[rows, QKVM:SIDE] = o_v[:, h * HALF_Q : (h + 1) * HALF_Q]


def pack_attn(*arrays):
    out = jax.ShapeDtypeStruct((8 * PAD, SIDE), BF)
    scratch = [pltpu.VMEM(a.shape, BF) for a in arrays]
    scratch += [pltpu.VMEM((MISC, MISC), F32), pltpu.SemaphoreType.DMA((9,))]
    return call(pack_attn_body, out, [HBM] * 9, VMEM, scratch, moved=MIB, vmem=60 * MIB)(
        *arrays
    )


def pack_ff_body(gate, up, down, out, gate_v, up_v, down_v, sems):
    fetch((gate, up, down), (gate_v, up_v, down_v), sems)
    for t in range(8):
        out[t * PAD : (t + 1) * PAD, :] = jnp.zeros((PAD, FFW), BF)
        width = min(FFS, FF - t * FFS)
        for i, ref in enumerate((gate_v, up_v, down_v)):
            out[t * PAD : t * PAD + ROWS, i * FFS : i * FFS + width] = ref[
                :, t * FFS : t * FFS + width
            ]


def pack_ff(*arrays):
    out = jax.ShapeDtypeStruct((8 * PAD, FFW), BF)
    scratch = [pltpu.VMEM(a.shape, BF) for a in arrays] + [pltpu.SemaphoreType.DMA((3,))]
    return call(pack_ff_body, out, [HBM] * 3, VMEM, scratch, moved=2 * MIB)(*arrays)


def unpack_body(
    index, attn, late, q_w, k_w, v_w, gate_w, up_w,
    q, k, v, o, gate, up, down, biases, gains,
):
    x, core = index[0], index[1]

    def block(i, h, start, width):
        row = pl.multiple_of((core ^ h) * PAD, PAD)
        return late[x ^ i, pl.ds(row, PAD), start : start + width].astype(F32)[:ROWS]

    def gain_part(weight, start, grad):
        width = grad.shape[1]
        part = weight[:, start : start + width].astype(F32) * grad
        return jnp.sum(part, axis=1, keepdims=True)

    attn_gain = jnp.zeros((ROWS, 1), F32)
    for h in range(2):
        part = attn[core ^ h].astype(F32)
        biases[h : h + 1, :] = part[ROWS : ROWS + 1]
        for ref, weight, start, width in (
            (q, q_w, 0, HALF_Q),
            (k, k_w, HALF_Q, HD),
            (v, v_w, HALF_Q + HD, HD),
        ):
            piece = part[:ROWS, start : start + width]
            ref[:, h * width : (h + 1) * width] = piece
            attn_gain = attn_gain + gain_part(weight, h * width, piece)
        o[:, h * HALF_Q : (h + 1) * HALF_Q] = sum(block(i, h, FFW, HALF_Q) for i in range(4))
    mlp_gain = jnp.zeros((ROWS, 1), F32)
    for t in range(8):
        width = min(FFS, FF - t * FFS)
        for i, (ref, weight) in enumerate(((gate, gate_w), (up, up_w), (down, None))):
            piece = block(t // 2, t % 2, i * FFS, width)
            ref[:, t * FFS : t * FFS + width] = piece
            if weight is not None:
                mlp_gain = mlp_gain + gain_part(weight, t * FFS, piece)
    gains[:, 0:1] = attn_gain
    gains[:, 1:2] = mlp_gain


def unpack_grads(index, *arrays):
    shapes = [(ROWS, D), (ROWS, KVH * HD), (ROWS, KVH * HD), (ROWS, D)]
    shapes += [(ROWS, FF)] * 3 + [(2, QKV), (ROWS, 2)]
    outs = [jax.ShapeDtypeStruct(dims, F32) for dims in shapes]
    ins = [pl.BlockSpec(memory_space=pltpu.SMEM)] + [VMEM] * 7
    return call(unpack_body, outs, ins, [VMEM] * 9, moved=5 * MIB)(index, *arrays)


def turn(values, cosine, sine, back):
    low = lax.broadcasted_iota(jnp.int32, values.shape, 1) < HD // 2
    if back:
        moved = pltpu.roll(values * sine, HD // 2, 1)
        return values * cosine + jnp.where(low, moved, -moved)
    moved = pltpu.roll(values, HD // 2, 1)
    return values * cosine + jnp.where(low, -moved, moved) * sine


def project_body(normed, weights, bias, cosine, sine, query, kv, w_v, sems):
    fetch((weights.at[:, pl.ds(0, QKV)],), (w_v,), sems)
    lin = product(normed[...], w_v[...]) + bias[...]
    for s in range(2):
        rows = slice(s * 2 * BLK, (s + 1) * 2 * BLK)
        for r in range(GROUP + 1):
            head = turn(lin[rows, r * HD : (r + 1) * HD], cosine[...], sine[...], False)
            if r < GROUP:
                query[rows, r * HD : (r + 1) * HD] = head.astype(BF)
            else:
                kv[rows, :HD] = head.astype(BF)
    kv[:, HD:] = lin[:, HALF_Q + HD :].astype(BF)


def project(normed, weights, bias, cosine, sine):
    count = normed.shape[0]
    outs = [jax.ShapeDtypeStruct((count, w), BF) for w in (HALF_Q, 2 * HD)]
    scratch = [pltpu.VMEM((D, QKV), BF), pltpu.SemaphoreType.DMA((1,))]
    return call(
        project_body, outs, [VMEM, ANY] + [VMEM] * 3, [VMEM] * 2, scratch,
        flops=2 * count * D * QKV, moved=5 * MIB,
    )(normed, weights, bias, cosine, sine)


def stacked(parts, s, start):
    own = 2 * BLK
    return jnp.concatenate(
        [
            part[(2 * h + s) * own : (2 * h + s + 1) * own, start : start + HD]
            for part in parts
            for h in range(2)
        ],
        0,
    )


def positions_of(block, iota):
    return jnp.where(iota < BLK, block * BLK, (2 * N_CTX - 2 - block) * BLK) + iota


def two_heads(values, rows, r):
    return jnp.concatenate(
        [values[rows, (2 * r + i) * HD : (2 * r + i + 1) * HD] for i in range(2)], 0
    )


def attend_body(index, query, kv0, kv1, kv2, kv3, context, probs, mask, p_v, sems):
    own = 2 * BLK
    yh, x = index[0], index[1]
    here = positions_of(yh * 4 + x, lax.broadcasted_iota(jnp.int32, (own, own), 1))
    for j in range(N_CTX):
        source = ((j % 2) ^ yh) * 4 + ((j // 2) ^ x)
        there = positions_of(source, lax.broadcasted_iota(jnp.int32, (own, own), 0))
        mask[j * own : (j + 1) * own, :] = jnp.where(here >= there, 0.0, -1e30)
    parts = (kv0, kv1, kv2, kv3)
    copies = []
    for s in range(2):
        keys = stacked(parts, s, 0)
        values = stacked(parts, s, HD).T
        rows = slice(s * own, (s + 1) * own)
        for r in range(GROUP):
            pair, side = s * PAIRS + r // 2, slice(r % 2 * own, (r % 2 + 1) * own)
            scores = against(keys, query[rows, r * HD : (r + 1) * HD])
            scores = scores * (1.0 / math.sqrt(HD)) + mask[...]
            terms = jnp.exp(scores - jnp.max(scores, axis=0, keepdims=True))
            p = terms / jnp.sum(terms, axis=0, keepdims=True)
            p_v[pair, :, side] = p
            if r % 2 == 1:
                one = pltpu.make_async_copy(p_v.at[pair], probs.at[pair], sems.at[pair])
                one.start()
                copies.append(one)
            context[rows, r * HD : (r + 1) * HD] = product(values, p.astype(BF)).T.astype(BF)
    for one in copies:
        one.wait()


def attend(index, query, parts):
    heads, keys, own = 2 * PAIRS, 2 * N_CTX * BLK, 4 * BLK
    outs = [
        jax.ShapeDtypeStruct(query.shape, BF),
        jax.ShapeDtypeStruct((heads, keys, own), F32),
    ]
    scratch = [
        pltpu.VMEM((keys, own // 2), F32),
        pltpu.VMEM((heads, keys, own), F32),
        pltpu.SemaphoreType.DMA((heads,)),
    ]
    return call(
        attend_body, outs, [pl.BlockSpec(memory_space=pltpu.SMEM)] + [VMEM] * 5, [VMEM, ANY],
        scratch, flops=4 * heads * keys * own * HD, moved=8 * MIB,
    )(index, query, *parts)


def attend_back_body(
    branch, weights, query, kv0, kv1, kv2, kv3, probs, cosine, sine,
    grad_query, out0, out1, out2, out3, w_v, p_v, sems,
):
    own, heads = 2 * BLK, 2 * PAIRS
    scale = 1.0 / math.sqrt(HD)
    weight = pltpu.make_async_copy(weights.at[:, pl.ds(QKVM, HALF_Q)], w_v, sems.at[heads])
    weight.start()
    loads = [
        pltpu.make_async_copy(probs.at[i], p_v.at[i], sems.at[i]) for i in range(heads)
    ]
    for one in loads:
        one.start()
    weight.wait()
    grad_context = product(branch[...], w_v[...]).astype(BF)
    parts, outs = (kv0, kv1, kv2, kv3), (out0, out1, out2, out3)
    for s in range(2):
        keys = stacked(parts, s, 0).T
        values = stacked(parts, s, HD)
        rows = slice(s * own, (s + 1) * own)
        grad_key = jnp.zeros((2 * N_CTX * BLK, HD), F32)
        grad_value = jnp.zeros((2 * N_CTX * BLK, HD), F32)
        for r in range(PAIRS):
            loads[s * PAIRS + r].wait()
            p = p_v[s * PAIRS + r]
            grad = two_heads(grad_context, rows, r)
            grad_p = against(values, grad)
            delta = jnp.sum(p * grad_p, axis=0, keepdims=True)
            grad_s = (p * (grad_p - delta)).astype(BF)
            back = product(keys, grad_s).T * scale
            for i in range(2):
                columns = slice((2 * r + i) * HD, (2 * r + i + 1) * HD)
                head = turn(back[i * own : (i + 1) * own], cosine[...], sine[...], True)
                grad_query[rows, columns] = head.astype(BF)
            grad_key = grad_key + product(grad_s, two_heads(query, rows, r))
            grad_value = grad_value + product(p.astype(BF), grad)
        for k, out in enumerate(outs):
            for h in range(2):
                to = slice((2 * h + s) * own, (2 * h + s + 1) * own)
                at = slice((2 * k + h) * own, (2 * k + h + 1) * own)
                out[to, :HD] = (grad_key[at] * scale).astype(BF)
                out[to, HD:] = grad_value[at].astype(BF)


def attend_back(branch, weights, query, parts, probs, cosine, sine):
    heads, keys, own = probs.shape
    outs = [jax.ShapeDtypeStruct(query.shape, BF)]
    outs += [jax.ShapeDtypeStruct(p.shape, BF) for p in parts]
    scratch = [
        pltpu.VMEM((D, HALF_Q), BF),
        pltpu.VMEM(probs.shape, F32),
        pltpu.SemaphoreType.DMA((heads + 1,)),
    ]
    return call(
        attend_back_body, outs, [VMEM, ANY] + [VMEM] * 5 + [ANY] + [VMEM] * 2, [VMEM] * 5,
        scratch, flops=10 * heads * keys * own * HD, moved=12 * MIB,
    )(branch, weights, query, *parts, probs, cosine, sine)


def weight_terms_body(rows, grads, inner, mixed, *refs):
    out = refs[-1]
    wide = inner.shape[1]
    out[:, :wide] = product(rows[...].T, inner[...]).astype(BF)
    out[:, wide : wide + mixed.shape[1]] = product(grads[...].T, mixed[...]).astype(BF)


def weight_terms(rows, grads, inner, mixed, width, *earlier):
    count = rows.shape[0]
    tile = 256
    column = pl.BlockSpec((count, tile), lambda i: (0, i))
    whole = [pl.BlockSpec(a.shape, lambda i: (0, 0)) for a in (inner, mixed)]
    return pl.pallas_call(
        weight_terms_body,
        grid=(D // tile,),
        out_shape=jax.ShapeDtypeStruct((D, width), BF),
        in_specs=[column, column] + whole + [ANY] * len(earlier),
        out_specs=pl.BlockSpec((tile, width), lambda i: (i, 0)),
        compiler_params=pltpu.CompilerParams(vmem_limit_bytes=48 * MIB),
        cost_estimate=pl.CostEstimate(
            flops=2 * count * D * FFW, bytes_accessed=26 * MIB, transcendentals=0
        ),
    )(rows, grads, inner, mixed, *earlier)


def fill_body(buffer, branch, context, out, part, sems):
    part[...] = product(branch[...].T, context[...]).astype(BF)
    fetch((part,), (out.at[:, pl.ds(FFW, HALF_Q)],), sems)


def fill(buffer, branch, context):
    return pl.pallas_call(
        fill_body,
        out_shape=jax.ShapeDtypeStruct(buffer.shape, BF),
        in_specs=[ANY, VMEM, VMEM],
        out_specs=ANY,
        scratch_shapes=[pltpu.VMEM((D, HALF_Q), BF), pltpu.SemaphoreType.DMA((1,))],
        input_output_aliases={0: 0},
        compiler_params=pltpu.CompilerParams(vmem_limit_bytes=48 * MIB),
        cost_estimate=pl.CostEstimate(
            flops=4 * BLK * 2 * D * HALF_Q, bytes_accessed=4 * MIB, transcendentals=0
        ),
    )(buffer, branch, context)


def plane_sum_body(index, got, *refs):
    keep, give = refs[-2:]
    parts = sum(got[i].astype(F32) for i in range(16)).astype(BF)
    first = index[0] == 0
    keep[...] = jnp.where(first, parts[0], parts[1])
    give[...] = jnp.where(first, parts[1], parts[0])


def plane_sum(index, got, *earlier):
    outs = [jax.ShapeDtypeStruct(got.shape[2:], BF)] * 2
    ins = [pl.BlockSpec(memory_space=pltpu.SMEM), VMEM] + [ANY] * len(earlier)
    return call(plane_sum_body, outs, ins, [VMEM] * 2, moved=2 * MIB)(index, got, *earlier)


def down_body(mixed, weights, *refs):
    mine, others, w_v, sems = refs[-4:]
    fetch((weights.at[:, pl.ds(2 * FFS, FFS)],), (w_v,), sems)
    tile = 256
    half = mine.shape[0]
    for base, out in ((half, others), (0, mine)):

        @pl.loop(0, half // tile)
        def _(i):
            at = pl.ds(pl.multiple_of(base + i * tile, tile), tile)
            to = pl.ds(pl.multiple_of(i * tile, tile), tile)
            out[to, :] = against(mixed[at, :], w_v[...]).astype(BF)


def down(mixed, weights, *earlier):
    half = mixed.shape[0] // 2
    outs = [jax.ShapeDtypeStruct((half, D), BF)] * 2
    scratch = [pltpu.VMEM((D, FFS), BF), pltpu.SemaphoreType.DMA((1,))]
    return call(
        down_body, outs, [VMEM, ANY] + [ANY] * len(earlier), [VMEM] * 2, scratch,
        flops=4 * half * D * FFS, moved=9 * MIB,
    )(mixed, weights, *earlier)


def ffn_body(
    rows, grads, weights, mixed, inner, back, back_others,
    rows_v, grads_v, gate_v, up_v, down_v, g_v, sems,
):
    half = rows.shape[0] // 2
    pairs = [
        (rows, rows_v),
        (weights.at[:, pl.ds(0, FFS)], gate_v),
        (weights.at[:, pl.ds(FFS, FFS)], up_v),
        (grads, grads_v),
        (weights.at[:, pl.ds(2 * FFS, FFS)], down_v),
    ]
    loads = [
        pltpu.make_async_copy(src, dst, sems.at[i]) for i, (src, dst) in enumerate(pairs)
    ]
    for one in loads:
        one.start()
    tile = 512
    steps = half // tile
    for one in loads[:2]:
        one.wait()

    @pl.loop(0, 2 * steps)
    def _(i):
        at = pl.ds(pl.multiple_of(i * tile, tile), tile)
        g_v[at, :] = product(rows_v[at, :], gate_v[...])

    for one in loads[2:]:
        one.wait()

    for base, out in ((half, back_others), (0, back)):

        @pl.loop(0, steps)
        def _(i):
            at = pl.ds(pl.multiple_of(base + i * tile, tile), tile)
            grad_mixed = product(grads_v[at, :], down_v[...])
            gate_val = g_v[at, :]
            up_val = product(rows_v[at, :], up_v[...])
            gate_sig = jax.nn.sigmoid(gate_val)
            swish = gate_val * gate_sig
            mixed[at, :] = (swish * up_val).astype(BF)
            grad_up = (grad_mixed * swish).astype(BF)
            grad_gate = (
                grad_mixed * up_val * gate_sig * (1.0 + gate_val * (1.0 - gate_sig))
            ).astype(BF)
            inner[at, :FFS] = grad_gate
            inner[at, FFS:] = grad_up
            to = pl.ds(pl.multiple_of(i * tile, tile), tile)
            out[to, :] = (
                against(grad_gate, gate_v[...]) + against(grad_up, up_v[...])
            ).astype(BF)


def ffn(rows, grads, weights):
    count = rows.shape[0]
    half = count // 2
    dims = [(count, FFS), (count, 2 * FFS), (half, D), (half, D)]
    outs = [jax.ShapeDtypeStruct(d, BF) for d in dims]
    scratch = [pltpu.VMEM((count, D), BF)] * 2 + [pltpu.VMEM((D, FFS), BF)] * 3
    scratch += [pltpu.VMEM((count, FFS), F32), pltpu.SemaphoreType.DMA((5,))]
    return call(
        ffn_body, outs, [ANY] * 3, [VMEM] * 4, scratch,
        flops=10 * count * D * FFS, moved=28 * MIB, vmem=56 * MIB,
    )(rows, grads, weights)


def per_device(
    tokens,
    cotangent,
    attn_gain,
    q_weight,
    q_bias,
    k_weight,
    k_bias,
    v_weight,
    v_bias,
    o_weight,
    mlp_gain,
    gate_weight,
    up_weight,
    down_weight,
):
    yh, x, z, yl, core = [lax.axis_index(a) for a in AXES]
    y = yh * 2 + yl
    ctx_rank = yh * 4 + x
    own = 2 * BLK
    both = 2 * own
    is_zero = core == 0

    place = jnp.arange(D, dtype=jnp.int32)
    place_r = place % ROWS
    place_x = place // ROWS % 4
    place_c = place // (ROWS * 4) % 2
    place_y = place // (ROWS * 8) % 4
    place_z = place // (ROWS * 32)
    place_dev = (((place_y // 2 * 4 + place_x) * 4 + place_z) * 2 + place_y % 2) * 2 + place_c
    natural = place_dev * ROWS + place_r
    to_order = (place[:, None] == natural[None, :]).astype(BF)

    tokens_flat = tokens.reshape(own, D)
    tokens_both = jnp.concatenate([tokens_flat, swap_core(tokens_flat)], 0)

    vectors = [arr[None] for arr in (attn_gain, mlp_gain, q_bias, k_bias, v_bias)]
    got = exchange(pack_attn(*vectors, q_weight, k_weight, v_weight, o_weight), TP)
    got_ff = after(pack_ff(gate_weight, up_weight, down_weight), got)
    got_ff = exchange(got_ff, TP)
    grad_low = product(cotangent.reshape(own, D), to_order).astype(BF)
    want = jnp.arange(8 * ROWS, dtype=jnp.int32)
    at = (want // ROWS % 4 * 2 + want // (4 * ROWS)) * PAD + want % ROWS
    pick = (at[:, None] == jnp.arange(8 * PAD, dtype=jnp.int32)[None, :]).astype(BF)
    rows_attn = product(pick, got).astype(BF)
    rows_ff = product(pick, got_ff).astype(BF)

    plane = ("z",) + Y
    grad_rows = neighbours(after(grad_low, rows_attn))
    attn_all = lax.all_gather(rows_attn, plane, axis=0, tiled=True)
    ff_all = lax.all_gather(rows_ff, plane, axis=0, tiled=True)
    attn_all = after(attn_all, grad_rows)
    weight_qkv = attn_all[:, :QKV]
    weight_o = attn_all[:, QKVM:]

    eight = (jnp.arange(8)[:, None] == jnp.arange(MISC)[None, :]).astype(BF)
    misc_rows = against(eight, attn_all[:, QKV:QKVM])
    gain_one = misc_rows[0:1]
    gain_two = misc_rows[1:2]
    bias_rows = misc_rows.astype(BF)
    bias_q = against(bias_rows[2:3], to_order)
    small = jnp.arange(KVH * HD, dtype=jnp.int32)
    to_small = (
        ((place_dev * 2 + place_r)[:, None] == small[None, :]) & (place_r < 2)[:, None]
    ).astype(BF)
    bias_kv = product(bias_rows[3:5], to_small)

    def side_of(row, width):
        return jnp.where(is_zero, row[:, :width], row[:, width:])

    bias_qkv = jnp.concatenate(
        [
            side_of(bias_q, HALF_Q),
            side_of(bias_kv[0:1], HD),
            side_of(bias_kv[1:2], HD),
        ],
        1,
    )

    offsets = jnp.arange(BLK, dtype=jnp.int32)
    query_pos = jnp.concatenate(
        [ctx_rank * BLK + offsets, (2 * N_CTX - 1 - ctx_rank) * BLK + offsets]
    )
    cosine_tab, sine_tab = rope_tables(query_pos)
    cosine_b = jnp.concatenate([cosine_tab, cosine_tab], 0)
    sine_b = jnp.concatenate([sine_tab, sine_tab], 0)

    inputs = product(tokens_both, to_order)
    scale_one = lax.rsqrt(jnp.mean(inputs * inputs, axis=-1, keepdims=True) + epsilon)
    unit_one = inputs * scale_one
    normed_one = (unit_one * gain_one).astype(BF)
    query_rot, kv_send = project(normed_one, attn_all, bias_qkv, cosine_tab, sine_tab)
    kv_parts = jnp.concatenate([kv_send, swap_yh(kv_send)], 0)
    kv_parts = [kv_parts] + [to_x(kv_parts, k) for k in range(1, 4)]
    slot = jnp.arange(4 * XCOLS, dtype=jnp.int32)
    slot_p = slot % XCOLS
    slot_zy = slot_p // (2 * ROWS)
    slot_dev = (slot_zy % 4 // 2 * 4 + slot // XCOLS) * 4 + slot_zy // 4
    slot_dev = (slot_dev * 2 + slot_zy % 2) * 2 + slot_p // ROWS % 2
    slot_at = jnp.where(slot_p < D // 4, slot_dev * ROWS + slot_p % ROWS, -1)
    by_x = (natural[:, None] == slot_at[None, :]).astype(BF)
    normed_x = jnp.where(
        (slot_p == D // 4)[None, :], 1.0, product(normed_one, by_x)
    ).astype(BF)
    query_rot = after(query_rot, normed_x)
    context_low, probs = attend(jnp.stack([yh, x]), query_rot, kv_parts)
    branch = against(context_low, weight_o)
    hidden_one = (
        inputs[:own] + branch[:own] + swap_core(branch[own:].astype(BF)).astype(F32)
    )
    scale_two = lax.rsqrt(jnp.mean(hidden_one * hidden_one, axis=-1, keepdims=True) + epsilon)
    unit_two = hidden_one * scale_two
    normed_two = (unit_two * gain_two).astype(BF)

    normed_rows = neighbours(normed_two)
    mixed_low, grad_inner, *grad_norm_part = ffn(
        normed_rows, grad_rows, ff_all
    )
    grad_norm_mine = add_low(grad_norm_part[0], swap_core(grad_norm_part[1]))
    grad_norm_two = neighbours_sum(grad_norm_mine)
    ff_buffer = weight_terms(
        normed_rows, grad_rows, grad_inner, mixed_low, FFW + HALF_Q, grad_norm_mine
    )
    grad_norm_two = after(grad_norm_two, ff_buffer)

    grad_unit_two = grad_norm_two * gain_two
    grad_hidden = grad_low.astype(F32) + scale_two * (
        grad_unit_two - unit_two * jnp.mean(grad_unit_two * unit_two, axis=-1, keepdims=True)
    )
    grad_branch = grad_hidden.astype(BF)
    grad_branch = jnp.concatenate([grad_branch, swap_core(grad_branch)], 0)
    late_grads = fill(ff_buffer, grad_branch, context_low)
    late_sum = lax.psum_scatter(late_grads, plane, scatter_dimension=0, tiled=True)
    branch_ready = hold(grad_branch, late_grads)
    grad_query, *kv_grads = attend_back(
        branch_ready, attn_all, query_rot, kv_parts, probs, cosine_tab, sine_tab
    )
    kv_grads = [kv_grads[0]] + [to_x(kv_grads[k], k) for k in range(1, 4)]
    q_grads = row_major(over_rows(normed_x, hold(grad_query, *kv_grads[1:])).astype(BF))
    q_got = exchange(q_grads, "x")
    grad_kv = sum(part.astype(F32) for part in kv_grads)
    grad_kv = grad_kv[:both] + swap_yh(grad_kv[both:].astype(BF)).astype(F32)
    grad_key = unrotate(grad_kv[:, :HD], cosine_b, sine_b)
    grad_kv = jnp.concatenate([grad_key, grad_kv[:, HD:]], 1).astype(BF)
    down_mine, down_others = down(mixed_low, ff_all, q_grads)
    grad_kv = hold(grad_kv, down_mine)
    kv_grads = row_major(over_rows(normed_x, grad_kv).astype(BF))
    kv_pieces = [
        lax.dynamic_slice_in_dim(kv_grads, (x ^ k) * XCOLS, XCOLS, 0) for k in range(4)
    ]
    kv_pieces = [kv_pieces[0]] + [to_x(kv_pieces[k], k) for k in range(1, 4)]
    kv_sum = sum(part.astype(F32) for part in kv_pieces).astype(BF)
    down_both = add_low(down_mine, swap_core(down_others)).reshape(4, own, D)
    down_both = jnp.concatenate(
        [lax.dynamic_index_in_dim(down_both, k ^ x, 0, False) for k in range(4)], 0
    )
    down_terms = lax.psum_scatter(down_both, "x", scatter_dimension=0, tiled=True)
    layer_sum = (hidden_one + down_terms.astype(F32)).astype(BF)
    layer_out = against(layer_sum, to_order).astype(BF).reshape(tokens.shape)
    grad_lin = hold(jnp.concatenate([grad_query, grad_kv], 1), kv_grads)
    grad_norm_one = against(grad_lin, weight_qkv)
    grad_norm_one = grad_norm_one[:own] + swap_core(grad_norm_one[own:].astype(BF)).astype(F32)
    unit_own = unit_one[:own]
    grad_unit_one = grad_norm_one * gain_one
    input_grad = grad_hidden + scale_one[:own] * (
        grad_unit_one - unit_own * jnp.mean(grad_unit_one * unit_own, axis=-1, keepdims=True)
    )
    input_high = input_grad.astype(BF)
    input_rest = (input_grad - input_high.astype(F32)).astype(BF)
    input_grad = (against(input_high, to_order) + against(input_rest, to_order)).reshape(
        tokens.shape
    )

    qkv_sum = jnp.concatenate([added(q_got, 4), kv_sum], 1)
    spot = jnp.arange(16 * 2 * PAD, dtype=jnp.int32)
    spot_r = spot % PAD
    spot_at = spot // PAD * ROWS + spot_r
    spot_at = jnp.where(spot_r < ROWS, spot_at, jnp.where(spot_r == ROWS, D // 4, -1))
    room = (spot_at[:, None] == jnp.arange(XCOLS, dtype=jnp.int32)[None, :]).astype(BF)
    qkv_rows = product(room, qkv_sum).astype(BF)

    spot = jnp.arange(8 * PAD, dtype=jnp.int32)
    spot_at = ((spot // (4 * PAD)) ^ core) * 4 + ((spot // PAD % 4) ^ x)
    spot_at = jnp.where(spot % PAD < ROWS, spot_at * ROWS + spot % PAD, -1)
    late_pick = (want[:, None] == spot_at[None, :]).astype(BF)
    late = over_rows(late_pick, hold(late_sum, qkv_rows)).astype(BF)
    late_pair = [late[: 4 * PAD], swap_core(late[4 * PAD :])]
    late_pair = [part.reshape(4, PAD, FFW + HALF_Q) for part in late_pair]
    late = jnp.concatenate(late_pair, 1)
    late = [late[0]] + [to_x(late[k], k) for k in range(1, 4)]
    qkv_sum = exchange(qkv_rows, plane)
    qkv_keep, qkv_give = plane_sum(core[None], qkv_sum.reshape(16, 2, PAD, QKV), *late[1:])
    qkv_sum = jnp.stack([qkv_keep, swap_core(qkv_give)])
    (
        q_weight_grad,
        k_weight_grad,
        v_weight_grad,
        o_weight_grad,
        gate_weight_grad,
        up_weight_grad,
        down_weight_grad,
        bias_sum,
        gain_sum,
    ) = unpack_grads(
        jnp.stack([x, core]), qkv_sum, jnp.stack(late),
        q_weight, k_weight, v_weight, gate_weight, up_weight,
    )
    attn_gain_grad = gain_sum[:, 0] / attn_gain.astype(F32)
    mlp_gain_grad = gain_sum[:, 1] / mlp_gain.astype(F32)
    device = ctx_rank * 16 + z * 4 + yl * 2 + core
    q_bias_grad = lax.dynamic_slice_in_dim(
        bias_sum[:, :HALF_Q].reshape(D), device * ROWS, ROWS, 0
    )
    k_bias_grad = bias_sum[:, HALF_Q : HALF_Q + HD].reshape(KVH * HD)
    v_bias_grad = lax.dynamic_slice_in_dim(
        bias_sum[:, HALF_Q + HD :].reshape(KVH * HD), device * 2, 2, 0
    )
    return (
        layer_out,
        input_grad,
        attn_gain_grad,
        q_weight_grad,
        q_bias_grad,
        k_weight_grad,
        k_bias_grad,
        v_weight_grad,
        v_bias_grad,
        o_weight_grad,
        mlp_gain_grad,
        gate_weight_grad,
        up_weight_grad,
        down_weight_grad,
    )


def solution(mesh):
    fine = Mesh(mesh.devices.reshape(2, 4, 4, 2, 2), AXES)
    acts = P(("z", "yl", "core"), None, CTX, None)
    vec, mat = P(AXES), P(AXES, None)
    return jax.shard_map(
        per_device,
        mesh=fine,
        in_specs=(acts, acts, vec, mat, vec, mat, vec, mat, vec, mat, vec, mat, mat, mat),
        out_specs=(acts, acts, vec, mat, vec, mat, P(), mat, vec, mat, vec, mat, mat, mat),
        check_vma=False,
    )
```

```python
import math

import jax
import jax.numpy as jnp
from jax import lax
from jax.experimental import pallas as pl
from jax.experimental.layout import Layout, with_layout_constraint
from jax.experimental.pallas import tpu as pltpu
from jax.sharding import Mesh, PartitionSpec as P

H = 12
KVH = 2
HD = 128
GROUP = H // KVH
D = 1536
FF = 8960
BLK = 64
N_CTX = 8
ROWS = 12
PAD = 16
FFS = 1152
HALF_Q = GROUP * HD
QKV = HALF_Q + 2 * HD
MISC = 128
PAIRS = GROUP // 2
QKVM = QKV + MISC
FFW = 3 * FFS
XCOLS = D // 4 + PAD
SIDE = QKVM + HALF_Q

epsilon = 1e-06
rope_base = 1000000.0

AXES = ("yh", "x", "z", "yl", "core")
Y = ("yh", "yl")
CTX = ("yh", "x")
TP = ("x", "core")
F32 = jnp.float32
BF = jnp.bfloat16


def add_low(left, right):
    return (left.astype(F32) + right.astype(F32)).astype(BF)


def swap_core(arr):
    return lax.ppermute(arr, "core", [(0, 1), (1, 0)])


def swap_yh(arr):
    return lax.ppermute(arr, "yh", [(0, 1), (1, 0)])


def to_x(arr, k):
    return lax.ppermute(arr, "x", [(i, i ^ k) for i in range(4)])


def after(arr, *earlier):
    return lax.optimization_barrier((arr,) + earlier)[0]


def row_major(arr):
    return with_layout_constraint(arr, Layout(major_to_minor=(0, 1)))


def exchange(arr, axis):
    return lax.all_to_all(arr, axis, split_axis=0, concat_axis=0, tiled=True)


def spread(block, axis, count):
    return exchange(jnp.tile(block, (count, 1)), axis)


def neighbours(block):
    mine = jnp.concatenate([block] + [to_x(block, k) for k in range(1, 4)], 0)
    return jnp.concatenate([mine, swap_core(mine)], 0)


def neighbours_sum(mine):
    rows = mine.shape[0] // 4
    total = mine[:rows].astype(F32)
    for k in range(1, 4):
        total = total + to_x(mine[k * rows : (k + 1) * rows], k).astype(F32)
    return total


def collect(whole, axis, count):
    return added(exchange(whole, axis), count)


def added(got, count):
    got = got.reshape(count, got.shape[0] // count, got.shape[1])
    return jnp.sum(got.astype(F32), axis=0).astype(BF)


def rope_tables(positions):
    half_dim = HD // 2
    frequency = jnp.exp(
        jnp.arange(half_dim, dtype=F32) * (-2.0 * math.log(rope_base) / HD)
    )
    angles = positions.astype(F32)[:, None] * frequency[None, :]
    cosine_tab = jnp.cos(angles)
    sine_tab = jnp.sin(angles)
    return (
        jnp.concatenate([cosine_tab, cosine_tab], -1),
        jnp.concatenate([sine_tab, sine_tab], -1),
    )


def rotate(values, cosine_tab, sine_tab):
    half_dim = values.shape[-1] // 2
    turned = jnp.concatenate([-values[..., half_dim:], values[..., :half_dim]], -1)
    return values * cosine_tab + turned * sine_tab


def unrotate(grads_in, cosine_tab, sine_tab):
    half_dim = grads_in.shape[-1] // 2
    scaled = grads_in * sine_tab
    return grads_in * cosine_tab + jnp.concatenate(
        [scaled[..., half_dim:], -scaled[..., :half_dim]], -1
    )


def product(left_arr, right_arr):
    return jnp.dot(left_arr, right_arr, preferred_element_type=F32)


def against(left_arr, right_arr):
    return lax.dot_general(
        left_arr, right_arr, (((1,), (1,)), ((), ())), preferred_element_type=F32
    )


def over_rows(left_arr, right_arr):
    return lax.dot_general(
        left_arr, right_arr, (((0,), (0,)), ((), ())), preferred_element_type=F32
    )


VMEM = pl.BlockSpec(memory_space=pltpu.VMEM)
ANY = pl.BlockSpec(memory_space=pl.ANY)
HBM = pl.BlockSpec(memory_space=pltpu.HBM)
MIB = 1 << 20


def call(body, outs, ins, out_specs, scratch=(), flops=0, moved=0, vmem=48 * MIB):
    return pl.pallas_call(
        body,
        out_shape=outs,
        in_specs=ins,
        out_specs=out_specs,
        scratch_shapes=scratch,
        compiler_params=pltpu.CompilerParams(vmem_limit_bytes=vmem),
        cost_estimate=pl.CostEstimate(flops=flops, bytes_accessed=moved, transcendentals=0),
    )


def fetch(sources, targets, sems):
    copies = [
        pltpu.make_async_copy(src, dst, sems.at[i])
        for i, (src, dst) in enumerate(zip(sources, targets))
    ]
    for one in copies:
        one.start()
    for one in copies:
        one.wait()


def hold(arr, *earlier):
    def body(*refs):
        refs[-1][...] = refs[0][...]

    out = jax.ShapeDtypeStruct(arr.shape, arr.dtype)
    size = 2 * arr.size * arr.dtype.itemsize
    return call(body, out, [VMEM] + [ANY] * len(earlier), VMEM, moved=size)(arr, *earlier)


def pack_attn_body(*refs):
    out, held, square, sems = refs[9], refs[10:19], refs[19], refs[20]
    fetch(refs[:9], held, sems)
    q_v, k_v, v_v, o_v = held[5:]
    square[...] = jnp.zeros_like(square)
    for i, vector in enumerate(held[:5]):
        square[i : i + 1, : vector.shape[1]] = vector[...].astype(F32)
    misc = square[...].T[:PAD].astype(BF)
    for t in range(8):
        h = t % 2
        rows = slice(t * PAD, t * PAD + ROWS)
        out[t * PAD : (t + 1) * PAD, :] = jnp.zeros((PAD, SIDE), BF)
        out[rows, :HALF_Q] = q_v[:, h * HALF_Q : (h + 1) * HALF_Q]
        out[rows, HALF_Q : HALF_Q + HD] = k_v[:, h * HD : (h + 1) * HD]
        out[rows, HALF_Q + HD : QKV] = v_v[:, h * HD : (h + 1) * HD]
        out[t * PAD : (t + 1) * PAD, QKV:QKVM] = misc
        out[rows, QKVM:SIDE] = o_v[:, h * HALF_Q : (h + 1) * HALF_Q]


def pack_attn(*arrays):
    out = jax.ShapeDtypeStruct((8 * PAD, SIDE), BF)
    scratch = [pltpu.VMEM(a.shape, BF) for a in arrays]
    scratch += [pltpu.VMEM((MISC, MISC), F32), pltpu.SemaphoreType.DMA((9,))]
    return call(pack_attn_body, out, [HBM] * 9, VMEM, scratch, moved=MIB, vmem=60 * MIB)(
        *arrays
    )


def pack_ff_body(gate, up, down, out, gate_v, up_v, down_v, sems):
    fetch((gate, up, down), (gate_v, up_v, down_v), sems)
    for t in range(8):
        out[t * PAD : (t + 1) * PAD, :] = jnp.zeros((PAD, FFW), BF)
        width = min(FFS, FF - t * FFS)
        for i, ref in enumerate((gate_v, up_v, down_v)):
            out[t * PAD : t * PAD + ROWS, i * FFS : i * FFS + width] = ref[
                :, t * FFS : t * FFS + width
            ]


def pack_ff(*arrays):
    out = jax.ShapeDtypeStruct((8 * PAD, FFW), BF)
    scratch = [pltpu.VMEM(a.shape, BF) for a in arrays] + [pltpu.SemaphoreType.DMA((3,))]
    return call(pack_ff_body, out, [HBM] * 3, VMEM, scratch, moved=2 * MIB)(*arrays)


def unpack_body(
    index, attn, late0, late1, late2, late3, q_w, k_w, v_w, gate_w, up_w,
    q, k, v, o, gate, up, down, biases, gains, late,
):
    x, core = index[0], index[1]
    for i, part in enumerate((late0, late1, late2, late3)):
        late[i] = part[...]

    def block(i, h, start, width):
        row = pl.multiple_of((core ^ h) * PAD, PAD)
        return late[x ^ i, pl.ds(row, PAD), start : start + width].astype(F32)[:ROWS]

    def gain_part(weight, start, grad):
        width = grad.shape[1]
        part = weight[:, start : start + width].astype(F32) * grad
        return jnp.sum(part, axis=1, keepdims=True)

    attn_gain = jnp.zeros((ROWS, 1), F32)
    for h in range(2):
        part = attn[core ^ h].astype(F32)
        biases[h : h + 1, :] = part[ROWS : ROWS + 1]
        for ref, weight, start, width in (
            (q, q_w, 0, HALF_Q),
            (k, k_w, HALF_Q, HD),
            (v, v_w, HALF_Q + HD, HD),
        ):
            piece = part[:ROWS, start : start + width]
            ref[:, h * width : (h + 1) * width] = piece
            attn_gain = attn_gain + gain_part(weight, h * width, piece)
        o[:, h * HALF_Q : (h + 1) * HALF_Q] = sum(block(i, h, FFW, HALF_Q) for i in range(4))
    mlp_gain = jnp.zeros((ROWS, 1), F32)
    for t in range(8):
        width = min(FFS, FF - t * FFS)
        for i, (ref, weight) in enumerate(((gate, gate_w), (up, up_w), (down, None))):
            piece = block(t // 2, t % 2, i * FFS, width)
            ref[:, t * FFS : t * FFS + width] = piece
            if weight is not None:
                mlp_gain = mlp_gain + gain_part(weight, t * FFS, piece)
    gains[:, 0:1] = attn_gain
    gains[:, 1:2] = mlp_gain


def unpack_grads(index, *arrays):
    shapes = [(ROWS, D), (ROWS, KVH * HD), (ROWS, KVH * HD), (ROWS, D)]
    shapes += [(ROWS, FF)] * 3 + [(2, QKV), (ROWS, 2)]
    outs = [jax.ShapeDtypeStruct(dims, F32) for dims in shapes]
    ins = [pl.BlockSpec(memory_space=pltpu.SMEM)] + [VMEM] * 10
    scratch = [pltpu.VMEM((4,) + arrays[1].shape, BF)]
    return call(unpack_body, outs, ins, [VMEM] * 9, scratch, moved=5 * MIB)(index, *arrays)


def turn(values, cosine, sine, back):
    low = lax.broadcasted_iota(jnp.int32, values.shape, 1) < HD // 2
    if back:
        moved = pltpu.roll(values * sine, HD // 2, 1)
        return values * cosine + jnp.where(low, moved, -moved)
    moved = pltpu.roll(values, HD // 2, 1)
    return values * cosine + jnp.where(low, -moved, moved) * sine


def project_body(normed, weights, bias, cosine, sine, query, kv, w_v, sems):
    fetch((weights.at[:, pl.ds(0, QKV)],), (w_v,), sems)
    lin = product(normed[...], w_v[...]) + bias[...]
    for s in range(2):
        rows = slice(s * 2 * BLK, (s + 1) * 2 * BLK)
        for r in range(GROUP + 1):
            head = turn(lin[rows, r * HD : (r + 1) * HD], cosine[...], sine[...], False)
            if r < GROUP:
                query[rows, r * HD : (r + 1) * HD] = head.astype(BF)
            else:
                kv[rows, :HD] = head.astype(BF)
    kv[:, HD:] = lin[:, HALF_Q + HD :].astype(BF)


def project(normed, weights, bias, cosine, sine):
    count = normed.shape[0]
    outs = [jax.ShapeDtypeStruct((count, w), BF) for w in (HALF_Q, 2 * HD)]
    scratch = [pltpu.VMEM((D, QKV), BF), pltpu.SemaphoreType.DMA((1,))]
    return call(
        project_body, outs, [VMEM, ANY] + [VMEM] * 3, [VMEM] * 2, scratch,
        flops=2 * count * D * QKV, moved=5 * MIB,
    )(normed, weights, bias, cosine, sine)


def stacked(parts, s, start):
    own = 2 * BLK
    return jnp.concatenate(
        [
            part[(2 * h + s) * own : (2 * h + s + 1) * own, start : start + HD]
            for part in parts
            for h in range(2)
        ],
        0,
    )


def positions_of(block, iota):
    return jnp.where(iota < BLK, block * BLK, (2 * N_CTX - 2 - block) * BLK) + iota


def two_heads(values, rows, r):
    return jnp.concatenate(
        [values[rows, (2 * r + i) * HD : (2 * r + i + 1) * HD] for i in range(2)], 0
    )


def attend_body(index, query, kv0, kv1, kv2, kv3, context, probs, mask, p_v, sems):
    own = 2 * BLK
    yh, x = index[0], index[1]
    here = positions_of(yh * 4 + x, lax.broadcasted_iota(jnp.int32, (own, own), 1))
    for j in range(N_CTX):
        source = ((j % 2) ^ yh) * 4 + ((j // 2) ^ x)
        there = positions_of(source, lax.broadcasted_iota(jnp.int32, (own, own), 0))
        mask[j * own : (j + 1) * own, :] = jnp.where(here >= there, 0.0, -1e30)
    parts = (kv0, kv1, kv2, kv3)
    copies = []
    for s in range(2):
        keys = stacked(parts, s, 0)
        values = stacked(parts, s, HD).T
        rows = slice(s * own, (s + 1) * own)
        for r in range(GROUP):
            pair, side = s * PAIRS + r // 2, slice(r % 2 * own, (r % 2 + 1) * own)
            scores = against(keys, query[rows, r * HD : (r + 1) * HD])
            scores = scores * (1.0 / math.sqrt(HD)) + mask[...]
            terms = jnp.exp(scores - jnp.max(scores, axis=0, keepdims=True))
            p = terms / jnp.sum(terms, axis=0, keepdims=True)
            p_v[pair, :, side] = p
            if r % 2 == 1:
                one = pltpu.make_async_copy(p_v.at[pair], probs.at[pair], sems.at[pair])
                one.start()
                copies.append(one)
            context[rows, r * HD : (r + 1) * HD] = product(values, p.astype(BF)).T.astype(BF)
    for one in copies:
        one.wait()


def attend(index, query, parts):
    heads, keys, own = 2 * PAIRS, 2 * N_CTX * BLK, 4 * BLK
    outs = [
        jax.ShapeDtypeStruct(query.shape, BF),
        jax.ShapeDtypeStruct((heads, keys, own), F32),
    ]
    scratch = [
        pltpu.VMEM((keys, own // 2), F32),
        pltpu.VMEM((heads, keys, own), F32),
        pltpu.SemaphoreType.DMA((heads,)),
    ]
    return call(
        attend_body, outs, [pl.BlockSpec(memory_space=pltpu.SMEM)] + [VMEM] * 5, [VMEM, ANY],
        scratch, flops=4 * heads * keys * own * HD, moved=8 * MIB,
    )(index, query, *parts)


def attend_back_body(
    branch, weights, query, kv0, kv1, kv2, kv3, probs, cosine, sine,
    grad_query, out0, out1, out2, out3, w_v, p_v, sems,
):
    own, heads = 2 * BLK, 2 * PAIRS
    scale = 1.0 / math.sqrt(HD)
    weight = pltpu.make_async_copy(weights.at[:, pl.ds(QKVM, HALF_Q)], w_v, sems.at[heads])
    weight.start()
    loads = [
        pltpu.make_async_copy(probs.at[i], p_v.at[i], sems.at[i]) for i in range(heads)
    ]
    for one in loads:
        one.start()
    weight.wait()
    grad_context = product(branch[...], w_v[...]).astype(BF)
    parts, outs = (kv0, kv1, kv2, kv3), (out0, out1, out2, out3)
    for s in range(2):
        keys = stacked(parts, s, 0).T
        values = stacked(parts, s, HD)
        rows = slice(s * own, (s + 1) * own)
        grad_key = jnp.zeros((2 * N_CTX * BLK, HD), F32)
        grad_value = jnp.zeros((2 * N_CTX * BLK, HD), F32)
        for r in range(PAIRS):
            loads[s * PAIRS + r].wait()
            p = p_v[s * PAIRS + r]
            grad = two_heads(grad_context, rows, r)
            grad_p = against(values, grad)
            delta = jnp.sum(p * grad_p, axis=0, keepdims=True)
            grad_s = (p * (grad_p - delta)).astype(BF)
            back = product(keys, grad_s).T * scale
            for i in range(2):
                columns = slice((2 * r + i) * HD, (2 * r + i + 1) * HD)
                head = turn(back[i * own : (i + 1) * own], cosine[...], sine[...], True)
                grad_query[rows, columns] = head.astype(BF)
            grad_key = grad_key + product(grad_s, two_heads(query, rows, r))
            grad_value = grad_value + product(p.astype(BF), grad)
        for k, out in enumerate(outs):
            for h in range(2):
                to = slice((2 * h + s) * own, (2 * h + s + 1) * own)
                at = slice((2 * k + h) * own, (2 * k + h + 1) * own)
                out[to, :HD] = (grad_key[at] * scale).astype(BF)
                out[to, HD:] = grad_value[at].astype(BF)


def attend_back(branch, weights, query, parts, probs, cosine, sine):
    heads, keys, own = probs.shape
    outs = [jax.ShapeDtypeStruct(query.shape, BF)]
    outs += [jax.ShapeDtypeStruct(p.shape, BF) for p in parts]
    scratch = [
        pltpu.VMEM((D, HALF_Q), BF),
        pltpu.VMEM(probs.shape, F32),
        pltpu.SemaphoreType.DMA((heads + 1,)),
    ]
    return call(
        attend_back_body, outs, [VMEM, ANY] + [VMEM] * 5 + [ANY] + [VMEM] * 2, [VMEM] * 5,
        scratch, flops=10 * heads * keys * own * HD, moved=12 * MIB,
    )(branch, weights, query, *parts, probs, cosine, sine)


def weight_terms_body(rows, grads, inner, mixed, *refs):
    out = refs[-1]
    wide = inner.shape[1]
    out[:, :wide] = product(rows[...].T, inner[...]).astype(BF)
    out[:, wide : wide + mixed.shape[1]] = product(grads[...].T, mixed[...]).astype(BF)


def weight_terms(rows, grads, inner, mixed, width, *earlier):
    count = rows.shape[0]
    tile = 256
    column = pl.BlockSpec((count, tile), lambda i: (0, i))
    whole = [pl.BlockSpec(a.shape, lambda i: (0, 0)) for a in (inner, mixed)]
    return pl.pallas_call(
        weight_terms_body,
        grid=(D // tile,),
        out_shape=jax.ShapeDtypeStruct((D, width), BF),
        in_specs=[column, column] + whole + [ANY] * len(earlier),
        out_specs=pl.BlockSpec((tile, width), lambda i: (i, 0)),
        compiler_params=pltpu.CompilerParams(vmem_limit_bytes=48 * MIB),
        cost_estimate=pl.CostEstimate(
            flops=2 * count * D * FFW, bytes_accessed=26 * MIB, transcendentals=0
        ),
    )(rows, grads, inner, mixed, *earlier)


def fill_body(buffer, branch, context, out, part, sems):
    part[...] = product(branch[...].T, context[...]).astype(BF)
    fetch((part,), (out.at[:, pl.ds(FFW, HALF_Q)],), sems)


def fill(buffer, branch, context):
    return pl.pallas_call(
        fill_body,
        out_shape=jax.ShapeDtypeStruct(buffer.shape, BF),
        in_specs=[ANY, VMEM, VMEM],
        out_specs=ANY,
        scratch_shapes=[pltpu.VMEM((D, HALF_Q), BF), pltpu.SemaphoreType.DMA((1,))],
        input_output_aliases={0: 0},
        compiler_params=pltpu.CompilerParams(vmem_limit_bytes=48 * MIB),
        cost_estimate=pl.CostEstimate(
            flops=4 * BLK * 2 * D * HALF_Q, bytes_accessed=4 * MIB, transcendentals=0
        ),
    )(buffer, branch, context)


def plane_sum_body(index, got, *refs):
    keep, give = refs[-2:]
    parts = sum(got[i].astype(F32) for i in range(16)).astype(BF)
    first = index[0] == 0
    keep[...] = jnp.where(first, parts[0], parts[1])
    give[...] = jnp.where(first, parts[1], parts[0])


def plane_sum(index, got, *earlier):
    outs = [jax.ShapeDtypeStruct(got.shape[2:], BF)] * 2
    ins = [pl.BlockSpec(memory_space=pltpu.SMEM), VMEM] + [ANY] * len(earlier)
    return call(plane_sum_body, outs, ins, [VMEM] * 2, moved=2 * MIB)(index, got, *earlier)


def down_body(mixed, weights, *refs):
    mine, others, w_v, sems = refs[-4:]
    fetch((weights.at[:, pl.ds(2 * FFS, FFS)],), (w_v,), sems)
    tile = 256
    half = mine.shape[0]
    for base, out in ((half, others), (0, mine)):

        @pl.loop(0, half // tile)
        def _(i):
            at = pl.ds(pl.multiple_of(base + i * tile, tile), tile)
            to = pl.ds(pl.multiple_of(i * tile, tile), tile)
            out[to, :] = against(mixed[at, :], w_v[...]).astype(BF)


def down(mixed, weights, *earlier):
    half = mixed.shape[0] // 2
    outs = [jax.ShapeDtypeStruct((half, D), BF)] * 2
    scratch = [pltpu.VMEM((D, FFS), BF), pltpu.SemaphoreType.DMA((1,))]
    return call(
        down_body, outs, [VMEM, ANY] + [ANY] * len(earlier), [VMEM] * 2, scratch,
        flops=4 * half * D * FFS, moved=9 * MIB,
    )(mixed, weights, *earlier)


def ffn_body(
    rows, grads, weights, mixed, inner, back, back_others,
    rows_v, grads_v, gate_v, up_v, down_v, g_v, sems,
):
    half = rows.shape[0] // 2
    pairs = [
        (rows, rows_v),
        (weights.at[:, pl.ds(0, FFS)], gate_v),
        (weights.at[:, pl.ds(FFS, FFS)], up_v),
        (grads, grads_v),
        (weights.at[:, pl.ds(2 * FFS, FFS)], down_v),
    ]
    loads = [
        pltpu.make_async_copy(src, dst, sems.at[i]) for i, (src, dst) in enumerate(pairs)
    ]
    for one in loads:
        one.start()
    tile = 512
    steps = half // tile
    for one in loads[:2]:
        one.wait()

    @pl.loop(0, 2 * steps)
    def _(i):
        at = pl.ds(pl.multiple_of(i * tile, tile), tile)
        g_v[at, :] = product(rows_v[at, :], gate_v[...])

    for one in loads[2:]:
        one.wait()

    for base, out in ((half, back_others), (0, back)):

        @pl.loop(0, steps)
        def _(i):
            at = pl.ds(pl.multiple_of(base + i * tile, tile), tile)
            grad_mixed = product(grads_v[at, :], down_v[...])
            gate_val = g_v[at, :]
            up_val = product(rows_v[at, :], up_v[...])
            gate_sig = jax.nn.sigmoid(gate_val)
            swish = gate_val * gate_sig
            mixed[at, :] = (swish * up_val).astype(BF)
            grad_up = (grad_mixed * swish).astype(BF)
            grad_gate = (
                grad_mixed * up_val * gate_sig * (1.0 + gate_val * (1.0 - gate_sig))
            ).astype(BF)
            inner[at, :FFS] = grad_gate
            inner[at, FFS:] = grad_up
            to = pl.ds(pl.multiple_of(i * tile, tile), tile)
            out[to, :] = (
                against(grad_gate, gate_v[...]) + against(grad_up, up_v[...])
            ).astype(BF)


def ffn(rows, grads, weights):
    count = rows.shape[0]
    half = count // 2
    dims = [(count, FFS), (count, 2 * FFS), (half, D), (half, D)]
    outs = [jax.ShapeDtypeStruct(d, BF) for d in dims]
    scratch = [pltpu.VMEM((count, D), BF)] * 2 + [pltpu.VMEM((D, FFS), BF)] * 3
    scratch += [pltpu.VMEM((count, FFS), F32), pltpu.SemaphoreType.DMA((5,))]
    return call(
        ffn_body, outs, [ANY] * 3, [VMEM] * 4, scratch,
        flops=10 * count * D * FFS, moved=28 * MIB, vmem=56 * MIB,
    )(rows, grads, weights)


def per_device(
    tokens,
    cotangent,
    attn_gain,
    q_weight,
    q_bias,
    k_weight,
    k_bias,
    v_weight,
    v_bias,
    o_weight,
    mlp_gain,
    gate_weight,
    up_weight,
    down_weight,
):
    yh, x, z, yl, core = [lax.axis_index(a) for a in AXES]
    y = yh * 2 + yl
    ctx_rank = yh * 4 + x
    own = 2 * BLK
    both = 2 * own
    is_zero = core == 0

    place = jnp.arange(D, dtype=jnp.int32)
    place_r = place % ROWS
    place_x = place // ROWS % 4
    place_c = place // (ROWS * 4) % 2
    place_y = place // (ROWS * 8) % 4
    place_z = place // (ROWS * 32)
    place_dev = (((place_y // 2 * 4 + place_x) * 4 + place_z) * 2 + place_y % 2) * 2 + place_c
    natural = place_dev * ROWS + place_r
    to_order = lax.optimization_barrier((place[:, None] == natural[None, :]).astype(BF))

    tokens_flat = tokens.reshape(own, D)
    tokens_both = jnp.concatenate([tokens_flat, swap_core(tokens_flat)], 0)

    vectors = [arr[None] for arr in (attn_gain, mlp_gain, q_bias, k_bias, v_bias)]
    got = exchange(pack_attn(*vectors, q_weight, k_weight, v_weight, o_weight), TP)
    got_ff = after(pack_ff(gate_weight, up_weight, down_weight), got)
    got_ff = exchange(got_ff, TP)
    grad_low = product(cotangent.reshape(own, D), to_order).astype(BF)
    want = jnp.arange(8 * ROWS, dtype=jnp.int32)
    at = (want // ROWS % 4 * 2 + want // (4 * ROWS)) * PAD + want % ROWS
    pick = (at[:, None] == jnp.arange(8 * PAD, dtype=jnp.int32)[None, :]).astype(BF)
    rows_attn = product(pick, got).astype(BF)
    rows_ff = product(pick, got_ff).astype(BF)

    plane = ("z",) + Y
    grad_rows = neighbours(after(grad_low, rows_attn))
    attn_all = lax.all_gather(rows_attn, plane, axis=0, tiled=True)
    ff_all = lax.all_gather(rows_ff, plane, axis=0, tiled=True)
    attn_all = after(attn_all, grad_rows)
    weight_qkv = attn_all[:, :QKV]
    weight_o = attn_all[:, QKVM:]

    eight = (jnp.arange(8)[:, None] == jnp.arange(MISC)[None, :]).astype(BF)
    misc_rows = against(eight, attn_all[:, QKV:QKVM])
    gain_one = misc_rows[0:1]
    gain_two = misc_rows[1:2]
    bias_rows = misc_rows.astype(BF)
    bias_q = against(bias_rows[2:3], to_order)
    small = jnp.arange(KVH * HD, dtype=jnp.int32)
    to_small = (
        ((place_dev * 2 + place_r)[:, None] == small[None, :]) & (place_r < 2)[:, None]
    ).astype(BF)
    bias_kv = product(bias_rows[3:5], to_small)

    def side_of(row, width):
        return jnp.where(is_zero, row[:, :width], row[:, width:])

    bias_qkv = jnp.concatenate(
        [
            side_of(bias_q, HALF_Q),
            side_of(bias_kv[0:1], HD),
            side_of(bias_kv[1:2], HD),
        ],
        1,
    )

    offsets = jnp.arange(BLK, dtype=jnp.int32)
    query_pos = jnp.concatenate(
        [ctx_rank * BLK + offsets, (2 * N_CTX - 1 - ctx_rank) * BLK + offsets]
    )
    cosine_tab, sine_tab = rope_tables(query_pos)
    cosine_b = jnp.concatenate([cosine_tab, cosine_tab], 0)
    sine_b = jnp.concatenate([sine_tab, sine_tab], 0)

    inputs = product(tokens_both, to_order)
    scale_one = lax.rsqrt(jnp.mean(inputs * inputs, axis=-1, keepdims=True) + epsilon)
    unit_one = inputs * scale_one
    normed_one = (unit_one * gain_one).astype(BF)
    query_rot, kv_send = project(normed_one, attn_all, bias_qkv, cosine_tab, sine_tab)
    kv_parts = jnp.concatenate([kv_send, swap_yh(kv_send)], 0)
    kv_parts = [kv_parts] + [to_x(kv_parts, k) for k in range(1, 4)]
    slot = jnp.arange(4 * XCOLS, dtype=jnp.int32)
    slot_p = slot % XCOLS
    slot_zy = slot_p // (2 * ROWS)
    slot_dev = (slot_zy % 4 // 2 * 4 + slot // XCOLS) * 4 + slot_zy // 4
    slot_dev = (slot_dev * 2 + slot_zy % 2) * 2 + slot_p // ROWS % 2
    slot_at = jnp.where(slot_p < D // 4, slot_dev * ROWS + slot_p % ROWS, -1)
    by_x = (natural[:, None] == slot_at[None, :]).astype(BF)
    normed_x = jnp.where(
        (slot_p == D // 4)[None, :], 1.0, product(normed_one, by_x)
    ).astype(BF)
    query_rot = after(query_rot, normed_x)
    context_low, probs = attend(jnp.stack([yh, x]), query_rot, kv_parts)
    branch = against(context_low, weight_o)
    hidden_one = (
        inputs[:own] + branch[:own] + swap_core(branch[own:].astype(BF)).astype(F32)
    )
    scale_two = lax.rsqrt(jnp.mean(hidden_one * hidden_one, axis=-1, keepdims=True) + epsilon)
    unit_two = hidden_one * scale_two
    normed_two = (unit_two * gain_two).astype(BF)

    normed_rows = neighbours(normed_two)
    mixed_low, grad_inner, *grad_norm_part = ffn(
        normed_rows, grad_rows, ff_all
    )
    grad_norm_mine = add_low(grad_norm_part[0], swap_core(grad_norm_part[1]))
    grad_norm_two = neighbours_sum(grad_norm_mine)
    ff_buffer = weight_terms(
        normed_rows, grad_rows, grad_inner, mixed_low, FFW + HALF_Q, grad_norm_mine
    )
    grad_norm_two = after(grad_norm_two, ff_buffer)

    grad_unit_two = grad_norm_two * gain_two
    grad_hidden = grad_low.astype(F32) + scale_two * (
        grad_unit_two - unit_two * jnp.mean(grad_unit_two * unit_two, axis=-1, keepdims=True)
    )
    grad_branch = grad_hidden.astype(BF)
    grad_branch = jnp.concatenate([grad_branch, swap_core(grad_branch)], 0)
    late_grads = fill(ff_buffer, grad_branch, context_low)
    late_sum = lax.psum_scatter(late_grads, plane, scatter_dimension=0, tiled=True)
    branch_ready = hold(grad_branch, late_grads)
    grad_query, *kv_grads = attend_back(
        branch_ready, attn_all, query_rot, kv_parts, probs, cosine_tab, sine_tab
    )
    kv_grads = [kv_grads[0]] + [to_x(kv_grads[k], k) for k in range(1, 4)]
    q_grads = row_major(over_rows(normed_x, hold(grad_query, *kv_grads[1:])).astype(BF))
    q_got = exchange(q_grads, "x")
    grad_kv = sum(part.astype(F32) for part in kv_grads)
    grad_kv = grad_kv[:both] + swap_yh(grad_kv[both:].astype(BF)).astype(F32)
    grad_key = unrotate(grad_kv[:, :HD], cosine_b, sine_b)
    grad_kv = jnp.concatenate([grad_key, grad_kv[:, HD:]], 1).astype(BF)
    down_mine, down_others = down(mixed_low, ff_all, q_grads)
    grad_kv = hold(grad_kv, down_mine)
    kv_grads = row_major(over_rows(normed_x, grad_kv).astype(BF))
    kv_pieces = [
        lax.dynamic_slice_in_dim(kv_grads, (x ^ k) * XCOLS, XCOLS, 0) for k in range(4)
    ]
    kv_pieces = [kv_pieces[0]] + [to_x(kv_pieces[k], k) for k in range(1, 4)]
    kv_sum = sum(part.astype(F32) for part in kv_pieces).astype(BF)
    down_both = add_low(down_mine, swap_core(down_others)).reshape(4, own, D)
    down_both = jnp.concatenate(
        [lax.dynamic_index_in_dim(down_both, k ^ x, 0, False) for k in range(4)], 0
    )
    down_terms = lax.psum_scatter(down_both, "x", scatter_dimension=0, tiled=True)
    layer_sum = (hidden_one + down_terms.astype(F32)).astype(BF)
    layer_out = against(layer_sum, to_order).astype(BF).reshape(tokens.shape)
    grad_lin = hold(jnp.concatenate([grad_query, grad_kv], 1), kv_grads)
    grad_norm_one = against(grad_lin, weight_qkv)
    grad_norm_one = grad_norm_one[:own] + swap_core(grad_norm_one[own:].astype(BF)).astype(F32)
    unit_own = unit_one[:own]
    grad_unit_one = grad_norm_one * gain_one
    input_grad = grad_hidden + scale_one[:own] * (
        grad_unit_one - unit_own * jnp.mean(grad_unit_one * unit_own, axis=-1, keepdims=True)
    )
    input_high = input_grad.astype(BF)
    input_rest = (input_grad - input_high.astype(F32)).astype(BF)
    input_grad = (against(input_high, to_order) + against(input_rest, to_order)).reshape(
        tokens.shape
    )

    qkv_sum = jnp.concatenate([added(q_got, 4), kv_sum], 1)
    spot = jnp.arange(16 * 2 * PAD, dtype=jnp.int32)
    spot_r = spot % PAD
    spot_at = spot // PAD * ROWS + spot_r
    spot_at = jnp.where(spot_r < ROWS, spot_at, jnp.where(spot_r == ROWS, D // 4, -1))
    room = (spot_at[:, None] == jnp.arange(XCOLS, dtype=jnp.int32)[None, :]).astype(BF)
    qkv_rows = product(room, qkv_sum).astype(BF)

    spot = jnp.arange(8 * PAD, dtype=jnp.int32)
    spot_at = ((spot // (4 * PAD)) ^ core) * 4 + ((spot // PAD % 4) ^ x)
    spot_at = jnp.where(spot % PAD < ROWS, spot_at * ROWS + spot % PAD, -1)
    late_pick = (want[:, None] == spot_at[None, :]).astype(BF)
    late = over_rows(late_pick, hold(late_sum, qkv_rows)).astype(BF)
    late_pair = [late[: 4 * PAD], swap_core(late[4 * PAD :])]
    late_pair = [part.reshape(4, PAD, FFW + HALF_Q) for part in late_pair]
    late = jnp.concatenate(late_pair, 1)
    late = [late[0]] + [to_x(late[k], k) for k in range(1, 4)]
    qkv_sum = exchange(qkv_rows, plane)
    qkv_keep, qkv_give = plane_sum(core[None], qkv_sum.reshape(16, 2, PAD, QKV), *late[1:])
    qkv_sum = jnp.stack([qkv_keep, swap_core(qkv_give)])
    (
        q_weight_grad,
        k_weight_grad,
        v_weight_grad,
        o_weight_grad,
        gate_weight_grad,
        up_weight_grad,
        down_weight_grad,
        bias_sum,
        gain_sum,
    ) = unpack_grads(
        jnp.stack([x, core]), qkv_sum, *late,
        q_weight, k_weight, v_weight, gate_weight, up_weight,
    )
    attn_gain_grad = gain_sum[:, 0] / attn_gain.astype(F32)
    mlp_gain_grad = gain_sum[:, 1] / mlp_gain.astype(F32)
    device = ctx_rank * 16 + z * 4 + yl * 2 + core
    q_bias_grad = lax.dynamic_slice_in_dim(
        bias_sum[:, :HALF_Q].reshape(D), device * ROWS, ROWS, 0
    )
    k_bias_grad = bias_sum[:, HALF_Q : HALF_Q + HD].reshape(KVH * HD)
    v_bias_grad = lax.dynamic_slice_in_dim(
        bias_sum[:, HALF_Q + HD :].reshape(KVH * HD), device * 2, 2, 0
    )
    return (
        layer_out,
        input_grad,
        attn_gain_grad,
        q_weight_grad,
        q_bias_grad,
        k_weight_grad,
        k_bias_grad,
        v_weight_grad,
        v_bias_grad,
        o_weight_grad,
        mlp_gain_grad,
        gate_weight_grad,
        up_weight_grad,
        down_weight_grad,
    )


def solution(mesh):
    fine = Mesh(mesh.devices.reshape(2, 4, 4, 2, 2), AXES)
    acts = P(("z", "yl", "core"), None, CTX, None)
    vec, mat = P(AXES), P(AXES, None)
    return jax.shard_map(
        per_device,
        mesh=fine,
        in_specs=(acts, acts, vec, mat, vec, mat, vec, mat, vec, mat, vec, mat, mat, mat),
        out_specs=(acts, acts, vec, mat, vec, mat, P(), mat, vec, mat, vec, mat, mat, mat),
        check_vma=False,
    )
```
